32 devices in a mesh: shard: 2 (over y), ctx: 4 (over x, core), tp: 4 (over z).
Axes of the slice: x: 2, y: 2, z: 4, core: 2. Of those that a mesh axis runs over, the one named last changes fastest.
Arguments:
- hidden: bfloat16 [8, 4096, 768], P('shard', ('ctx', 'tp')), may hold values from -6 to 6
- bank: bfloat16 [8, 16384, 768], P(('shard', 'ctx'), 'tp'), may hold values from -6 to 6
- indices: int32 [8, 1024], P(('shard', 'ctx')), may hold values from 0 to 16383, as said below
- lengths: int32 [8], replicated, may hold values from 512 to 4096, as said below
- cotangent: bfloat16 [8, 4096, 768], P('shard', ('ctx', 'tp')), may hold values from -6 to 6
- query_self: bfloat16 [768, 768], P('shard', 'tp'), may hold values from -0.21875 to 0.21875
- key_self: bfloat16 [768, 768], P('shard', 'tp'), may hold values from -0.21875 to 0.21875
- value_self: bfloat16 [768, 768], P('shard', 'tp'), may hold values from -0.21875 to 0.21875
- out_self: bfloat16 [768, 768], P('tp', 'shard'), may hold values from -1.25 to 1.25
- query_cross: bfloat16 [768, 768], P('shard', 'tp'), may hold values from -0.21875 to 0.21875
- key_cross: bfloat16 [768, 768], P('shard', 'tp'), may hold values from -0.21875 to 0.21875
- value_cross: bfloat16 [768, 768], P('shard', 'tp'), may hold values from -0.21875 to 0.21875
- out_cross: bfloat16 [768, 768], P('tp', 'shard'), may hold values from -1.75 to 1.75
- up_weight: bfloat16 [768, 3072], P('shard', 'tp'), may hold values from -0.21875 to 0.21875
- down_weight: bfloat16 [3072, 768], P('tp', 'shard'), may hold values from -0.109375 to 0.109375
- norm_gain: bfloat16 [3, 768], P(None, 'shard'), may hold values from 0.5 to 1.5
- norm_bias: bfloat16 [3, 768], P(None, 'shard'), may hold values from -0.29882812 to 0.29882812
Outputs:
- output: bfloat16 [8, 4096, 768], P('shard', ('ctx', 'tp'))
- gradient_hidden: float32 [8, 4096, 768], P('shard', ('ctx', 'tp'))
- gradient_bank: float32 [8, 16384, 768], P(('shard', 'ctx'), 'tp')
- gradient_query_self: float32 [768, 768], P('shard', 'tp')
- gradient_key_self: float32 [768, 768], P('shard', 'tp')
- gradient_value_self: float32 [768, 768], P('shard', 'tp')
- gradient_out_self: float32 [768, 768], P('tp', 'shard')
- gradient_query_cross: float32 [768, 768], P('shard', 'tp')
- gradient_key_cross: float32 [768, 768], P('shard', 'tp')
- gradient_value_cross: float32 [768, 768], P('shard', 'tp')
- gradient_out_cross: float32 [768, 768], P('tp', 'shard')
- gradient_up_weight: float32 [768, 3072], P('shard', 'tp')
- gradient_down_weight: float32 [3072, 768], P('tp', 'shard')
- gradient_norm_gain: float32 [3, 768], P(None, 'shard')
- gradient_norm_bias: float32 [3, 768], P(None, 'shard')
- statistics: float32 [6], replicated
The draws below stay inside these ranges and needn't reach their ends.
Inputs may be any that keep to these rules, and one draw needn't show every extreme that they name: The 1024 indices of one sequence are distinct, and each sequence's list holds row 0 and row 16383. `lengths`: the valid tokens of a sequence are its first positions; some sequence has all 4096 valid and some has 512.
All inputs are finite; a program needn't handle non-finite values.
Results may differ from the reference program's by a relative error of at most 0.025.
Values may be sent and summed in bfloat16 or wider, within the bound.
No kernel may reach another device: no remote copies, remote signals or barrier semaphores. Data moves between devices by JAX's collectives and lax.ppermute only.
A program may use at most 256 MiB of HBM per device.

```python
import jax
import jax.numpy as jnp
from jax import lax

D = 768
HEADS = 12
HEAD_DIM = 64
FF = 3072
LEN = 4096
BLK = 256
TOPK = 1024
BANK = 16384
TILE = 512
SEQS = 8


def draw_indices(key, part):

    def one_row(row_key):
        first_key, second_key = jax.random.split(row_key)
        middle = jax.random.permutation(first_key, BANK - 2)[:TOPK - 2].astype(jnp.int32) + 1
        picked = jnp.concatenate([middle, jnp.array([0, BANK - 1], dtype=jnp.int32)])
        return jax.random.permutation(second_key, picked)
    return jax.vmap(one_row)(jax.random.split(key, SEQS)).astype(jnp.int32)


def draw_lengths(key, part):
    first_key, second_key = jax.random.split(key)
    length_rows = jax.random.randint(first_key, (SEQS,), LEN // 8, LEN + 1, dtype=jnp.int32)
    shuffled = jax.random.permutation(second_key, SEQS)
    length_rows = length_rows.at[shuffled[0]].set(LEN)
    return length_rows.at[shuffled[1]].set(LEN // 8).astype(jnp.int32)


def levels(rng, extent, shards, low, top_value):
    factor_of, own = 1.0, jax.random.fold_in(rng, 6)
    for axis_at, shards_of in shards:
        draws = jnp.exp(jax.random.uniform(jax.random.fold_in(own, axis_at), (shards_of,), jnp.float32, low / len(shards), top_value / len(shards)))
        factor_of = factor_of * jnp.repeat(draws, extent[axis_at] // shards_of).reshape([-1 if axis == axis_at else 1 for axis in range(len(extent))])
    return factor_of


def noise(rng, shape, deviation, limit, pieces=(), held_as=jnp.bfloat16):
    entries = jax.random.normal(rng, shape, jnp.float32) * deviation
    if len(pieces) > 0:
        entries = levels(rng, shape, pieces, -0.22, 0.18) * entries
    return jnp.clip(entries, min=-limit, max=limit).astype(held_as)


def setup_inputs(seed: int = 0) -> dict:
    seeds = jax.random.split(jax.random.key(seed), 18)
    hidden = noise(seeds[0], (SEQS, LEN, D), 1.0, 6.0, ((0, 2), (1, 16)))
    bank = noise(seeds[1], (SEQS, BANK, D), 1.0, 6.0, ((0, 8), (1, 4)))
    indices = draw_indices(jax.random.fold_in(seeds[17], 71), 0)
    lengths = draw_lengths(jax.random.fold_in(seeds[17], 71), 0)
    cotangent = noise(seeds[4], (SEQS, LEN, D), 1.0, 6.0, ((0, 2), (1, 16)))
    query_self = noise(seeds[5], (D, HEADS * HEAD_DIM), D ** -0.5, 0.21875, ((0, 2), (1, 4)))
    key_self = noise(seeds[6], (D, HEADS * HEAD_DIM), D ** -0.5, 0.21875, ((0, 2), (1, 4)))
    value_self = noise(seeds[7], (D, HEADS * HEAD_DIM), D ** -0.5, 0.21875, ((0, 2), (1, 4)))
    out_self = noise(seeds[8], (HEADS * HEAD_DIM, D), (HEADS * HEAD_DIM // 32) ** -0.5, 1.25, ((0, 4), (1, 2)))
    query_cross = noise(seeds[9], (D, HEADS * HEAD_DIM), D ** -0.5, 0.21875, ((0, 2), (1, 4)))
    key_cross = noise(seeds[10], (D, HEADS * HEAD_DIM), D ** -0.5, 0.21875, ((0, 2), (1, 4)))
    value_cross = noise(seeds[11], (D, HEADS * HEAD_DIM), D ** -0.5, 0.21875, ((0, 2), (1, 4)))
    out_cross = noise(seeds[12], (HEADS * HEAD_DIM, D), (HEADS * HEAD_DIM // 64) ** -0.5, 1.75, ((0, 4), (1, 2)))
    up_weight = noise(seeds[13], (D, FF), D ** -0.5, 0.21875, ((0, 2), (1, 4)))
    down_weight = noise(seeds[14], (FF, D), FF ** -0.5, 0.109375, ((0, 4), (1, 2)))
    norm_gain = jnp.clip(1.0 + 0.1 * jax.random.normal(seeds[15], (3, D), jnp.float32), 0.5, 1.5).astype(jnp.bfloat16)
    norm_bias = jnp.clip(jax.random.uniform(seeds[16], (3, D), jnp.float32, -0.29882812, 0.29882812) * levels(seeds[16], (3, D), ((1, 2),), -0.4, 0.0), -0.29882812, 0.29882812).astype(jnp.bfloat16)
    return {"hidden": hidden, "bank": bank, "indices": indices, "lengths": lengths, "cotangent": cotangent, "query_self": query_self, "key_self": key_self, "value_self": value_self, "out_self": out_self, "query_cross": query_cross, "key_cross": key_cross, "value_cross": value_cross, "out_cross": out_cross, "up_weight": up_weight, "down_weight": down_weight, "norm_gain": norm_gain, "norm_bias": norm_bias}


@jax.custom_vjp
def low(v):
    return lax.optimization_barrier(v.astype(jnp.bfloat16)).astype(jnp.float32)

@jax.custom_vjp
def low_back(v):
    return v

def low_keep(v):
    return (low(v), None)

def low_pass(kept, grad):
    return (grad,)

def back_keep(v):
    return (v, None)

def back_low(kept, grad):
    return (low(grad),)
low.defvjp(low_keep, low_pass)
low_back.defvjp(back_keep, back_low)
HIGHEST = lax.Precision.HIGHEST
EPSILON = 1e-05
NEGATIVE = -1e+30

def product(left, right):
    return jnp.dot(left, right, precision=HIGHEST, preferred_element_type=jnp.float32)

def both_low(value):
    return low_back(low(value))

def layer_norm(summed, gain_row, bias_row):
    average = lax.optimization_barrier(jnp.mean(summed, axis=-1, keepdims=True))
    centred = summed - average
    variance = lax.optimization_barrier(jnp.mean(centred * centred, axis=-1, keepdims=True))
    return centred * lax.rsqrt(variance + EPSILON) * gain_row + bias_row

def softmax_rows(scores):
    largest = lax.optimization_barrier(jnp.max(scores, axis=-1, keepdims=True))
    raised = jnp.exp(scores - largest)
    return raised / lax.optimization_barrier(jnp.sum(raised, axis=-1, keepdims=True))

def attention(queries, key_rows, value_rows, length, masked):
    key_place = jnp.arange(key_rows.shape[0], dtype=jnp.int32)
    scaling = HEAD_DIM ** (-0.5)

    def one_tile(tile_start):
        query_rows = lax.dynamic_slice_in_dim(queries, tile_start, TILE, 0)
        scores = low_back(jnp.einsum('qhd,khd->hqk', query_rows, key_rows, precision=HIGHEST) * scaling)
        if masked:
            query_block = (tile_start + jnp.arange(TILE, dtype=jnp.int32)) // BLK
            allowed = (key_place[None, :] // BLK <= query_block[:, None]) & (key_place[None, :] < length)
            scores = jnp.where(allowed[None], scores, NEGATIVE)
        softmax_out = low(softmax_rows(scores))
        return jnp.einsum('hqk,khd->qhd', softmax_out, value_rows, precision=HIGHEST)
    starts = jnp.arange(queries.shape[0] // TILE, dtype=jnp.int32) * TILE
    tile_outs = lax.map(jax.checkpoint(one_tile), starts)
    return tile_outs.reshape(queries.shape[0], HEADS * HEAD_DIM)

def head_view(matrix):
    return matrix.reshape(matrix.shape[0], HEADS, HEAD_DIM)

def sequence_layer(params, hidden_sequence, bank_sequence, chosen, length):
    query_self, key_self, value_self, out_self, query_cross, key_cross, value_cross, out_cross, up_weight, down_weight, norm_gain, norm_bias = params
    queries = both_low(product(hidden_sequence, query_self))
    key_rows = both_low(product(hidden_sequence, key_self))
    value_rows = both_low(product(hidden_sequence, value_self))
    attended = both_low(attention(head_view(queries), head_view(key_rows), head_view(value_rows), length, True))
    branch_one = low_back(product(attended, out_self))
    first = layer_norm(hidden_sequence + branch_one, norm_gain[0], norm_bias[0])
    first_low = low(first)
    selected = jnp.take(bank_sequence, chosen, axis=0)
    cross_query = both_low(product(first_low, query_cross))
    cross_key = both_low(product(selected, key_cross))
    cross_value = both_low(product(selected, value_cross))
    cross_attended = both_low(attention(head_view(cross_query), head_view(cross_key), head_view(cross_value), length, False))
    branch_two = low_back(product(cross_attended, out_cross))
    second = layer_norm(first + branch_two, norm_gain[1], norm_bias[1])
    second_low = low(second)
    inner_act = low_back(product(second_low, up_weight))
    active = low(jax.nn.gelu(inner_act, approximate=False))
    branch_three = low_back(product(active, down_weight))
    output = layer_norm(second + branch_three, norm_gain[2], norm_bias[2])
    valid_rows = (jnp.arange(LEN, dtype=jnp.int32) < length).astype(jnp.float32)[:, None]
    square_sums = jnp.stack([jnp.sum(valid_rows * matrix * matrix) for matrix in (hidden_sequence, branch_one, first, branch_two, second, branch_three)])
    return (output, square_sums)

def reference(hidden, bank, indices, lengths, cotangent, query_self, key_self, value_self, out_self, query_cross, key_cross, value_cross, out_cross, up_weight, down_weight, norm_gain, norm_bias):
    params = tuple((weight.astype(jnp.float32) for weight in (query_self, key_self, value_self, out_self, query_cross, key_cross, value_cross, out_cross, up_weight, down_weight, norm_gain, norm_bias)))
    zero_grads = jax.tree.map(jnp.zeros_like, params)

    def one_sequence(totals, inputs):
        hidden_sequence, bank_sequence, chosen, length, cotangent_sequence = inputs

        def forward(params_in, hidden_in, bank_in):
            return sequence_layer(params_in, hidden_in, bank_in, chosen, length)
        output, pullback, square_sums = jax.vjp(forward, params, hidden_sequence.astype(jnp.float32), bank_sequence.astype(jnp.float32), has_aux=True)
        valid_rows = (jnp.arange(LEN, dtype=jnp.int32) < length).astype(jnp.float32)[:, None]
        back_params, back_hidden, back_bank = pullback(cotangent_sequence.astype(jnp.float32) * valid_rows)
        totals = jax.tree.map(jnp.add, totals, back_params)
        return (totals, (output.astype(jnp.bfloat16), back_hidden, back_bank, square_sums))
    totals, stacked = lax.scan(one_sequence, zero_grads, (hidden, bank, indices, lengths, cotangent))
    outputs, back_hidden, back_bank, square_sums = stacked
    token_total = jnp.sum(lengths).astype(jnp.float32) * D
    statistics = jnp.sqrt(lax.optimization_barrier(jnp.sum(square_sums, axis=0)) / token_total)
    back_query_self, back_key_self, back_value_self, back_out_self, back_query_cross, back_key_cross, back_value_cross, back_out_cross, back_up, back_down, back_gain, back_bias = totals
    return (outputs, back_hidden, back_bank, back_query_self, back_key_self, back_value_self, back_out_self, back_query_cross, back_key_cross, back_value_cross, back_out_cross, back_up, back_down, back_gain, back_bias, statistics)
```

```python
import functools

import jax
import jax.numpy as jnp
from jax import lax
from jax.experimental import pallas as pl
from jax.experimental.pallas import tpu as pltpu
from jax.sharding import PartitionSpec as P

HEADS = 12
HEAD_DIM = 64
BLK = 256

EPSILON = 1e-05
NEGATIVE = -1e30
LOG2E = 1.4426950408889634
SCALING = HEAD_DIM**-0.5
QUERY_SCALE = SCALING * LOG2E

KEYS = 512
QUERIES = 1024
VMEM_LIMIT = 56 * 2**20

bf16 = jnp.bfloat16
f32 = jnp.float32


def dot_nn(left, right):
    return lax.dot_general(left, right, (((1,), (0,)), ((), ())), preferred_element_type=f32)


def dot_nt(left, right):
    return lax.dot_general(left, right, (((1,), (1,)), ((), ())), preferred_element_type=f32)


def row_index(rows, columns):
    return lax.broadcasted_iota(jnp.int32, (rows, columns), 0)


def place_index(rows, columns, start):
    return lax.broadcasted_iota(jnp.int32, (rows, columns), 1) + start


def three_parts(row, ones_row):
    high = row.astype(bf16).astype(f32)
    rest = row - high
    middle = rest.astype(bf16).astype(f32)
    lowest = rest - middle
    at = row_index(16, row.shape[1])
    last = jnp.where(at == 3, 1.0, 0.0) if ones_row else jnp.zeros_like(at, f32)
    rows = jnp.where(at == 0, high, jnp.where(at == 1, middle, jnp.where(at == 2, lowest, last)))
    return rows.astype(bf16)


def self_forward_kernel(length_ref, x_ref, out_ref, total_ref, keys, values, held):
    length = length_ref[pl.program_id(0)]
    places = x_ref.shape[2]
    quarter_tiles = out_ref.shape[3] // QUERIES
    per_query = QUERIES // KEYS
    half = BLK
    key_tiles = (length + KEYS - 1) // KEYS

    def prepare(tile, _):
        start = pl.multiple_of(tile * KEYS, KEYS)
        rows = x_ref[0, HEAD_DIM : 2 * HEAD_DIM, pl.ds(start, KEYS)].astype(f32)
        at, place = row_index(16, KEYS), place_index(16, KEYS, start)
        mask = jnp.where((at == 0) & (place >= length), NEGATIVE, 0.0)
        stacked = jnp.concatenate([rows, mask, jnp.zeros((48, KEYS), f32)], axis=0)
        keys[pl.ds(start, KEYS), :] = stacked.T.astype(bf16)
        values[0:HEAD_DIM, pl.ds(start, KEYS)] = x_ref[
            0, 2 * HEAD_DIM : 3 * HEAD_DIM, pl.ds(start, KEYS)
        ]
        return 0

    lax.fori_loop(0, key_tiles, prepare, 0)
    values[HEAD_DIM : HEAD_DIM + 16, :] = jnp.ones((16, places), bf16)

    def query_tile(index, _):
        first_query = pl.multiple_of(index * QUERIES, QUERIES)
        ones_row = jnp.where(row_index(16, QUERIES) == 0, 1.0, 0.0).astype(bf16)
        queries = jnp.concatenate(
            [x_ref[0, 0:HEAD_DIM, pl.ds(first_query, QUERIES)], ones_row, jnp.zeros((48, QUERIES), bf16)],
            axis=0,
        )

        def score(tile):
            start = pl.multiple_of(tile * KEYS, KEYS)
            scores = dot_nn(keys[pl.ds(start, KEYS), :], queries)
            held[lax.rem(tile, 2)] = scores
            return jnp.max(scores, axis=0, keepdims=True)

        def step(tile, carry):
            largest, total, next_largest = carry
            updated = jnp.maximum(largest, next_largest)
            start = pl.multiple_of(tile * KEYS, KEYS)
            chances = jnp.exp2(held[lax.rem(tile, 2)] - updated).astype(bf16)
            total = total * jnp.exp2(largest - updated) + dot_nn(
                values[:, pl.ds(start, KEYS)], chances
            )
            return updated, total, score(jnp.minimum(tile + 1, key_tiles - 1))

        largest = jnp.full((1, QUERIES), NEGATIVE, f32)
        total = jnp.zeros((HEAD_DIM + 16, QUERIES), f32)
        largest, total, _ = lax.fori_loop(
            0, jnp.minimum(index * per_query, key_tiles), step, (largest, total, score(0))
        )

        def part(low, high, start, size, largest, total):
            scores = dot_nn(keys[pl.ds(start, size), :], queries[:, low:high])
            before = largest[:, low:high]
            updated = jnp.maximum(before, jnp.max(scores, axis=0, keepdims=True))
            chances = jnp.exp2(scores - updated).astype(bf16)
            summed = dot_nn(values[:, pl.ds(start, size)], chances)
            return updated, total[:, low:high] * jnp.exp2(before - updated) + summed

        for at in range(per_query):

            def diagonal(_, carry):
                largest, total = carry
                low = at * KEYS
                start = pl.multiple_of(first_query + low, KEYS)
                pieces = [(largest[:, :low], total[:, :low])] if low else []
                pieces.append(part(low, low + half, start, half, largest, total))
                pieces.append(part(low + half, low + KEYS, start, KEYS, largest, total))
                if low + KEYS < QUERIES:
                    pieces.append(part(low + KEYS, QUERIES, start, KEYS, largest, total))
                return tuple(jnp.concatenate(piece, axis=1) for piece in zip(*pieces))

            present = (index * per_query + at < key_tiles).astype(jnp.int32)
            largest, total = lax.fori_loop(0, present, diagonal, (largest, total))
        row_total = total[HEAD_DIM : HEAD_DIM + 1]
        inner = pl.multiple_of(lax.rem(index, quarter_tiles) * QUERIES, QUERIES)
        out_ref[index // quarter_tiles, 0, :, pl.ds(inner, QUERIES)] = (
            total[:HEAD_DIM] / row_total
        ).astype(bf16)
        total_ref[0, :, pl.ds(first_query, QUERIES)] = largest + jnp.log2(row_total)
        return 0

    lax.fori_loop(0, places // QUERIES, query_tile, 0)


def self_forward(unit_lengths, projected, quarters):
    units, _, places = projected.shape
    return pl.pallas_call(
        self_forward_kernel,
        grid_spec=pltpu.PrefetchScalarGridSpec(
            num_scalar_prefetch=1,
            grid=(units,),
            in_specs=[pl.BlockSpec((1, 3 * HEAD_DIM, places), lambda u, n: (u, 0, 0))],
            out_specs=[
                pl.BlockSpec((quarters, 1, HEAD_DIM, places // quarters), lambda u, n: (0, u, 0, 0)),
                pl.BlockSpec((1, 1, places), lambda u, n: (u, 0, 0)),
            ],
            scratch_shapes=[
                pltpu.VMEM((places, 128), bf16),
                pltpu.VMEM((HEAD_DIM + 16, places), bf16),
                pltpu.VMEM((2, KEYS, QUERIES), f32),
            ],
        ),
        out_shape=[
            jax.ShapeDtypeStruct((quarters, units, HEAD_DIM, places // quarters), bf16),
            jax.ShapeDtypeStruct((units, 1, places), f32),
        ],
        compiler_params=pltpu.CompilerParams(vmem_limit_bytes=VMEM_LIMIT),
        name="self_forward",
    )(unit_lengths, projected)


def self_backward_kernel(
    length_ref, x_ref, out_ref, back_ref, total_ref, grad_ref, keys, values, queries, backs, query_sum
):
    length = length_ref[pl.program_id(0)]
    places = x_ref.shape[2]
    quarter_tiles = out_ref.shape[3] // KEYS
    half = BLK
    key_tiles = (length + KEYS - 1) // KEYS

    def prepare(tile, _):
        start = pl.multiple_of(tile * KEYS, KEYS)
        key_rows = x_ref[0, HEAD_DIM : 2 * HEAD_DIM, pl.ds(start, KEYS)].astype(f32)
        value_rows = x_ref[0, 2 * HEAD_DIM : 3 * HEAD_DIM, pl.ds(start, KEYS)].astype(f32)
        at, place = row_index(16, KEYS), place_index(16, KEYS, start)
        ones = jnp.where(at < 3, 1.0, 0.0)
        mask = jnp.where((at == 3) & (place >= length), NEGATIVE, ones)
        blank = jnp.zeros((48, KEYS), f32)
        keys[pl.ds(start, KEYS), :] = jnp.concatenate([key_rows, mask, blank], axis=0).T.astype(bf16)
        values[pl.ds(start, KEYS), :] = jnp.concatenate([value_rows, ones, blank], axis=0).T.astype(
            bf16
        )
        blank = blank.astype(bf16)
        queries[:, pl.ds(start, KEYS)] = jnp.concatenate(
            [
                x_ref[0, 0:HEAD_DIM, pl.ds(start, KEYS)],
                three_parts(-total_ref[0, :, pl.ds(start, KEYS)], True),
                blank,
            ],
            axis=0,
        )
        inner = pl.multiple_of(lax.rem(tile, quarter_tiles) * KEYS, KEYS)
        back = back_ref[tile // quarter_tiles, 0, :, pl.ds(inner, KEYS)]
        out = out_ref[tile // quarter_tiles, 0, :, pl.ds(inner, KEYS)]
        delta = jnp.sum(back.astype(f32) * out.astype(f32), axis=0, keepdims=True)
        backs[:, pl.ds(start, KEYS)] = jnp.concatenate(
            [back, three_parts(-delta, False), blank], axis=0
        )
        query_sum[:, pl.ds(start, KEYS)] = jnp.zeros((HEAD_DIM, KEYS), f32)
        return 0

    lax.fori_loop(0, key_tiles, prepare, 0)

    def tile_terms(key_start, key_size, query_start, query_size, back_key, back_value):
        query = queries[:, pl.ds(query_start, query_size)]
        back = backs[:, pl.ds(query_start, query_size)]
        chances = jnp.exp2(dot_nn(keys[pl.ds(key_start, key_size), :], query))
        back_chances = dot_nn(values[pl.ds(key_start, key_size), :], back)
        back_scores = (chances * back_chances).astype(bf16)
        back_value = back_value + dot_nt(back[:HEAD_DIM], chances.astype(bf16))
        back_key = back_key + dot_nt(query[:HEAD_DIM], back_scores)
        query_sum[:, pl.ds(query_start, query_size)] += dot_nn(
            x_ref[0, HEAD_DIM : 2 * HEAD_DIM, pl.ds(key_start, key_size)], back_scores
        )
        return back_key, back_value

    def place_of(tile):
        inner = pl.multiple_of(lax.rem(tile, quarter_tiles) * KEYS, KEYS)
        return tile // quarter_tiles, inner

    def key_tile(index, _):
        start = pl.multiple_of(index * KEYS, KEYS)
        second = pl.multiple_of(start + half, half)
        blank = jnp.zeros((HEAD_DIM, half), f32)
        first_part = tile_terms(start, half, start, KEYS, blank, blank)
        second_part = tile_terms(second, half, second, half, blank, blank)
        begun = tuple(jnp.concatenate(pair, axis=1) for pair in zip(first_part, second_part))

        def step(tile, carry):
            return tile_terms(start, KEYS, pl.multiple_of(tile * KEYS, KEYS), KEYS, *carry)

        back_key, back_value = lax.fori_loop(index + 1, key_tiles, step, begun)
        quarter, inner = place_of(index)
        grad_ref[quarter, 0, HEAD_DIM : 2 * HEAD_DIM, pl.ds(inner, KEYS)] = (
            back_key * (1.0 / LOG2E)
        ).astype(bf16)
        grad_ref[quarter, 0, 2 * HEAD_DIM : 3 * HEAD_DIM, pl.ds(inner, KEYS)] = back_value.astype(
            bf16
        )
        return 0

    lax.fori_loop(0, key_tiles, key_tile, 0)

    def finish(tile, _):
        quarter, inner = place_of(tile)
        start = pl.multiple_of(tile * KEYS, KEYS)
        grad_ref[quarter, 0, 0:HEAD_DIM, pl.ds(inner, KEYS)] = (
            query_sum[:, pl.ds(start, KEYS)] * SCALING
        ).astype(bf16)
        return 0

    lax.fori_loop(0, key_tiles, finish, 0)

    def clear(tile, _):
        quarter, inner = place_of(tile)
        grad_ref[quarter, 0, :, pl.ds(inner, KEYS)] = jnp.zeros((3 * HEAD_DIM, KEYS), bf16)
        return 0

    lax.fori_loop(key_tiles, places // KEYS, clear, 0)


def self_backward(unit_lengths, projected, attended, back, totals):
    units, _, places = projected.shape
    quarters = attended.shape[0]
    quarter = places // quarters
    spread = pl.BlockSpec((quarters, 1, HEAD_DIM, quarter), lambda u, n: (0, u, 0, 0))
    return pl.pallas_call(
        self_backward_kernel,
        grid_spec=pltpu.PrefetchScalarGridSpec(
            num_scalar_prefetch=1,
            grid=(units,),
            in_specs=[
                pl.BlockSpec((1, 3 * HEAD_DIM, places), lambda u, n: (u, 0, 0)),
                spread,
                spread,
                pl.BlockSpec((1, 1, places), lambda u, n: (u, 0, 0)),
            ],
            out_specs=pl.BlockSpec((quarters, 1, 3 * HEAD_DIM, quarter), lambda u, n: (0, u, 0, 0)),
            scratch_shapes=[
                pltpu.VMEM((places, 128), bf16),
                pltpu.VMEM((places, 128), bf16),
                pltpu.VMEM((128, places), bf16),
                pltpu.VMEM((128, places), bf16),
                pltpu.VMEM((HEAD_DIM, places), f32),
            ],
        ),
        out_shape=jax.ShapeDtypeStruct((quarters, units, 3 * HEAD_DIM, quarter), bf16),
        compiler_params=pltpu.CompilerParams(vmem_limit_bytes=VMEM_LIMIT),
        name="self_backward",
    )(unit_lengths, projected, attended, back, totals)


def cross_forward_kernel(query_ref, pair_ref, out_ref, total_ref):
    places = query_ref.shape[1]
    keys = pair_ref[0, 0, 0:HEAD_DIM, :].astype(f32).T.astype(bf16)
    values = jnp.concatenate(
        [pair_ref[0, 0, HEAD_DIM:, :], jnp.ones((16, pair_ref.shape[3]), bf16)], axis=0
    )
    for start in range(0, places, KEYS):
        scores = dot_nn(keys, query_ref[:, start : start + KEYS])
        largest = jnp.max(scores, axis=0, keepdims=True)
        chances = jnp.exp2(scores - largest).astype(bf16)
        total = dot_nn(values, chances)
        row_total = total[HEAD_DIM : HEAD_DIM + 1]
        out_ref[:, start : start + KEYS] = (total[:HEAD_DIM] / row_total).astype(bf16)
        total_ref[0, :, start : start + KEYS] = largest + jnp.log2(row_total)


def cross_forward(queries, pairs):
    width, places = queries.shape
    units = pairs.shape[1]
    rows = pl.BlockSpec((HEAD_DIM, places), lambda h: (h, 0))
    return pl.pallas_call(
        cross_forward_kernel,
        grid=(width // HEAD_DIM,),
        in_specs=[
            rows,
            pl.BlockSpec((1, 1) + pairs.shape[2:], lambda h: (h // units, h % units, 0, 0)),
        ],
        out_specs=[rows, pl.BlockSpec((1, 1, places), lambda h: (h, 0, 0))],
        out_shape=[
            jax.ShapeDtypeStruct((width, places), bf16),
            jax.ShapeDtypeStruct((width // HEAD_DIM, 1, places), f32),
        ],
        compiler_params=pltpu.CompilerParams(vmem_limit_bytes=VMEM_LIMIT),
        name="cross_forward",
    )(queries, pairs)


def cross_backward_kernel(query_ref, pair_ref, out_ref, back_ref, total_ref, grad_ref, pair_grad_ref):
    places = query_ref.shape[1]
    rows = pair_ref.shape[3]
    at = row_index(64, rows)
    ones = jnp.where(at < 3, 1.0, 0.0)
    key_major = pair_ref[0, 0, 0:HEAD_DIM, :]
    keys = jnp.concatenate([key_major.astype(f32), ones], axis=0).T.astype(bf16)
    values = jnp.concatenate([pair_ref[0, 0, HEAD_DIM:, :].astype(f32), ones], axis=0).T.astype(bf16)
    blank = jnp.zeros((48, KEYS), bf16)
    back_key = jnp.zeros((HEAD_DIM, rows), f32)
    back_value = jnp.zeros((HEAD_DIM, rows), f32)
    for start in range(0, places, KEYS):
        span = slice(start, start + KEYS)
        plain, back = query_ref[:, span], back_ref[:, span]
        query = jnp.concatenate([plain, three_parts(-total_ref[0, :, span], False), blank], axis=0)
        delta = jnp.sum(back.astype(f32) * out_ref[:, span].astype(f32), axis=0, keepdims=True)
        back_rows = jnp.concatenate([back, three_parts(-delta, False), blank], axis=0)
        chances = jnp.exp2(dot_nn(keys, query))
        back_scores = (chances * dot_nn(values, back_rows)).astype(bf16)
        back_value = back_value + dot_nt(back, chances.astype(bf16))
        back_key = back_key + dot_nt(plain, back_scores)
        grad_ref[:, span] = (dot_nn(key_major, back_scores) * SCALING).astype(bf16)
    pair_grad_ref[0, 0, 0:HEAD_DIM, :] = (back_key * (1.0 / LOG2E)).astype(bf16)
    pair_grad_ref[0, 0, HEAD_DIM:, :] = back_value.astype(bf16)


def cross_backward(queries, pairs, attended, back, totals):
    width, places = queries.shape
    units = pairs.shape[1]
    rows = pl.BlockSpec((HEAD_DIM, places), lambda h: (h, 0))
    pair = pl.BlockSpec((1, 1) + pairs.shape[2:], lambda h: (h // units, h % units, 0, 0))
    return pl.pallas_call(
        cross_backward_kernel,
        grid=(width // HEAD_DIM,),
        in_specs=[rows, pair, rows, rows, pl.BlockSpec((1, 1, places), lambda h: (h, 0, 0))],
        out_specs=[rows, pair],
        out_shape=[
            jax.ShapeDtypeStruct((width, places), bf16),
            jax.ShapeDtypeStruct(pairs.shape, bf16),
        ],
        compiler_params=pltpu.CompilerParams(vmem_limit_bytes=VMEM_LIMIT),
        name="cross_backward",
    )(queries, pairs, attended, back, totals)


def layer_norm(summed, gain_row, bias_row):
    average = jnp.mean(summed, axis=-1, keepdims=True)
    centred = summed - average
    variance = jnp.mean(centred * centred, axis=-1, keepdims=True)
    return centred * lax.rsqrt(variance + EPSILON) * gain_row + bias_row


def gelu_exact(inner_act):
    return jax.nn.gelu(inner_act, approximate=False)


def product(spec, left, right):
    return jnp.einsum(spec, left, right, preferred_element_type=f32)


def per_device(
    hidden,
    bank,
    indices,
    lengths,
    cotangent,
    query_self,
    key_self,
    value_self,
    out_self,
    query_cross,
    key_cross,
    value_cross,
    out_cross,
    up_weight,
    down_weight,
    norm_gain,
    norm_bias,
):
    shard_count = lax.axis_size("shard")
    context_count = lax.axis_size("ctx")
    tensor_count = lax.axis_size("tp")
    shard_index = lax.axis_index("shard")
    context_index = lax.axis_index("ctx")
    tensor_index = lax.axis_index("tp")
    group_sequences, device_places, model_width = hidden.shape
    units = HEADS // context_count
    group_width = units * HEAD_DIM
    quarter = device_places * tensor_count
    shard_rows = query_self.shape[0]
    piece_rows = shard_rows // context_count

    swap = [
        (c * tensor_count + z, z * context_count + c)
        for c in range(context_count)
        for z in range(tensor_count)
    ]

    def to_plane(rows):
        received = lax.all_to_all(rows, "tp", split_axis=0, concat_axis=0, tiled=True)
        return received.reshape(quarter, rows.shape[-1])

    def from_plane(rows):
        blocks = rows.reshape(tensor_count, device_places, rows.shape[-1])
        return lax.all_to_all(blocks, "tp", split_axis=0, concat_axis=0, tiled=True)

    def over_context(parts):
        return lax.all_to_all(parts, "ctx", split_axis=0, concat_axis=0, tiled=True)

    group_lengths = lax.dynamic_slice_in_dim(
        lengths, shard_index * group_sequences, group_sequences
    )
    length = group_lengths[tensor_index]
    unit_lengths = jnp.full((units,), length, jnp.int32)

    def by_unit(weights):
        stacked = jnp.stack([w.reshape(-1, units, HEAD_DIM) for w in weights], axis=2)
        return stacked.reshape(weights[0].shape[0], -1)

    local_self = by_unit([query_self, key_self, value_self])
    local_pair = by_unit([key_cross, value_cross])
    self_width, pair_width = local_self.shape[1], local_pair.shape[1]
    own = lax.ppermute(jnp.concatenate([local_self, local_pair], axis=1), ("ctx", "tp"), swap)
    own = lax.all_gather(own, "shard", axis=0, tiled=True)
    own_self, own_pair = own[:, :self_width], own[:, self_width:]

    def gather_all(columns):
        rows = lax.dynamic_slice_in_dim(columns, context_index * piece_rows, piece_rows, 0)
        everything = lax.all_gather(rows, ("tp", "shard", "ctx"), axis=0, tiled=True)
        return everything.reshape(tensor_count, model_width, columns.shape[1])

    norms = jnp.concatenate([norm_gain, norm_bias], axis=0).T
    bundle = gather_all(
        jnp.concatenate([out_self.T, query_cross, out_cross.T, local_self, norms], axis=1)
    )
    out_self_t = bundle[:, :, :group_width]
    query_cross_w = bundle[:, :, group_width : 2 * group_width]
    out_cross_t = bundle[:, :, 2 * group_width : 3 * group_width]
    self_w = bundle[:, :, 3 * group_width : 3 * group_width + self_width]
    norm_rows = bundle[0, :, 3 * group_width + self_width :].T.astype(f32)
    gain_rows, bias_rows = norm_rows[:3], norm_rows[3:]
    feed = gather_all(jnp.concatenate([up_weight, down_weight.T], axis=1))
    feed_width = up_weight.shape[1]
    up_w, down_t = feed[:, :, :feed_width], feed[:, :, feed_width:]

    places = context_index * quarter + jnp.arange(quarter, dtype=jnp.int32)
    valid_rows = (places < length).astype(f32)[:, None]

    x_low = to_plane(hidden)
    x_all = lax.all_gather(x_low, "ctx", axis=0, tiled=True)
    query_scale = jnp.where(jnp.arange(3 * HEAD_DIM) < HEAD_DIM, QUERY_SCALE, 1.0).astype(f32)
    projected = product("df,pd->fp", own_self, x_all).reshape(units, 3 * HEAD_DIM, -1)
    projected = (projected * query_scale[None, :, None]).astype(bf16)
    self_out, self_total = self_forward(unit_lengths, projected, context_count)
    self_att = over_context(self_out).reshape(context_count, group_width, quarter)

    bank_local = bank.shape[1]
    retrieved = indices.shape[1]
    owner_tensor = indices[0] // bank_local
    local_rows = indices[0] - owner_tensor * bank_local
    owned = (owner_tensor == tensor_index)[:, None]
    picked = jnp.where(owned, jnp.take(bank[0], local_rows, axis=0), jnp.zeros((), bf16))
    picked = lax.all_to_all(
        picked.reshape(tensor_count, -1, model_width), "tp", split_axis=0, concat_axis=0, tiled=True
    )
    picked = jnp.sum(picked.astype(f32), axis=0).astype(bf16)
    lists = lax.all_gather(picked, "ctx", axis=0, tiled=False)
    selected = lax.all_to_all(lists, "tp", split_axis=0, concat_axis=0, tiled=True).reshape(
        retrieved, model_width
    )
    own_pairs = product("df,kd->fk", own_pair, selected).astype(bf16)
    pairs = lax.all_gather(
        own_pairs.reshape(units, 2 * HEAD_DIM, retrieved), "ctx", axis=0, tiled=False
    )

    x_float = x_low.astype(f32)
    branch_one = product("tnp,tdn->pd", self_att, out_self_t)
    first_sum = x_float + branch_one
    first = layer_norm(first_sum, gain_rows[0], bias_rows[0])
    first_low = first.astype(bf16)
    cross_query = (product("tdn,pd->tnp", query_cross_w, first_low) * QUERY_SCALE).astype(bf16)
    cross_query = cross_query.reshape(HEADS * HEAD_DIM, quarter)
    cross_out, cross_total = cross_forward(cross_query, pairs)
    cross_att = cross_out.reshape(tensor_count, group_width, quarter)
    branch_two = product("tnp,tdn->pd", cross_att, out_cross_t)
    second_sum = first + branch_two
    second = layer_norm(second_sum, gain_rows[1], bias_rows[1])
    second_low = second.astype(bf16)
    inner_act = product("pd,tdf->tpf", second_low, up_w)
    active_float, gelu_pull = jax.vjp(gelu_exact, inner_act)
    active = active_float.astype(bf16)
    branch_three = product("tpf,tdf->pd", active, down_t)
    third_sum = second + branch_three
    output = layer_norm(third_sum, gain_rows[2], bias_rows[2])
    output = from_plane(output.astype(bf16))

    def valid_squares(matrix):
        return jnp.sum(valid_rows * matrix * matrix)

    square_terms = jnp.stack(
        [
            valid_squares(matrix)
            for matrix in (x_float, branch_one, first, branch_two, second, branch_three)
        ]
    )

    def norm_back(summed, layer_index, back_in):
        normed, pullback = jax.vjp(
            layer_norm, summed, gain_rows[layer_index], bias_rows[layer_index]
        )
        return pullback(back_in)

    back_output = to_plane(cotangent).astype(f32) * valid_rows
    back_third, gain_three, bias_three = norm_back(third_sum, 2, back_output)
    back_three = back_third.astype(bf16)
    back_active = product("pd,tdf->tpf", back_three, down_t)
    back_inner = gelu_pull(back_active)[0].astype(bf16)
    back_down = product("pd,tpf->tdf", back_three, active)
    back_up = product("pd,tpf->tdf", second_low, back_inner)
    back_second = back_third + product("tpf,tdf->pd", back_inner, up_w)
    back_second_sum, gain_two, bias_two = norm_back(second_sum, 1, back_second)
    back_two = back_second_sum.astype(bf16)
    back_cross = product("tdn,pd->tnp", out_cross_t, back_two).astype(bf16)
    back_out_cross = product("pd,tnp->tdn", back_two, cross_att)
    back_query, back_pairs = cross_backward(
        cross_query, pairs, cross_out, back_cross.reshape(cross_out.shape), cross_total
    )
    back_query = back_query.reshape(tensor_count, group_width, quarter)
    back_query_cross = product("pd,tnp->tdn", first_low, back_query)
    back_first = back_second_sum + product("tnp,tdn->pd", back_query, query_cross_w)
    back_first_sum, gain_one, bias_one = norm_back(first_sum, 0, back_first)
    back_one = back_first_sum.astype(bf16)
    back_self = product("tdn,pd->tnp", out_self_t, back_one).astype(bf16)
    back_out_self = product("pd,tnp->tdn", back_one, self_att)
    back_self = over_context(back_self.reshape(context_count, units, HEAD_DIM, quarter))

    back_pairs = jnp.sum(over_context(back_pairs).astype(f32), axis=0).astype(bf16)
    back_pairs = back_pairs.reshape(pair_width, retrieved)
    back_selected = product("fk,df->kd", back_pairs, own_pair).astype(bf16)
    back_selected = over_context(back_selected.reshape(context_count, -1, model_width))
    back_selected = jnp.sum(back_selected.astype(f32), axis=0).astype(bf16)
    back_lists = lax.all_gather(back_selected, "tp", axis=0, tiled=False)
    back_rows = over_context(back_lists).reshape(retrieved, model_width)
    back_rows = jnp.where(owned, back_rows.astype(f32), 0.0)
    back_bank = jnp.zeros(bank.shape[1:], f32).at[local_rows].add(back_rows)[None]

    back_projected = self_backward(unit_lengths, projected, self_out, back_self, self_total)
    back_parts = over_context(back_projected).reshape(context_count, self_width, quarter)
    back_hidden = back_first_sum + product("tfp,tdf->pd", back_parts, self_w)
    back_hidden = from_plane(back_hidden.astype(bf16)).astype(f32)

    def reduce_own(gradient):
        pieces = gradient.astype(bf16).reshape(shard_count * tensor_count, -1, gradient.shape[1])
        pieces = lax.all_to_all(pieces, ("shard", "tp"), split_axis=0, concat_axis=0, tiled=True)
        piece = jnp.sum(pieces.astype(f32), axis=0).astype(bf16)
        piece = lax.ppermute(piece, ("ctx", "tp"), swap)
        return lax.all_gather(piece, "ctx", axis=0, tiled=True)

    def reduce_all(gradient):
        rows = gradient.astype(bf16).reshape(tensor_count * model_width, gradient.shape[2])
        piece = lax.psum_scatter(rows, ("tp", "shard", "ctx"), scatter_dimension=0, tiled=True)
        return lax.all_gather(piece, "ctx", axis=0, tiled=True)

    back_pair_w = reduce_own(product("kd,fk->df", selected, back_pairs))
    back_feed = reduce_all(jnp.concatenate([back_up, back_down], axis=2))
    back_mixed = reduce_all(
        jnp.concatenate([back_out_self, back_query_cross, back_out_cross], axis=2)
    )
    back_self_w = reduce_own(
        product(
            "qpd,qfp->df",
            x_all.reshape(context_count, quarter, model_width),
            back_projected.reshape(context_count, self_width, quarter),
        )
    )

    def apart(stacked, count):
        split = stacked.reshape(shard_rows, units, count, HEAD_DIM)
        return [split[:, :, at].reshape(shard_rows, group_width).astype(f32) for at in range(count)]

    back_query_self, back_key_self, back_value_self = apart(back_self_w, 3)
    back_key_cross, back_value_cross = apart(back_pair_w, 2)
    back_mixed = back_mixed.astype(f32)
    back_feed = back_feed.astype(f32)

    square_total, gain_total, bias_total = lax.psum(
        (
            square_terms,
            jnp.stack([gain_one, gain_two, gain_three]),
            jnp.stack([bias_one, bias_two, bias_three]),
        ),
        ("shard", "ctx", "tp"),
    )
    token_total = jnp.sum(lengths).astype(f32) * model_width
    statistics = jnp.sqrt(square_total / token_total)
    back_gain = lax.dynamic_slice_in_dim(gain_total, shard_index * shard_rows, shard_rows, 1)
    back_bias = lax.dynamic_slice_in_dim(bias_total, shard_index * shard_rows, shard_rows, 1)
    return (
        output,
        back_hidden,
        back_bank,
        back_query_self,
        back_key_self,
        back_value_self,
        back_mixed[:, :group_width].T,
        back_mixed[:, group_width : 2 * group_width],
        back_key_cross,
        back_value_cross,
        back_mixed[:, 2 * group_width :].T,
        back_feed[:, :feed_width],
        back_feed[:, feed_width:].T,
        back_gain,
        back_bias,
        statistics,
    )


def solution(mesh):
    return jax.shard_map(
        per_device,
        mesh=mesh,
        in_specs=(
            P("shard", ("ctx", "tp"), None),
            P(("shard", "ctx"), "tp", None),
            P(("shard", "ctx"), None),
            P(),
            P("shard", ("ctx", "tp"), None),
            P("shard", "tp"),
            P("shard", "tp"),
            P("shard", "tp"),
            P("tp", "shard"),
            P("shard", "tp"),
            P("shard", "tp"),
            P("shard", "tp"),
            P("tp", "shard"),
            P("shard", "tp"),
            P("tp", "shard"),
            P(None, "shard"),
            P(None, "shard"),
        ),
        out_specs=(
            P("shard", ("ctx", "tp"), None),
            P("shard", ("ctx", "tp"), None),
            P(("shard", "ctx"), "tp", None),
            P("shard", "tp"),
            P("shard", "tp"),
            P("shard", "tp"),
            P("tp", "shard"),
            P("shard", "tp"),
            P("shard", "tp"),
            P("shard", "tp"),
            P("tp", "shard"),
            P("shard", "tp"),
            P("tp", "shard"),
            P(None, "shard"),
            P(None, "shard"),
            P(),
        ),
        check_vma=False,
    )
```

```python
import functools

import jax
import jax.numpy as jnp
from jax import lax
from jax.experimental import pallas as pl
from jax.experimental.pallas import tpu as pltpu
from jax.sharding import PartitionSpec as P

HEADS = 12
HEAD_DIM = 64
BLK = 256

EPSILON = 1e-05
NEGATIVE = -1e30
LOG2E = 1.4426950408889634
SCALING = HEAD_DIM**-0.5
QUERY_SCALE = SCALING * LOG2E

KEYS = 512
QUERIES = 1024
VMEM_LIMIT = 56 * 2**20

bf16 = jnp.bfloat16
f32 = jnp.float32

CONTEXT, TENSOR, LENGTH, UNIT_LENGTHS = 0, 1, 2, 3


def lasting(microseconds):
    return pl.CostEstimate(
        flops=int(microseconds * 1.1e9), bytes_accessed=0, transcendentals=0
    )


def dot_nn(left, right):
    return lax.dot_general(left, right, (((1,), (0,)), ((), ())), preferred_element_type=f32)


def dot_nt(left, right):
    return lax.dot_general(left, right, (((1,), (1,)), ((), ())), preferred_element_type=f32)


def dot_tn(left, right):
    return lax.dot_general(left, right, (((0,), (0,)), ((), ())), preferred_element_type=f32)


def dot_tt(left, right):
    return lax.dot_general(left, right, (((0,), (1,)), ((), ())), preferred_element_type=f32)


def row_index(rows, columns):
    return lax.broadcasted_iota(jnp.int32, (rows, columns), 0)


def place_index(rows, columns, start):
    return lax.broadcasted_iota(jnp.int32, (rows, columns), 1) + start


def three_parts(row, ones_row):
    high = row.astype(bf16).astype(f32)
    rest = row - high
    middle = rest.astype(bf16).astype(f32)
    lowest = rest - middle
    at = row_index(16, row.shape[1])
    last = jnp.where(at == 3, 1.0, 0.0) if ones_row else jnp.zeros_like(at, f32)
    rows = jnp.where(at == 0, high, jnp.where(at == 1, middle, jnp.where(at == 2, lowest, last)))
    return rows.astype(bf16)


def self_forward_kernel(meta_ref, x_ref, *refs, begin):
    out_refs, (total_ref, keys, values, held) = refs[:-4], refs[-4:]
    length = meta_ref[UNIT_LENGTHS + begin + pl.program_id(0)]
    places = x_ref.shape[2]
    quarter_tiles = out_refs[0].shape[2] // QUERIES
    per_query = QUERIES // KEYS
    half = BLK
    key_tiles = (length + KEYS - 1) // KEYS

    def prepare(tile, _):
        start = pl.multiple_of(tile * KEYS, KEYS)
        rows = x_ref[0, HEAD_DIM : 2 * HEAD_DIM, pl.ds(start, KEYS)].astype(f32)
        at, place = row_index(16, KEYS), place_index(16, KEYS, start)
        mask = jnp.where((at == 0) & (place >= length), NEGATIVE, 0.0)
        stacked = jnp.concatenate([rows, mask, jnp.zeros((48, KEYS), f32)], axis=0)
        keys[pl.ds(start, KEYS), :] = stacked.T.astype(bf16)
        values[0:HEAD_DIM, pl.ds(start, KEYS)] = x_ref[
            0, 2 * HEAD_DIM : 3 * HEAD_DIM, pl.ds(start, KEYS)
        ]
        return 0

    lax.fori_loop(0, key_tiles, prepare, 0)
    values[HEAD_DIM : HEAD_DIM + 16, :] = jnp.ones((16, places), bf16)

    def query_tile(index, _):
        first_query = pl.multiple_of(index * QUERIES, QUERIES)
        ones_row = jnp.where(row_index(16, QUERIES) == 0, 1.0, 0.0).astype(bf16)
        queries = jnp.concatenate(
            [x_ref[0, 0:HEAD_DIM, pl.ds(first_query, QUERIES)], ones_row, jnp.zeros((48, QUERIES), bf16)],
            axis=0,
        )

        def score(tile):
            start = pl.multiple_of(tile * KEYS, KEYS)
            scores = dot_nn(keys[pl.ds(start, KEYS), :], queries)
            held[lax.rem(tile, 2)] = scores
            return jnp.max(scores, axis=0, keepdims=True)

        def step(tile, carry):
            largest, total, next_largest = carry
            updated = jnp.maximum(largest, next_largest)
            start = pl.multiple_of(tile * KEYS, KEYS)
            chances = jnp.exp2(held[lax.rem(tile, 2)] - updated).astype(bf16)
            total = total * jnp.exp2(largest - updated) + dot_nn(
                values[:, pl.ds(start, KEYS)], chances
            )
            return updated, total, score(jnp.minimum(tile + 1, key_tiles - 1))

        largest = jnp.full((1, QUERIES), NEGATIVE, f32)
        total = jnp.zeros((HEAD_DIM + 16, QUERIES), f32)
        largest, total, _ = lax.fori_loop(
            0, jnp.minimum(index * per_query, key_tiles), step, (largest, total, score(0))
        )

        def part(low, high, start, size, largest, total):
            scores = dot_nn(keys[pl.ds(start, size), :], queries[:, low:high])
            before = largest[:, low:high]
            updated = jnp.maximum(before, jnp.max(scores, axis=0, keepdims=True))
            chances = jnp.exp2(scores - updated).astype(bf16)
            summed = dot_nn(values[:, pl.ds(start, size)], chances)
            return updated, total[:, low:high] * jnp.exp2(before - updated) + summed

        for at in range(per_query):

            def diagonal(_, carry):
                largest, total = carry
                low = at * KEYS
                start = pl.multiple_of(first_query + low, KEYS)
                pieces = [(largest[:, :low], total[:, :low])] if low else []
                pieces.append(part(low, low + half, start, half, largest, total))
                pieces.append(part(low + half, low + KEYS, start, KEYS, largest, total))
                if low + KEYS < QUERIES:
                    pieces.append(part(low + KEYS, QUERIES, start, KEYS, largest, total))
                return tuple(jnp.concatenate(piece, axis=1) for piece in zip(*pieces))

            present = (index * per_query + at < key_tiles).astype(jnp.int32)
            largest, total = lax.fori_loop(0, present, diagonal, (largest, total))
        row_total = total[HEAD_DIM : HEAD_DIM + 1]
        inner = pl.multiple_of(lax.rem(index, quarter_tiles) * QUERIES, QUERIES)
        result = (total[:HEAD_DIM] / row_total).astype(bf16)
        slot = (index // quarter_tiles) ^ meta_ref[CONTEXT]
        for at, out_ref in enumerate(out_refs):

            @pl.when(slot == at)
            def _():
                out_ref[0, :, pl.ds(inner, QUERIES)] = result

        total_ref[0, :, pl.ds(first_query, QUERIES)] = largest + jnp.log2(row_total)
        return 0

    lax.fori_loop(0, places // QUERIES, query_tile, 0)


def self_forward(meta, projected, quarters, begin, units):
    places = projected.shape[2]
    quarter = places // quarters
    return pl.pallas_call(
        functools.partial(self_forward_kernel, begin=begin),
        grid_spec=pltpu.PrefetchScalarGridSpec(
            num_scalar_prefetch=1,
            grid=(units,),
            in_specs=[pl.BlockSpec((1, 3 * HEAD_DIM, places), lambda u, n: (begin + u, 0, 0))],
            out_specs=[pl.BlockSpec((1, HEAD_DIM, quarter), lambda u, n: (u, 0, 0))] * quarters
            + [pl.BlockSpec((1, 1, places), lambda u, n: (u, 0, 0))],
            scratch_shapes=[
                pltpu.VMEM((places, 128), bf16),
                pltpu.VMEM((HEAD_DIM + 16, places), bf16),
                pltpu.VMEM((2, KEYS, QUERIES), f32),
            ],
        ),
        out_shape=[jax.ShapeDtypeStruct((units, HEAD_DIM, quarter), bf16)] * quarters
        + [jax.ShapeDtypeStruct((units, 1, places), f32)],
        cost_estimate=lasting(20 * units),
        compiler_params=pltpu.CompilerParams(vmem_limit_bytes=VMEM_LIMIT),
        name="self_forward",
    )(meta, projected)


def self_backward_kernel(meta_ref, x_ref, total_ref, *refs, begin):
    keys, values, queries, backs, query_sum = refs[-5:]
    quarters = (len(refs) - 5) // 3
    out_refs, back_refs, grad_refs = (refs[at * quarters : (at + 1) * quarters] for at in range(3))
    length = meta_ref[UNIT_LENGTHS + begin + pl.program_id(0)]
    places = x_ref.shape[2]
    quarter_tiles = out_refs[0].shape[2] // KEYS
    half = BLK
    key_tiles = (length + KEYS - 1) // KEYS

    def prepare(tile, _):
        start = pl.multiple_of(tile * KEYS, KEYS)
        key_rows = x_ref[0, HEAD_DIM : 2 * HEAD_DIM, pl.ds(start, KEYS)].astype(f32)
        value_rows = x_ref[0, 2 * HEAD_DIM : 3 * HEAD_DIM, pl.ds(start, KEYS)].astype(f32)
        at, place = row_index(16, KEYS), place_index(16, KEYS, start)
        ones = jnp.where(at < 3, 1.0, 0.0)
        mask = jnp.where((at == 3) & (place >= length), NEGATIVE, ones)
        blank = jnp.zeros((48, KEYS), f32)
        keys[pl.ds(start, KEYS), :] = jnp.concatenate([key_rows, mask, blank], axis=0).T.astype(bf16)
        values[pl.ds(start, KEYS), :] = jnp.concatenate([value_rows, ones, blank], axis=0).T.astype(
            bf16
        )
        blank = blank.astype(bf16)
        queries[:, pl.ds(start, KEYS)] = jnp.concatenate(
            [
                x_ref[0, 0:HEAD_DIM, pl.ds(start, KEYS)],
                three_parts(-total_ref[0, :, pl.ds(start, KEYS)], True),
                blank,
            ],
            axis=0,
        )
        slot = (tile // quarter_tiles) ^ meta_ref[CONTEXT]
        inner = pl.multiple_of(lax.rem(tile, quarter_tiles) * KEYS, KEYS)
        for at in range(quarters):

            @pl.when(slot == at)
            def _():
                back = back_refs[at][0, :, pl.ds(inner, KEYS)]
                out = out_refs[at][0, :, pl.ds(inner, KEYS)]
                delta = jnp.sum(back.astype(f32) * out.astype(f32), axis=0, keepdims=True)
                backs[:, pl.ds(start, KEYS)] = jnp.concatenate(
                    [back, three_parts(-delta, False), blank], axis=0
                )

        query_sum[:, pl.ds(start, KEYS)] = jnp.zeros((HEAD_DIM, KEYS), f32)
        return 0

    lax.fori_loop(0, key_tiles, prepare, 0)

    def tile_terms(key_start, key_size, query_start, query_size, back_key, back_value):
        query = queries[:, pl.ds(query_start, query_size)]
        back = backs[:, pl.ds(query_start, query_size)]
        chances = jnp.exp2(dot_nn(keys[pl.ds(key_start, key_size), :], query))
        back_chances = dot_nn(values[pl.ds(key_start, key_size), :], back)
        back_scores = (chances * back_chances).astype(bf16)
        back_value = back_value + dot_nt(back[:HEAD_DIM], chances.astype(bf16))
        back_key = back_key + dot_nt(query[:HEAD_DIM], back_scores)
        query_sum[:, pl.ds(query_start, query_size)] += dot_nn(
            x_ref[0, HEAD_DIM : 2 * HEAD_DIM, pl.ds(key_start, key_size)], back_scores
        )
        return back_key, back_value

    def write(tile, rows, value):
        inner = pl.multiple_of(lax.rem(tile, quarter_tiles) * KEYS, KEYS)
        slot = (tile // quarter_tiles) ^ meta_ref[CONTEXT]
        for at in range(quarters):

            @pl.when(slot == at)
            def _():
                grad_refs[at][0, rows, pl.ds(inner, KEYS)] = value

    def key_tile(index, _):
        start = pl.multiple_of(index * KEYS, KEYS)
        second = pl.multiple_of(start + half, half)
        blank = jnp.zeros((HEAD_DIM, half), f32)
        first_part = tile_terms(start, half, start, KEYS, blank, blank)
        second_part = tile_terms(second, half, second, half, blank, blank)
        begun = tuple(jnp.concatenate(pair, axis=1) for pair in zip(first_part, second_part))

        def step(tile, carry):
            return tile_terms(start, KEYS, pl.multiple_of(tile * KEYS, KEYS), KEYS, *carry)

        back_key, back_value = lax.fori_loop(index + 1, key_tiles, step, begun)
        both = jnp.concatenate([back_key * (1.0 / LOG2E), back_value], axis=0).astype(bf16)
        write(index, slice(HEAD_DIM, 3 * HEAD_DIM), both)
        return 0

    lax.fori_loop(0, key_tiles, key_tile, 0)

    def finish(tile, _):
        start = pl.multiple_of(tile * KEYS, KEYS)
        write(tile, slice(0, HEAD_DIM), (query_sum[:, pl.ds(start, KEYS)] * SCALING).astype(bf16))
        return 0

    lax.fori_loop(0, key_tiles, finish, 0)

    def clear(tile, _):
        write(tile, slice(0, 3 * HEAD_DIM), jnp.zeros((3 * HEAD_DIM, KEYS), bf16))
        return 0

    lax.fori_loop(key_tiles, places // KEYS, clear, 0)


def self_backward(meta, projected, totals, attended, back, begin, origin):
    units, places = 1, projected.shape[2]
    quarters = len(attended)
    quarter = places // quarters
    return pl.pallas_call(
        functools.partial(self_backward_kernel, begin=begin),
        grid_spec=pltpu.PrefetchScalarGridSpec(
            num_scalar_prefetch=1,
            grid=(units,),
            in_specs=[
                pl.BlockSpec((1, 3 * HEAD_DIM, places), lambda u, n: (begin + u, 0, 0)),
                pl.BlockSpec((1, 1, places), lambda u, n: (begin - origin + u, 0, 0)),
            ]
            + [pl.BlockSpec((1, HEAD_DIM, quarter), lambda u, n: (begin - origin + u, 0, 0))]
            * quarters
            + [pl.BlockSpec((1, HEAD_DIM, quarter), lambda u, n: (begin + u, 0, 0))] * quarters,
            out_specs=[pl.BlockSpec((1, 3 * HEAD_DIM, quarter), lambda u, n: (u, 0, 0))] * quarters,
            scratch_shapes=[
                pltpu.VMEM((places, 128), bf16),
                pltpu.VMEM((places, 128), bf16),
                pltpu.VMEM((128, places), bf16),
                pltpu.VMEM((128, places), bf16),
                pltpu.VMEM((HEAD_DIM, places), f32),
            ],
        ),
        out_shape=[jax.ShapeDtypeStruct((units, 3 * HEAD_DIM, quarter), bf16)] * quarters,
        cost_estimate=lasting(30 * units),
        compiler_params=pltpu.CompilerParams(vmem_limit_bytes=VMEM_LIMIT),
        name="self_backward",
    )(meta, projected, totals, *attended, *back)


def cross_forward_kernel(meta_ref, query_ref, pair_ref, out_ref, total_ref):
    places = query_ref.shape[1]
    keys = pair_ref[0, 0, 0:HEAD_DIM, :].astype(f32).T.astype(bf16)
    values = jnp.concatenate(
        [pair_ref[0, 0, HEAD_DIM:, :], jnp.ones((16, pair_ref.shape[3]), bf16)], axis=0
    )
    for start in range(0, places, KEYS):
        scores = dot_nn(keys, query_ref[:, start : start + KEYS])
        largest = jnp.max(scores, axis=0, keepdims=True)
        chances = jnp.exp2(scores - largest).astype(bf16)
        total = dot_nn(values, chances)
        row_total = total[HEAD_DIM : HEAD_DIM + 1]
        out_ref[:, start : start + KEYS] = (total[:HEAD_DIM] / row_total).astype(bf16)
        total_ref[0, :, start : start + KEYS] = largest + jnp.log2(row_total)


def pair_spec(pairs):
    units = pairs.shape[1]

    def place(h, meta):
        return h // units, h % units, 0, 0

    return pl.BlockSpec((1, 1) + pairs.shape[2:], place)


def cross_forward(meta, queries, pairs):
    width, places = queries.shape
    rows = pl.BlockSpec((HEAD_DIM, places), lambda h, n: (h, 0))
    return pl.pallas_call(
        cross_forward_kernel,
        grid_spec=pltpu.PrefetchScalarGridSpec(
            num_scalar_prefetch=1,
            grid=(width // HEAD_DIM,),
            in_specs=[rows, pair_spec(pairs)],
            out_specs=[rows, pl.BlockSpec((1, 1, places), lambda h, n: (h, 0, 0))],
        ),
        out_shape=[
            jax.ShapeDtypeStruct((width, places), bf16),
            jax.ShapeDtypeStruct((width // HEAD_DIM, 1, places), f32),
        ],
        cost_estimate=lasting(25),
        compiler_params=pltpu.CompilerParams(vmem_limit_bytes=VMEM_LIMIT),
        name="cross_forward",
    )(meta, queries, pairs)


def cross_backward_kernel(
    meta_ref, query_ref, pair_ref, out_ref, back_ref, total_ref, grad_ref, pair_grad_ref
):
    places = query_ref.shape[1]
    rows = pair_ref.shape[3]
    at = row_index(64, rows)
    ones = jnp.where(at < 3, 1.0, 0.0)
    key_major = pair_ref[0, 0, 0:HEAD_DIM, :]
    keys = jnp.concatenate([key_major.astype(f32), ones], axis=0).T.astype(bf16)
    values = jnp.concatenate([pair_ref[0, 0, HEAD_DIM:, :].astype(f32), ones], axis=0).T.astype(bf16)
    blank = jnp.zeros((48, KEYS), bf16)
    back_key = jnp.zeros((HEAD_DIM, rows), f32)
    back_value = jnp.zeros((HEAD_DIM, rows), f32)
    for start in range(0, places, KEYS):
        span = slice(start, start + KEYS)
        plain, back = query_ref[:, span], back_ref[:, span]
        query = jnp.concatenate([plain, three_parts(-total_ref[0, :, span], False), blank], axis=0)
        delta = jnp.sum(back.astype(f32) * out_ref[:, span].astype(f32), axis=0, keepdims=True)
        back_rows = jnp.concatenate([back, three_parts(-delta, False), blank], axis=0)
        chances = jnp.exp2(dot_nn(keys, query))
        back_scores = (chances * dot_nn(values, back_rows)).astype(bf16)
        back_value = back_value + dot_nt(back, chances.astype(bf16))
        back_key = back_key + dot_nt(plain, back_scores)
        grad_ref[:, span] = (dot_nn(key_major, back_scores) * SCALING).astype(bf16)
    pair_grad_ref[0, 0, 0:HEAD_DIM, :] = (back_key * (1.0 / LOG2E)).astype(bf16)
    pair_grad_ref[0, 0, HEAD_DIM:, :] = back_value.astype(bf16)


def cross_backward(meta, queries, pairs, attended, back, totals):
    width, places = queries.shape
    rows = pl.BlockSpec((HEAD_DIM, places), lambda h, n: (h, 0))
    return pl.pallas_call(
        cross_backward_kernel,
        grid_spec=pltpu.PrefetchScalarGridSpec(
            num_scalar_prefetch=1,
            grid=(width // HEAD_DIM,),
            in_specs=[
                rows,
                pair_spec(pairs),
                rows,
                rows,
                pl.BlockSpec((1, 1, places), lambda h, n: (h, 0, 0)),
            ],
            out_specs=[rows, pair_spec(pairs)],
        ),
        out_shape=[
            jax.ShapeDtypeStruct((width, places), bf16),
            jax.ShapeDtypeStruct(pairs.shape, bf16),
        ],
        cost_estimate=lasting(36),
        compiler_params=pltpu.CompilerParams(vmem_limit_bytes=VMEM_LIMIT),
        name="cross_backward",
    )(meta, queries, pairs, attended, back, totals)


def normed(summed):
    centred = summed - jnp.mean(summed, axis=-1, keepdims=True)
    variance = jnp.mean(centred * centred, axis=-1, keepdims=True)
    inverse = lax.rsqrt(variance + EPSILON)
    return centred * inverse, inverse


def normed_back(normal, inverse, scaled):
    shared = jnp.mean(scaled, axis=-1, keepdims=True)
    along = jnp.mean(scaled * normal, axis=-1, keepdims=True)
    return (scaled - shared - normal * along) * inverse


def valid_column(meta_ref, quarter, rows):
    start = meta_ref[CONTEXT] * quarter + pl.program_id(0) * rows
    place = lax.broadcasted_iota(jnp.int32, (rows, 1), 0) + start
    return jnp.where(place < meta_ref[LENGTH], 1.0, 0.0)


def add_rows(sum_ref, *terms):
    @pl.when(pl.program_id(0) == 0)
    def _():
        sum_ref[...] = jnp.zeros_like(sum_ref)

    for at, term in enumerate(terms):
        sum_ref[at : at + 1, :] += jnp.sum(term, axis=0, keepdims=True)


def project_kernel(meta_ref, weight_ref, *refs, parts, rows):
    piece_refs, (x_ref, out_ref) = refs[:-2], refs[-2:]
    at_row = lax.broadcasted_iota(jnp.int32, (weight_ref.shape[0], 1), 0)
    scale = jnp.where(lax.rem(at_row, 3 * HEAD_DIM) < HEAD_DIM, QUERY_SCALE, 1.0)
    quarter = x_ref.shape[0] // (len(piece_refs) // parts)
    for at, piece_ref in enumerate(piece_refs):
        step, part = divmod(at, parts)
        result = (dot_nt(weight_ref[...], piece_ref[...]) * scale).astype(bf16)
        for block in range(quarter // (rows * parts)):
            place = (block * parts + part) * rows
            start = pl.multiple_of((meta_ref[CONTEXT] ^ step) * quarter + place, rows)
            run = slice(block * rows, (block + 1) * rows)
            x_ref[pl.ds(start, rows), :] = piece_ref[run, :]
            out_ref[:, pl.ds(start, rows)] = result[:, run]


def project(meta, weight, pieces, parts, rows):
    places, width = pieces[0].shape[0] * len(pieces), pieces[0].shape[1]
    whole = pl.BlockSpec(memory_space=pltpu.VMEM)
    return pl.pallas_call(
        functools.partial(project_kernel, parts=parts, rows=rows),
        in_specs=[pl.BlockSpec(memory_space=pltpu.SMEM)] + [whole] * (1 + len(pieces)),
        out_specs=[whole, whole],
        out_shape=[
            jax.ShapeDtypeStruct((places, width), bf16),
            jax.ShapeDtypeStruct((weight.shape[0], places), bf16),
        ],
        cost_estimate=lasting(10),
        compiler_params=pltpu.CompilerParams(vmem_limit_bytes=VMEM_LIMIT),
        name="project",
    )(meta, weight, *pieces)


def first_kernel(
    meta_ref, x_ref, norm_ref, out_w_ref, query_w_ref, *refs, quarter
):
    att_refs, (sum_ref, low_ref, query_ref, total_ref) = refs[:-4], refs[-4:]
    groups = query_w_ref.shape[0]
    branch = None
    for at in range(groups):
        att = jnp.concatenate([ref[...] for ref in att_refs[at::groups]], axis=0)
        term = dot_tt(att, out_w_ref[meta_ref[CONTEXT] ^ at])
        branch = term if branch is None else branch + term
    x = x_ref[...].astype(f32)
    summed = x + branch
    normal, _ = normed(summed)
    first = normal * norm_ref[0:1, :] + norm_ref[3:4, :]
    first_low = first.astype(bf16)
    sum_ref[...] = summed
    low_ref[...] = first_low
    query = jnp.concatenate([dot_nn(first_low, query_w_ref[at]) for at in range(groups)], axis=1)
    query_ref[...] = (query * QUERY_SCALE).T.astype(bf16)
    valid = valid_column(meta_ref, quarter, x.shape[0])
    add_rows(total_ref, valid * x * x, valid * branch * branch, valid * first * first)


def whole_spec(array):
    zeros = (0,) * array.ndim
    return pl.BlockSpec(array.shape, lambda b, n: zeros, pipeline_mode=pl.Buffered(1))


def first_step(meta, x_all, norms, out_w, query_w, att, rows):
    width = x_all.shape[1]
    quarter = att[0].shape[1]
    blocks = quarter // rows
    tokens = pl.BlockSpec((rows, width), lambda b, n: (b, 0))
    turned = pl.BlockSpec((width, rows), lambda b, n: (0, b))
    return pl.pallas_call(
        functools.partial(first_kernel, quarter=quarter),
        grid_spec=pltpu.PrefetchScalarGridSpec(
            num_scalar_prefetch=1,
            grid=(blocks,),
            in_specs=[
                pl.BlockSpec((rows, width), lambda b, n: (n[CONTEXT] * blocks + b, 0)),
                whole_spec(norms),
                whole_spec(out_w),
                whole_spec(query_w),
            ]
            + [pl.BlockSpec((piece.shape[0], rows), lambda b, n: (0, b)) for piece in att],
            out_specs=[tokens, tokens, turned, pl.BlockSpec((8, width), lambda b, n: (0, 0))],
        ),
        out_shape=[
            jax.ShapeDtypeStruct((quarter, width), f32),
            jax.ShapeDtypeStruct((quarter, width), bf16),
            jax.ShapeDtypeStruct((width, quarter), bf16),
            jax.ShapeDtypeStruct((8, width), f32),
        ],
        cost_estimate=lasting(8),
        compiler_params=pltpu.CompilerParams(vmem_limit_bytes=VMEM_LIMIT),
        name="first_step",
    )(meta, x_all, norms, out_w, query_w, *att)


def gelu_and_slope(inner):
    chance = 0.5 * (1.0 + lax.erf(inner * 0.7071067811865476))
    density = jnp.exp2(inner * inner * (-0.5 * LOG2E)) * 0.3989422804014327
    return inner * chance, chance + inner * density


def feed_kernel(
    meta_ref, att_ref, sum_ref, norm_ref, out_w_ref, feed_ref, *refs, quarter
):
    groups, width = feed_ref.shape[0], sum_ref.shape[1]
    cot_ref, output_ref, *refs = refs
    low_ref, active_ref, inner_ref, back_three_ref, back_two_ref, back_sum_ref, back_att_ref = refs[:7]
    total_ref, slope_ref = refs[7:]
    rows = sum_ref.shape[0]
    part = out_w_ref.shape[2]
    gain = [norm_ref[at : at + 1, :] for at in range(3)]
    bias = [norm_ref[3 + at : 4 + at, :] for at in range(3)]
    branch_two = None
    for at in range(groups):
        term = dot_tt(att_ref[at * part : (at + 1) * part, :], out_w_ref[at])
        branch_two = term if branch_two is None else branch_two + term
    normal, _ = normed(sum_ref[...])
    normal_two, inverse_two = normed(normal * gain[0] + bias[0] + branch_two)
    second = normal_two * gain[1] + bias[1]
    second_low = second.astype(bf16)
    low_ref[...] = second_low
    branch_three = None
    for at in range(groups):
        inner = dot_nn(second_low, feed_ref[at, :, :width])
        active, slope = gelu_and_slope(inner)
        active = active.astype(bf16)
        active_ref[:, at * width : (at + 1) * width] = active
        slope_ref[:, at * width : (at + 1) * width] = slope
        term = dot_nt(active, feed_ref[at, :, width:])
        branch_three = term if branch_three is None else branch_three + term
    normal_three, inverse_three = normed(second + branch_three)
    output_ref[...] = (normal_three * gain[2] + bias[2]).astype(bf16)
    valid = valid_column(meta_ref, quarter, rows)
    back_output = cot_ref[...].astype(f32) * valid
    back_third = normed_back(normal_three, inverse_three, back_output * gain[2])
    back_three = back_third.astype(bf16)
    back_three_ref[...] = back_three
    back_second = back_third
    for at in range(groups):
        back_active = dot_nn(back_three, feed_ref[at, :, width:])
        back_inner = (back_active * slope_ref[:, at * width : (at + 1) * width]).astype(bf16)
        inner_ref[:, at * width : (at + 1) * width] = back_inner
        back_second = back_second + dot_nt(back_inner, feed_ref[at, :, :width])
    back_second_sum = normed_back(normal_two, inverse_two, back_second * gain[1])
    back_sum_ref[...] = back_second_sum
    back_two = back_second_sum.astype(bf16)
    back_two_ref[...] = back_two
    back_att = jnp.concatenate([dot_nn(back_two, out_w_ref[at]) for at in range(groups)], axis=1)
    back_att_ref[...] = back_att.T.astype(bf16)
    add_rows(
        total_ref,
        valid * branch_two * branch_two,
        valid * second * second,
        valid * branch_three * branch_three,
        back_second * normal_two,
        back_output * normal_three,
        back_second,
        back_output,
    )


def feed_step(meta, att, first_sum, norms, out_w, feed, cotangent, rows):
    quarter, width = first_sum.shape
    groups = feed.shape[0]
    hidden_width = groups * width
    tokens = pl.BlockSpec((rows, width), lambda b, n: (b, 0))
    wide = pl.BlockSpec((rows, hidden_width), lambda b, n: (b, 0))
    turned = pl.BlockSpec((width, rows), lambda b, n: (0, b))
    return pl.pallas_call(
        functools.partial(feed_kernel, quarter=quarter),
        grid_spec=pltpu.PrefetchScalarGridSpec(
            num_scalar_prefetch=1,
            grid=(quarter // rows,),
            in_specs=[
                turned,
                tokens,
                whole_spec(norms),
                whole_spec(out_w),
                whole_spec(feed),
                tokens,
            ],
            out_specs=[tokens, tokens, wide, wide, tokens, tokens, tokens, turned]
            + [pl.BlockSpec((8, width), lambda b, n: (0, 0))],
            scratch_shapes=[pltpu.VMEM((rows, hidden_width), f32)],
        ),
        out_shape=[
            jax.ShapeDtypeStruct((quarter, width), bf16),
            jax.ShapeDtypeStruct((quarter, width), bf16),
            jax.ShapeDtypeStruct((quarter, hidden_width), bf16),
            jax.ShapeDtypeStruct((quarter, hidden_width), bf16),
            jax.ShapeDtypeStruct((quarter, width), bf16),
            jax.ShapeDtypeStruct((quarter, width), bf16),
            jax.ShapeDtypeStruct((quarter, width), f32),
            jax.ShapeDtypeStruct((width, quarter), bf16),
            jax.ShapeDtypeStruct((8, width), f32),
        ],
        cost_estimate=lasting(45),
        compiler_params=pltpu.CompilerParams(vmem_limit_bytes=VMEM_LIMIT),
        name="feed_step",
    )(meta, att, first_sum, norms, out_w, feed, cotangent)


def last_kernel(meta_ref, query_ref, back_sum_ref, sum_ref, norm_ref, query_w_ref, out_w_ref, *refs):
    back_refs, (back_ref, low_ref, total_ref) = refs[:-3], refs[-3:]
    groups, _, part = query_w_ref.shape
    back_first = back_sum_ref[...]
    for at in range(groups):
        back_first = back_first + dot_tt(query_ref[at * part : (at + 1) * part, :], query_w_ref[at])
    normal, inverse = normed(sum_ref[...])
    back_first_sum = normed_back(normal, inverse, back_first * norm_ref[0:1, :])
    back_ref[...] = back_first_sum
    back_one = back_first_sum.astype(bf16)
    low_ref[...] = back_one
    for at, ref in enumerate(back_refs):
        ref[...] = dot_nn(back_one, out_w_ref[meta_ref[CONTEXT] ^ at]).T.astype(bf16)
    add_rows(total_ref, back_first * normal, back_first)


def last_step(meta, back_query, back_second_sum, first_sum, norms, query_w, out_w, rows):
    quarter, width = first_sum.shape
    groups, _, part = query_w.shape
    tokens = pl.BlockSpec((rows, width), lambda b, n: (b, 0))
    turned = pl.BlockSpec((width, rows), lambda b, n: (0, b))
    return pl.pallas_call(
        last_kernel,
        grid_spec=pltpu.PrefetchScalarGridSpec(
            num_scalar_prefetch=1,
            grid=(quarter // rows,),
            in_specs=[
                turned,
                tokens,
                tokens,
                whole_spec(norms),
                whole_spec(query_w),
                whole_spec(out_w),
            ],
            out_specs=[pl.BlockSpec((part, rows), lambda b, n: (0, b))] * groups
            + [tokens, tokens, pl.BlockSpec((8, width), lambda b, n: (0, 0))],
        ),
        out_shape=[jax.ShapeDtypeStruct((part, quarter), bf16)] * groups
        + [
            jax.ShapeDtypeStruct((quarter, width), f32),
            jax.ShapeDtypeStruct((quarter, width), bf16),
            jax.ShapeDtypeStruct((8, width), f32),
        ],
        cost_estimate=lasting(8),
        compiler_params=pltpu.CompilerParams(vmem_limit_bytes=VMEM_LIMIT),
        name="last_step",
    )(meta, back_query, back_second_sum, first_sum, norms, query_w, out_w)


def hidden_kernel(meta_ref, back_ref, weight_ref, *refs):
    groups = weight_ref.shape[0]
    whole_refs, part_refs, out_ref = refs[: -1 - groups], refs[-1 - groups : -1], refs[-1]
    total = back_ref[...]
    for at in range(groups):
        group = meta_ref[CONTEXT] ^ at
        part = jnp.concatenate([ref[group] for ref in whole_refs] + [part_refs[at][...]], axis=0)
        total = total + dot_tt(part, weight_ref[group])
    out_ref[...] = total.astype(bf16)


def hidden_step(meta, back_first_sum, weights, parts, rows):
    quarter, width = back_first_sum.shape

    def columns(part):
        lead = part.shape[:-1]
        zeros = (0,) * len(lead)
        return pl.BlockSpec(lead + (rows,), lambda b, n: zeros + (b,))

    return pl.pallas_call(
        hidden_kernel,
        grid_spec=pltpu.PrefetchScalarGridSpec(
            num_scalar_prefetch=1,
            grid=(quarter // rows,),
            in_specs=[
                pl.BlockSpec((rows, width), lambda b, n: (b, 0)),
                whole_spec(weights),
            ]
            + [columns(part) for part in parts],
            out_specs=pl.BlockSpec((rows, width), lambda b, n: (b, 0)),
        ),
        out_shape=jax.ShapeDtypeStruct((quarter, width), bf16),
        cost_estimate=lasting(8),
        compiler_params=pltpu.CompilerParams(vmem_limit_bytes=VMEM_LIMIT),
        name="hidden_step",
    )(meta, back_first_sum, weights, *parts)


def turned_once(pairs):
    @pl.when(pl.program_id(0) == 0)
    def _():
        for source, target in pairs:
            target[...] = source[...].astype(f32).T.astype(bf16)


def put_halves(meta_ref, keep_ref, send_ref, low, high, result):
    shards, rows = keep_ref.shape[1:3]
    core = lax.rem(meta_ref[CONTEXT], 2)
    result = result.astype(bf16)
    for half, (even_ref, odd_ref) in enumerate(((keep_ref, send_ref), (send_ref, keep_ref))):

        @pl.when(core == half)
        def _():
            for shard in range(shards):
                start = 2 * shard * rows
                even_ref[0, shard, :, low:high] = result[start : start + rows]
                odd_ref[0, shard, :, low:high] = result[start + rows : start + 2 * rows]


def feed_grad_kernel(
    meta_ref, low_ref, inner_ref, back_ref, active_ref, two_ref, cross_ref, keep_ref, send_ref, *turned
):
    width = low_ref.shape[1]
    put = functools.partial(put_halves, meta_ref, keep_ref, send_ref)
    turned_once(zip((low_ref, back_ref, two_ref), turned))
    put(0, width, dot_nn(turned[0][...], inner_ref[...]))
    put(width, 2 * width, dot_nn(turned[1][...], active_ref[...]))
    put(2 * width, keep_ref.shape[3], dot_nt(turned[2][...], cross_ref[...]))


def feed_grad(meta, second_low, back_inner, back_three, active, back_two, cross_att, shards):
    tokens, width = second_low.shape
    groups = active.shape[1] // width
    part = width // groups
    left = pl.BlockSpec((tokens, width), lambda b, n: (0, 0))
    right = pl.BlockSpec((tokens, width), lambda b, n: (0, b))
    half = (shards, width // (2 * shards), 2 * width + part)
    return pl.pallas_call(
        feed_grad_kernel,
        grid_spec=pltpu.PrefetchScalarGridSpec(
            num_scalar_prefetch=1,
            grid=(groups,),
            in_specs=[
                left,
                right,
                left,
                right,
                left,
                pl.BlockSpec((part, tokens), lambda b, n: (b, 0)),
            ],
            out_specs=[pl.BlockSpec((1,) + half, lambda b, n: (b, 0, 0, 0))] * 2,
            scratch_shapes=[pltpu.VMEM((width, tokens), bf16)] * 3,
        ),
        out_shape=[jax.ShapeDtypeStruct((groups,) + half, bf16)] * 2,
        cost_estimate=lasting(18),
        compiler_params=pltpu.CompilerParams(vmem_limit_bytes=VMEM_LIMIT),
        name="feed_grad",
    )(meta, second_low, back_inner, back_three, active, back_two, cross_att)


def mixed_grad_kernel(
    meta_ref, one_ref, low_ref, selected_ref, query_ref, pair_ref, *refs
):
    keep_ref, send_ref, *turned = refs[-5:]
    att_refs = refs[:-5]
    turned_once(zip((one_ref, low_ref, selected_ref), turned))
    slot = pl.program_id(0) ^ meta_ref[CONTEXT]
    att = None
    for at in range(4):
        piece = jnp.concatenate([ref[...] for ref in att_refs[at::4]], axis=0)
        att = piece if att is None else jnp.where(slot == at, piece, att)
    result = jnp.concatenate(
        [
            dot_nt(turned[0][...], att),
            dot_nt(turned[1][...], query_ref[...]),
            dot_nt(turned[2][...], pair_ref[0]),
        ],
        axis=1,
    )
    put_halves(meta_ref, keep_ref, send_ref, 0, result.shape[1], result)


def mixed_grad(meta, back_one, first_low, selected, back_query, back_pairs, att, shards):
    tokens, width = back_one.shape
    groups = 4
    part = width // groups
    pair_width, retrieved = back_pairs.shape[1:]
    half = (shards, width // (2 * shards), 2 * part + pair_width)
    return pl.pallas_call(
        mixed_grad_kernel,
        grid_spec=pltpu.PrefetchScalarGridSpec(
            num_scalar_prefetch=1,
            grid=(groups,),
            in_specs=[
                whole_spec(back_one),
                whole_spec(first_low),
                whole_spec(selected),
                pl.BlockSpec((part, tokens), lambda b, n: (b, 0)),
                pl.BlockSpec((1, pair_width, retrieved), lambda b, n: (b, 0, 0)),
            ]
            + [whole_spec(piece) for piece in att],
            out_specs=[pl.BlockSpec((1,) + half, lambda b, n: (b, 0, 0, 0))] * 2,
            scratch_shapes=[
                pltpu.VMEM((width, tokens), bf16),
                pltpu.VMEM((width, tokens), bf16),
                pltpu.VMEM((width, retrieved), bf16),
            ],
        ),
        out_shape=[jax.ShapeDtypeStruct((groups,) + half, bf16)] * 2,
        cost_estimate=lasting(14),
        compiler_params=pltpu.CompilerParams(vmem_limit_bytes=VMEM_LIMIT),
        name="mixed_grad",
    )(meta, back_one, first_low, selected, back_query, back_pairs, *att)


def own_grad_kernel(meta_ref, x_ref, *refs):
    part_refs, out_ref = refs[:-1], refs[-1]
    quarter = part_refs[0].shape[1]
    total = None
    for at, part_ref in enumerate(part_refs):
        start = pl.multiple_of((meta_ref[CONTEXT] ^ at) * quarter, quarter)
        term = dot_nn(part_ref[...], x_ref[pl.ds(start, quarter), :])
        total = term if total is None else total + term
    out_ref[...] = total.T.astype(bf16)


def own_grad(meta, x_all, parts):
    whole = pl.BlockSpec(memory_space=pltpu.VMEM)
    return pl.pallas_call(
        own_grad_kernel,
        in_specs=[pl.BlockSpec(memory_space=pltpu.SMEM)] + [whole] * (1 + len(parts)),
        out_specs=whole,
        out_shape=jax.ShapeDtypeStruct((x_all.shape[1], parts[0].shape[0]), bf16),
        cost_estimate=lasting(7),
        compiler_params=pltpu.CompilerParams(vmem_limit_bytes=VMEM_LIMIT),
        name="own_grad",
    )(meta, x_all, *parts)


def product(spec, left, right):
    return jnp.einsum(spec, left, right, preferred_element_type=f32)


def turn(array, axis, step):
    count = lax.axis_size(axis)
    return lax.ppermute(array, axis, [(at, at ^ step) for at in range(count)])


def to_others(parts, axis):
    return [parts[0]] + [turn(parts[at], axis, at) for at in range(1, len(parts))]


def gather_context(array):
    far = turn(array, "ctx", 2)
    return [array, turn(array, "ctx", 1), far, turn(far, "ctx", 1)]


def gather(array, axis, dim):
    step = 1
    while step < lax.axis_size(axis):
        other = turn(array, axis, step)
        later = (lax.axis_index(axis) & step) > 0
        array = jnp.concatenate(
            [jnp.where(later, other, array), jnp.where(later, array, other)], axis=dim
        )
        step *= 2
    return array


def in_slots(pieces, index):
    for step in (1, 2):
        later = (index & step) > 0
        pieces = [jnp.where(later, pieces[at ^ step], pieces[at]) for at in range(len(pieces))]
    return pieces


def gather_direct(array, axis, dim):
    pieces = [array] + [turn(array, axis, at) for at in range(1, 4)]
    return jnp.concatenate(in_slots(pieces, lax.axis_index(axis)), axis=dim)


def exchange(parts, axes):
    return lax.all_to_all(parts, axes, split_axis=0, concat_axis=0, tiled=True)


def add_up(pieces):
    total = pieces[0].astype(f32)
    for piece in pieces[1:]:
        total = total + piece.astype(f32)
    return total


def sum_everywhere(vector):
    steps = []
    for axis in ("ctx", "tp", "shard"):
        step = 1
        while step < lax.axis_size(axis):
            vector = vector + turn(vector, axis, step)
            steps.append(vector)
            step *= 2
    return steps


class StagedSum:
    def __init__(self, keep, send):
        self.terms, self.send = [keep], send

    def beside(self, kernel):
        self.terms[1:] = [after(term, kernel) for term in self.terms[1:]]

    def over_core(self):
        self.terms.append(turn(self.send, "ctx", 1))

    def over_shard(self):
        count, index = lax.axis_size("shard"), lax.axis_index("shard")

        def part(at):
            return add_up([lax.dynamic_index_in_dim(t, at, 1, keepdims=False) for t in self.terms])

        if count == 2:
            self.send = part(1 - index).astype(bf16)
            own = [lax.dynamic_index_in_dim(t, index, 1, keepdims=False) for t in self.terms]
            self.terms = own + [turn(self.send, "shard", 1)]
        else:
            self.send = jnp.moveaxis(add_up(self.terms).astype(bf16), 1, 0)
            self.terms = [jnp.sum(exchange(self.send, "shard").astype(f32), axis=0).astype(bf16)]

    def over_x(self):
        rows = self.terms[0].shape[1] // 2
        index = lax.axis_index("ctx") // 2

        def part(at):
            return [lax.dynamic_slice_in_dim(t, at * rows, rows, 1) for t in self.terms]

        self.send = add_up(part(1 - index)).astype(bf16)
        self.terms = part(index) + [turn(self.send, "ctx", 2)]

    def send_of_quarter(self):
        self.terms = [add_up(self.terms).astype(bf16)]
        return self.terms[0]

    def over_tensor(self):
        self.send = add_up(self.terms).astype(bf16)
        index = lax.axis_index("tp")
        parts = [
            lax.dynamic_index_in_dim(self.send, index ^ at, 0, keepdims=False)
            for at in range(self.send.shape[0])
        ]
        self.terms = to_others(parts, "tp")

    def total(self):
        self.send = add_up(self.terms).astype(bf16)
        return self.send

    def spread(self):
        total = self.send
        for step in (2, 1):
            other = turn(total, "ctx", step)
            later = (lax.axis_index("ctx") & step) > 0
            total = jnp.concatenate(
                [jnp.where(later, other, total), jnp.where(later, total, other)], axis=0
            )
        return total.astype(f32)


def after(value, *earlier):
    return lax.optimization_barrier((value,) + earlier)[0]


def per_device(
    hidden,
    bank,
    indices,
    lengths,
    cotangent,
    query_self,
    key_self,
    value_self,
    out_self,
    query_cross,
    key_cross,
    value_cross,
    out_cross,
    up_weight,
    down_weight,
    norm_gain,
    norm_bias,
):
    context_count = lax.axis_size("ctx")
    tensor_count = lax.axis_size("tp")
    shard_index = lax.axis_index("shard")
    context_index = lax.axis_index("ctx")
    tensor_index = lax.axis_index("tp")
    group_sequences, device_places, model_width = hidden.shape
    units = HEADS // context_count
    group_width = units * HEAD_DIM
    quarter = device_places * tensor_count
    shard_rows = query_self.shape[0]
    piece_rows = shard_rows // context_count
    feed_width = up_weight.shape[1]

    swap = [
        (c * tensor_count + z, z * context_count + c)
        for c in range(context_count)
        for z in range(tensor_count)
    ]

    group_lengths = lax.dynamic_slice_in_dim(
        lengths, shard_index * group_sequences, group_sequences
    )
    length = group_lengths[tensor_index]
    meta = jnp.stack([context_index, tensor_index, length] + [length] * units).astype(jnp.int32)

    def by_unit(weights):
        stacked = jnp.stack([w.reshape(-1, units, HEAD_DIM) for w in weights], axis=2)
        return stacked.reshape(weights[0].shape[0], -1)

    local_self = by_unit([query_self, key_self, value_self])
    local_pair = by_unit([key_cross, value_cross])
    self_width, pair_width = local_self.shape[1], local_pair.shape[1]

    def gather_all(columns):
        rows = lax.dynamic_slice_in_dim(columns, context_index * piece_rows, piece_rows, 0)
        everything = lax.all_gather(rows, ("tp", "shard", "ctx"), axis=0, tiled=True)
        return everything.reshape(tensor_count, model_width, columns.shape[1])

    bank_local = bank.shape[1]
    retrieved = indices.shape[1]
    owner_tensor = indices[0] // bank_local
    local_rows = indices[0] - owner_tensor * bank_local
    owned = (owner_tensor == tensor_index)[:, None]
    picked = jnp.where(owned, jnp.take(bank[0], local_rows, axis=0), jnp.zeros((), bf16))

    half = device_places // 2
    own_self = lax.ppermute(local_self.T, ("ctx", "tp"), swap)
    low, far = [], []
    for at in range(2):
        part = hidden[:, at * half : (at + 1) * half]
        part = exchange(after(part, own_self) if at else part, "tp").reshape(quarter // 2, model_width)
        low.append(part)
        far.append(turn(after(part, *far), "ctx", 2))
    own_self = gather(own_self, "shard", 1)
    far[1] = after(far[1], own_self)
    x_low = low[1]
    beside = [turn(part, "ctx", 1) for part in low]
    across = [turn(part, "ctx", 1) for part in far]
    picked = exchange(after(picked, x_low).reshape(tensor_count, -1, model_width), "tp")
    x_all, projected = project(meta, own_self, low + beside + far + across, 2, half)
    projected = projected.reshape(units, 3 * HEAD_DIM, -1)

    norms = jnp.concatenate([norm_gain, norm_bias], axis=0).T
    bundle = jnp.concatenate([out_self.T, query_cross, out_cross.T, local_pair, norms], axis=1)
    bundle = gather_all(after(bundle, x_low))
    out_self_t = bundle[:, :, :group_width]
    query_cross_w = bundle[:, :, group_width : 2 * group_width]
    out_cross_t = bundle[:, :, 2 * group_width : 3 * group_width]
    pair_w = bundle[:, :, 3 * group_width : 3 * group_width + pair_width]
    norm_rows = bundle[0, :, 3 * group_width + pair_width :].T.astype(f32)
    norm_rows = jnp.pad(norm_rows, ((0, 2), (0, 0)))
    feed = gather_all(after(jnp.concatenate([up_weight, down_weight.T], axis=1), x_low))

    self_out, self_totals, self_att = [], [], []

    def forward(begin, *ready):
        *out, total = self_forward(meta, after(projected, *ready), context_count, begin, 1)
        self_out.append(out)
        self_totals.append(total)
        self_att.extend(piece.reshape(-1, quarter) for piece in to_others(out, "ctx"))
        return total

    picked = jnp.sum(after(picked, projected).astype(f32), axis=0).astype(bf16)
    done = forward(0, picked)
    picked = after(lax.ppermute(picked, ("ctx", "tp"), swap), done)
    done = forward(1, picked, done)
    lists = [picked] + [turn(picked, "ctx", at) for at in range(1, context_count)]
    lists = [after(piece, done) for piece in lists]
    done = forward(2, *lists, done)
    selected = jnp.concatenate(in_slots(lists, context_index))
    cot = exchange(after(cotangent, done), "tp")
    pairs = product("tdf,kd->tfk", pair_w, selected).astype(bf16)
    pairs = pairs.reshape(context_count, units, 2 * HEAD_DIM, retrieved)
    first_sum, first_low, cross_query, first_totals = first_step(
        meta, after(x_all, pairs), norm_rows, out_self_t, query_cross_w, self_att, device_places
    )
    cross_att, cross_total = cross_forward(meta, cross_query, pairs)
    cot = after(cot, cross_att).reshape(quarter, model_width)
    fed = feed_step(meta, cross_att, first_sum, norm_rows, out_cross_t, feed, cot, device_places)
    output, second_low, active, back_inner, back_three, back_two, back_second_sum, back_cross, totals = fed
    shard_count = lax.axis_size("shard")
    feed_sum = StagedSum(
        *feed_grad(
            meta, second_low, back_inner, back_three, active, back_two, cross_att, shard_count
        )
    )
    feed_sum.over_core()
    output = exchange(output.reshape(tensor_count, device_places, model_width), "tp")
    back_query, back_pairs = cross_backward(
        meta, cross_query, pairs, cross_att, after(back_cross, feed_sum.send), cross_total
    )
    back_pairs = back_pairs.reshape(context_count, pair_width, retrieved)
    feed_sum.over_shard()
    back_selected = product("tfk,tdf->kd", back_pairs, pair_w).astype(bf16)
    back_selected = back_selected.reshape(context_count, -1, model_width)
    *back_self, back_first_sum, back_one, last_totals = last_step(
        meta,
        back_query,
        after(back_second_sum, output, feed_sum.send, back_selected),
        first_sum,
        norm_rows,
        query_cross_w,
        out_self_t,
        device_places,
    )
    back_selected = after(exchange(back_selected, "ctx"), back_one)
    back_self = [piece.reshape(units, HEAD_DIM, quarter) for piece in to_others(back_self, "ctx")]
    mixed_sum = StagedSum(
        *mixed_grad(
            meta, back_one, first_low, selected, back_query, back_pairs, self_att, shard_count
        )
    )
    self_w = gather_all(after(local_self, first_low))

    squares = jnp.sum(jnp.concatenate([first_totals[:3], totals[:3]], axis=0), axis=1)
    rows = jnp.stack(
        [
            last_totals[0],
            totals[3],
            totals[4],
            last_totals[1],
            totals[5],
            totals[6],
            jnp.pad(squares, (0, model_width - squares.shape[0])),
        ]
    )

    def backward(begin, *ready):
        return self_backward(
            meta,
            after(projected, *ready),
            self_totals[begin],
            self_out[begin],
            back_self,
            begin,
            begin,
        )

    def parts_of(grads):
        return [piece.reshape(-1, quarter) for piece in to_others(grads, "ctx")]

    back_selected = jnp.sum(back_selected.astype(f32), axis=0).astype(bf16)
    grads = [backward(0, mixed_sum.send, back_selected)]
    mixed_sum.over_core()
    back_rows = lax.ppermute(back_selected, ("ctx", "tp"), swap)
    for running in (feed_sum, mixed_sum):
        running.beside(grads[0][0])
    back_rows = after(back_rows, grads[0][0])
    feed_sum.over_x()
    mixed_sum.over_shard()

    back_parts = [exchange(jnp.concatenate(in_slots(grads[0], context_index)), "ctx")]
    grads.append(backward(1, back_rows, feed_sum.send, mixed_sum.send, *grads[0]))
    back_rows = [back_rows] + [turn(back_rows, "tp", at) for at in range(1, tensor_count)]
    back_rows = [after(piece, grads[1][0]) for piece in back_rows]
    back_parts = [after(back_parts[0], grads[1][0])]
    own_grads = []
    for running in (feed_sum, mixed_sum):
        running.beside(grads[1][0])
    feed_sum.over_tensor()
    mixed_sum.over_x()

    back_parts.append(exchange(jnp.concatenate(in_slots(grads[1], context_index)), "ctx"))
    ready = (feed_sum.send, mixed_sum.send, back_parts[0], *back_rows)
    grads.append(backward(2, *ready, *grads[1]))
    back_parts[1] = after(back_parts[1], grads[2][0])
    for running in (feed_sum, mixed_sum):
        running.beside(grads[2][0])
    back_parts += parts_of(grads[2])
    ready = (feed_sum.total(), mixed_sum.send_of_quarter(), back_parts[1])
    for at in range(units):
        own_grads.append(
            own_grad(meta, after(x_all, *ready), [p.reshape(-1, quarter) for p in grads[at]])
        )
    mixed_sum.terms = [after(term, back_parts[-1]) for term in mixed_sum.terms]
    mixed_sum.over_tensor()
    mixed_sum.total()
    rows_steps = sum_everywhere(after(rows, own_grads[2]))

    own_sum = jnp.concatenate(own_grads, axis=1)
    own_sum = own_sum.reshape(shard_count, -1, own_sum.shape[1])
    if shard_count == 2:
        mine = lax.dynamic_index_in_dim(own_sum, shard_index, 0, keepdims=False)
        other = lax.dynamic_index_in_dim(own_sum, 1 - shard_index, 0, keepdims=False)
        own_sum = add_up([mine, turn(other, "shard", 1)])
    else:
        own_sum = jnp.sum(exchange(own_sum, "shard").astype(f32), axis=0)
    own_sum = own_sum.astype(bf16).reshape(tensor_count, -1, own_sum.shape[-1])
    own_sum = [
        lax.dynamic_index_in_dim(own_sum, tensor_index ^ at, 0, keepdims=False)
        for at in range(tensor_count)
    ]
    own_sum = add_up(to_others(own_sum, "tp")).astype(bf16)
    own_sum = lax.ppermute(own_sum, ("ctx", "tp"), swap)

    back_hidden = hidden_step(meta, back_first_sum, self_w, back_parts, device_places)
    back_rows = jnp.concatenate(in_slots([after(p, back_hidden, own_sum) for p in back_rows], tensor_index))
    back_hidden = exchange(back_hidden.reshape(tensor_count, device_places, model_width), "tp")
    back_rows = jnp.where(owned, back_rows.astype(f32), 0.0)
    back_bank = jnp.zeros(bank.shape[1:], f32).at[local_rows].add(back_rows)[None]

    own_all = gather_direct(own_sum, "ctx", 0)
    back_mixed = mixed_sum.spread()
    back_feed = feed_sum.spread()
    rows = rows_steps[-1]
    shard_columns = lax.dynamic_slice_in_dim(rows, shard_index * shard_rows, shard_rows, 1)
    back_gain, back_bias = shard_columns[:3], shard_columns[3:6]
    token_total = jnp.sum(lengths).astype(f32) * model_width
    statistics = jnp.sqrt(rows[6, : squares.shape[0]] / token_total)

    def apart(stacked, count):
        split = stacked.reshape(shard_rows, units, count, HEAD_DIM)
        return [split[:, :, at].reshape(shard_rows, group_width).astype(f32) for at in range(count)]

    back_query_self, back_key_self, back_value_self = apart(own_all, 3)
    back_key_cross, back_value_cross = apart(back_mixed[:, 2 * group_width :], 2)
    return (
        output,
        back_hidden.astype(f32),
        back_bank,
        back_query_self,
        back_key_self,
        back_value_self,
        back_mixed[:, :group_width].T,
        back_mixed[:, group_width : 2 * group_width],
        back_key_cross,
        back_value_cross,
        back_feed[:, 2 * feed_width :].T,
        back_feed[:, :feed_width],
        back_feed[:, feed_width : 2 * feed_width].T,
        back_gain,
        back_bias,
        statistics,
    )


def solution(mesh):
    return jax.shard_map(
        per_device,
        mesh=mesh,
        in_specs=(
            P("shard", ("ctx", "tp"), None),
            P(("shard", "ctx"), "tp", None),
            P(("shard", "ctx"), None),
            P(),
            P("shard", ("ctx", "tp"), None),
            P("shard", "tp"),
            P("shard", "tp"),
            P("shard", "tp"),
            P("tp", "shard"),
            P("shard", "tp"),
            P("shard", "tp"),
            P("shard", "tp"),
            P("tp", "shard"),
            P("shard", "tp"),
            P("tp", "shard"),
            P(None, "shard"),
            P(None, "shard"),
        ),
        out_specs=(
            P("shard", ("ctx", "tp"), None),
            P("shard", ("ctx", "tp"), None),
            P(("shard", "ctx"), "tp", None),
            P("shard", "tp"),
            P("shard", "tp"),
            P("shard", "tp"),
            P("tp", "shard"),
            P("shard", "tp"),
            P("shard", "tp"),
            P("shard", "tp"),
            P("tp", "shard"),
            P("shard", "tp"),
            P("tp", "shard"),
            P(None, "shard"),
            P(None, "shard"),
            P(),
        ),
        check_vma=False,
    )
```

```python
import functools

import jax
import jax.numpy as jnp
from jax import lax
from jax.experimental import pallas as pl
from jax.experimental.pallas import tpu as pltpu
from jax.sharding import PartitionSpec as P

HEADS = 12
HEAD_DIM = 64
BLK = 256

EPSILON = 1e-05
NEGATIVE = -1e30
LOG2E = 1.4426950408889634
SCALING = HEAD_DIM**-0.5
QUERY_SCALE = SCALING * LOG2E

KEYS = 512
QUERIES = 1024
CROSS = 1024
VMEM_LIMIT = 56 * 2**20

bf16 = jnp.bfloat16
f32 = jnp.float32

CONTEXT, TENSOR, LENGTH, UNIT_LENGTHS = 0, 1, 2, 3


def lasting(microseconds):
    return pl.CostEstimate(
        flops=int(microseconds * 1.1e9), bytes_accessed=0, transcendentals=0
    )


def dot_nn(left, right):
    return lax.dot_general(left, right, (((1,), (0,)), ((), ())), preferred_element_type=f32)


def dot_nt(left, right):
    return lax.dot_general(left, right, (((1,), (1,)), ((), ())), preferred_element_type=f32)


def dot_tn(left, right):
    return lax.dot_general(left, right, (((0,), (0,)), ((), ())), preferred_element_type=f32)


def dot_tt(left, right):
    return lax.dot_general(left, right, (((0,), (1,)), ((), ())), preferred_element_type=f32)


def row_index(rows, columns):
    return lax.broadcasted_iota(jnp.int32, (rows, columns), 0)


def place_index(rows, columns, start):
    return lax.broadcasted_iota(jnp.int32, (rows, columns), 1) + start


def three_parts(row, ones_row):
    high = row.astype(bf16).astype(f32)
    rest = row - high
    middle = rest.astype(bf16).astype(f32)
    lowest = rest - middle
    at = row_index(16, row.shape[1])
    last = jnp.where(at == 3, 1.0, 0.0) if ones_row else jnp.zeros_like(at, f32)
    rows = jnp.where(at == 0, high, jnp.where(at == 1, middle, jnp.where(at == 2, lowest, last)))
    return rows.astype(bf16)


def self_forward_kernel(meta_ref, x_ref, *refs, begin):
    out_refs, (total_ref, keys, values, even, odd) = refs[:-5], refs[-5:]
    length = meta_ref[UNIT_LENGTHS + begin + pl.program_id(0)]
    places = x_ref.shape[2]
    quarter_tiles = out_refs[0].shape[2] // QUERIES
    per_query = QUERIES // KEYS
    half = BLK
    key_tiles = (length + KEYS - 1) // KEYS

    def prepare(tile, _):
        start = pl.multiple_of(tile * KEYS, KEYS)
        rows = x_ref[0, HEAD_DIM : 2 * HEAD_DIM, pl.ds(start, KEYS)].astype(f32)
        at, place = row_index(16, KEYS), place_index(16, KEYS, start)
        mask = jnp.where((at == 0) & (place >= length), NEGATIVE, 0.0)
        stacked = jnp.concatenate([rows, mask, jnp.zeros((48, KEYS), f32)], axis=0)
        keys[pl.ds(start, KEYS), :] = stacked.T.astype(bf16)
        values[0:HEAD_DIM, pl.ds(start, KEYS)] = x_ref[
            0, 2 * HEAD_DIM : 3 * HEAD_DIM, pl.ds(start, KEYS)
        ]
        return 0

    lax.fori_loop(0, key_tiles, prepare, 0)
    values[HEAD_DIM : HEAD_DIM + 16, :] = jnp.ones((16, places), bf16)

    def query_tile(index, _):
        first_query = pl.multiple_of(index * QUERIES, QUERIES)
        ones_row = jnp.where(row_index(16, QUERIES) == 0, 1.0, 0.0).astype(bf16)
        queries = jnp.concatenate(
            [x_ref[0, 0:HEAD_DIM, pl.ds(first_query, QUERIES)], ones_row, jnp.zeros((48, QUERIES), bf16)],
            axis=0,
        )

        def score(tile, held):
            start = pl.multiple_of(jnp.minimum(tile, key_tiles - 1) * KEYS, KEYS)
            scores = dot_nn(keys[pl.ds(start, KEYS), :], queries)
            held[...] = scores
            return jnp.max(scores, axis=0, keepdims=True)

        def step(tile, held, carry):
            largest, total, next_largest = carry
            updated = jnp.maximum(largest, next_largest)
            start = pl.multiple_of(tile * KEYS, KEYS)
            chances = jnp.exp2(held[...] - updated).astype(bf16)
            total = total * jnp.exp2(largest - updated) + dot_nn(
                values[:, pl.ds(start, KEYS)], chances
            )
            return updated, total

        def two_steps(pair, carry):
            upper = score(2 * pair + 1, odd)
            carry = step(2 * pair, even, carry)
            lower = score(2 * pair + 2, even)
            return *step(2 * pair + 1, odd, (*carry, upper)), lower

        count = jnp.minimum(index * per_query, key_tiles)
        largest = jnp.full((1, QUERIES), NEGATIVE, f32)
        total = jnp.zeros((HEAD_DIM + 16, QUERIES), f32)
        carry = lax.fori_loop(0, count // 2, two_steps, (largest, total, score(0, even)))

        def last_step_of(_, carry):
            return *step(count - 1, even, carry), carry[2]

        largest, total, _ = lax.fori_loop(0, lax.rem(count, 2), last_step_of, carry)

        def part(low, high, start, size, largest, total):
            scores = dot_nn(keys[pl.ds(start, size), :], queries[:, low:high])
            before = largest[:, low:high]
            updated = jnp.maximum(before, jnp.max(scores, axis=0, keepdims=True))
            chances = jnp.exp2(scores - updated).astype(bf16)
            summed = dot_nn(values[:, pl.ds(start, size)], chances)
            return updated, total[:, low:high] * jnp.exp2(before - updated) + summed

        for at in range(per_query):

            def diagonal(_, carry):
                largest, total = carry
                low = at * KEYS
                start = pl.multiple_of(first_query + low, KEYS)
                pieces = [(largest[:, :low], total[:, :low])] if low else []
                pieces.append(part(low, low + half, start, half, largest, total))
                pieces.append(part(low + half, low + KEYS, start, KEYS, largest, total))
                if low + KEYS < QUERIES:
                    pieces.append(part(low + KEYS, QUERIES, start, KEYS, largest, total))
                return tuple(jnp.concatenate(piece, axis=1) for piece in zip(*pieces))

            present = (index * per_query + at < key_tiles).astype(jnp.int32)
            largest, total = lax.fori_loop(0, present, diagonal, (largest, total))
        row_total = total[HEAD_DIM : HEAD_DIM + 1]
        inner = pl.multiple_of(lax.rem(index, quarter_tiles) * QUERIES, QUERIES)
        result = (total[:HEAD_DIM] / row_total).astype(bf16)
        slot = (index // quarter_tiles) ^ meta_ref[CONTEXT]
        for at, out_ref in enumerate(out_refs):

            @pl.when(slot == at)
            def _():
                out_ref[0, :, pl.ds(inner, QUERIES)] = result

        total_ref[0, :, pl.ds(first_query, QUERIES)] = largest + jnp.log2(row_total)
        return 0

    lax.fori_loop(0, places // QUERIES, query_tile, 0)


def self_forward(meta, projected, quarters, begin, units):
    places = projected.shape[2]
    quarter = places // quarters
    return pl.pallas_call(
        functools.partial(self_forward_kernel, begin=begin),
        grid_spec=pltpu.PrefetchScalarGridSpec(
            num_scalar_prefetch=1,
            grid=(units,),
            in_specs=[pl.BlockSpec((1, 3 * HEAD_DIM, places), lambda u, n: (begin + u, 0, 0))],
            out_specs=[pl.BlockSpec((1, HEAD_DIM, quarter), lambda u, n: (u, 0, 0))] * quarters
            + [pl.BlockSpec((1, 1, places), lambda u, n: (u, 0, 0))],
            scratch_shapes=[
                pltpu.VMEM((places, 128), bf16),
                pltpu.VMEM((HEAD_DIM + 16, places), bf16),
                pltpu.VMEM((KEYS, QUERIES), f32),
                pltpu.VMEM((KEYS, QUERIES), f32),
            ],
        ),
        out_shape=[jax.ShapeDtypeStruct((units, HEAD_DIM, quarter), bf16)] * quarters
        + [jax.ShapeDtypeStruct((units, 1, places), f32)],
        cost_estimate=lasting(20 * units),
        compiler_params=pltpu.CompilerParams(vmem_limit_bytes=VMEM_LIMIT),
        name="self_forward",
    )(meta, projected)


def self_backward_kernel(meta_ref, x_ref, total_ref, *refs, begin):
    keys, values, queries, backs, query_sum = refs[-5:]
    quarters = (len(refs) - 5) // 3
    out_refs, back_refs, grad_refs = (refs[at * quarters : (at + 1) * quarters] for at in range(3))
    length = meta_ref[UNIT_LENGTHS + begin + pl.program_id(0)]
    places = x_ref.shape[2]
    quarter_tiles = out_refs[0].shape[2] // KEYS
    half = BLK
    key_tiles = (length + KEYS - 1) // KEYS

    def prepare(tile, _):
        start = pl.multiple_of(tile * KEYS, KEYS)
        key_rows = x_ref[0, HEAD_DIM : 2 * HEAD_DIM, pl.ds(start, KEYS)].astype(f32)
        value_rows = x_ref[0, 2 * HEAD_DIM : 3 * HEAD_DIM, pl.ds(start, KEYS)].astype(f32)
        at, place = row_index(16, KEYS), place_index(16, KEYS, start)
        ones = jnp.where(at < 3, 1.0, 0.0)
        mask = jnp.where((at == 3) & (place >= length), NEGATIVE, ones)
        blank = jnp.zeros((48, KEYS), f32)
        keys[pl.ds(start, KEYS), :] = jnp.concatenate([key_rows, mask, blank], axis=0).T.astype(bf16)
        values[pl.ds(start, KEYS), :] = jnp.concatenate([value_rows, ones, blank], axis=0).T.astype(
            bf16
        )
        blank = blank.astype(bf16)
        queries[:, pl.ds(start, KEYS)] = jnp.concatenate(
            [
                x_ref[0, 0:HEAD_DIM, pl.ds(start, KEYS)],
                three_parts(-total_ref[0, :, pl.ds(start, KEYS)], True),
                blank,
            ],
            axis=0,
        )
        slot = (tile // quarter_tiles) ^ meta_ref[CONTEXT]
        inner = pl.multiple_of(lax.rem(tile, quarter_tiles) * KEYS, KEYS)
        for at in range(quarters):

            @pl.when(slot == at)
            def _():
                back = back_refs[at][0, :, pl.ds(inner, KEYS)]
                out = out_refs[at][0, :, pl.ds(inner, KEYS)]
                delta = jnp.sum(back.astype(f32) * out.astype(f32), axis=0, keepdims=True)
                backs[:, pl.ds(start, KEYS)] = jnp.concatenate(
                    [back, three_parts(-delta, False), blank], axis=0
                )

        query_sum[:, pl.ds(start, KEYS)] = jnp.zeros((HEAD_DIM, KEYS), f32)
        return 0

    lax.fori_loop(0, key_tiles, prepare, 0)

    def tile_terms(key_start, key_size, query_start, query_size, back_key, back_value):
        query = queries[:, pl.ds(query_start, query_size)]
        back = backs[:, pl.ds(query_start, query_size)]
        chances = jnp.exp2(dot_nn(keys[pl.ds(key_start, key_size), :], query))
        back_chances = dot_nn(values[pl.ds(key_start, key_size), :], back)
        back_scores = (chances * back_chances).astype(bf16)
        back_value = back_value + dot_nt(back[:HEAD_DIM], chances.astype(bf16))
        back_key = back_key + dot_nt(query[:HEAD_DIM], back_scores)
        query_sum[:, pl.ds(query_start, query_size)] += dot_nn(
            x_ref[0, HEAD_DIM : 2 * HEAD_DIM, pl.ds(key_start, key_size)], back_scores
        )
        return back_key, back_value

    def write(tile, rows, value):
        inner = pl.multiple_of(lax.rem(tile, quarter_tiles) * KEYS, KEYS)
        slot = (tile // quarter_tiles) ^ meta_ref[CONTEXT]
        for at in range(quarters):

            @pl.when(slot == at)
            def _():
                grad_refs[at][0, rows, pl.ds(inner, KEYS)] = value

    def key_tile(index, _):
        start = pl.multiple_of(index * KEYS, KEYS)
        second = pl.multiple_of(start + half, half)
        blank = jnp.zeros((HEAD_DIM, half), f32)
        first_part = tile_terms(start, half, start, KEYS, blank, blank)
        second_part = tile_terms(second, half, second, half, blank, blank)
        begun = tuple(jnp.concatenate(pair, axis=1) for pair in zip(first_part, second_part))

        def step(tile, carry):
            return tile_terms(start, KEYS, pl.multiple_of(tile * KEYS, KEYS), KEYS, *carry)

        back_key, back_value = lax.fori_loop(index + 1, key_tiles, step, begun)
        both = jnp.concatenate([back_key * (1.0 / LOG2E), back_value], axis=0).astype(bf16)
        write(index, slice(HEAD_DIM, 3 * HEAD_DIM), both)
        return 0

    lax.fori_loop(0, key_tiles, key_tile, 0)

    def finish(tile, _):
        start = pl.multiple_of(tile * KEYS, KEYS)
        write(tile, slice(0, HEAD_DIM), (query_sum[:, pl.ds(start, KEYS)] * SCALING).astype(bf16))
        return 0

    lax.fori_loop(0, key_tiles, finish, 0)

    def clear(tile, _):
        write(tile, slice(0, 3 * HEAD_DIM), jnp.zeros((3 * HEAD_DIM, KEYS), bf16))
        return 0

    lax.fori_loop(key_tiles, places // KEYS, clear, 0)


def self_backward(meta, projected, totals, attended, back, begin, origin):
    units, places = 1, projected.shape[2]
    quarters = len(attended)
    quarter = places // quarters
    return pl.pallas_call(
        functools.partial(self_backward_kernel, begin=begin),
        grid_spec=pltpu.PrefetchScalarGridSpec(
            num_scalar_prefetch=1,
            grid=(units,),
            in_specs=[
                pl.BlockSpec((1, 3 * HEAD_DIM, places), lambda u, n: (begin + u, 0, 0)),
                pl.BlockSpec((1, 1, places), lambda u, n: (begin - origin + u, 0, 0)),
            ]
            + [pl.BlockSpec((1, HEAD_DIM, quarter), lambda u, n: (begin - origin + u, 0, 0))]
            * quarters
            + [pl.BlockSpec((1, HEAD_DIM, quarter), lambda u, n: (begin + u, 0, 0))] * quarters,
            out_specs=[pl.BlockSpec((1, 3 * HEAD_DIM, quarter), lambda u, n: (u, 0, 0))] * quarters,
            scratch_shapes=[
                pltpu.VMEM((places, 128), bf16),
                pltpu.VMEM((places, 128), bf16),
                pltpu.VMEM((128, places), bf16),
                pltpu.VMEM((128, places), bf16),
                pltpu.VMEM((HEAD_DIM, places), f32),
            ],
        ),
        out_shape=[jax.ShapeDtypeStruct((units, 3 * HEAD_DIM, quarter), bf16)] * quarters,
        cost_estimate=lasting(30 * units),
        compiler_params=pltpu.CompilerParams(vmem_limit_bytes=VMEM_LIMIT),
        name="self_backward",
    )(meta, projected, totals, *attended, *back)


def cross_forward_kernel(meta_ref, query_ref, pair_ref, out_ref, total_ref):
    places = query_ref.shape[1]
    keys = pair_ref[0, 0, 0:HEAD_DIM, :].astype(f32).T.astype(bf16)
    values = jnp.concatenate(
        [pair_ref[0, 0, HEAD_DIM:, :], jnp.ones((16, pair_ref.shape[3]), bf16)], axis=0
    )
    for start in range(0, places, CROSS):
        scores = dot_nn(keys, query_ref[:, start : start + CROSS])
        largest = jnp.max(scores, axis=0, keepdims=True)
        chances = jnp.exp2(scores - largest).astype(bf16)
        total = dot_nn(values, chances)
        row_total = total[HEAD_DIM : HEAD_DIM + 1]
        out_ref[:, start : start + CROSS] = (total[:HEAD_DIM] / row_total).astype(bf16)
        total_ref[0, :, start : start + CROSS] = largest + jnp.log2(row_total)


def pair_spec(pairs):
    units = pairs.shape[1]

    def place(h, meta):
        return h // units, h % units, 0, 0

    return pl.BlockSpec((1, 1) + pairs.shape[2:], place)


def cross_forward(meta, queries, pairs):
    width, places = queries.shape
    rows = pl.BlockSpec((HEAD_DIM, places), lambda h, n: (h, 0))
    return pl.pallas_call(
        cross_forward_kernel,
        grid_spec=pltpu.PrefetchScalarGridSpec(
            num_scalar_prefetch=1,
            grid=(width // HEAD_DIM,),
            in_specs=[rows, pair_spec(pairs)],
            out_specs=[rows, pl.BlockSpec((1, 1, places), lambda h, n: (h, 0, 0))],
        ),
        out_shape=[
            jax.ShapeDtypeStruct((width, places), bf16),
            jax.ShapeDtypeStruct((width // HEAD_DIM, 1, places), f32),
        ],
        cost_estimate=lasting(25),
        compiler_params=pltpu.CompilerParams(vmem_limit_bytes=VMEM_LIMIT),
        name="cross_forward",
    )(meta, queries, pairs)


def cross_backward_kernel(
    meta_ref, query_ref, pair_ref, out_ref, back_ref, total_ref, grad_ref, pair_grad_ref
):
    places = query_ref.shape[1]
    rows = pair_ref.shape[3]
    at = row_index(64, rows)
    ones = jnp.where(at < 3, 1.0, 0.0)
    key_major = pair_ref[0, 0, 0:HEAD_DIM, :]
    keys = jnp.concatenate([key_major.astype(f32), ones], axis=0).T.astype(bf16)
    values = jnp.concatenate([pair_ref[0, 0, HEAD_DIM:, :].astype(f32), ones], axis=0).T.astype(bf16)
    blank = jnp.zeros((48, KEYS), bf16)
    back_key = jnp.zeros((HEAD_DIM, rows), f32)
    back_value = jnp.zeros((HEAD_DIM, rows), f32)
    for start in range(0, places, KEYS):
        span = slice(start, start + KEYS)
        plain, back = query_ref[:, span], back_ref[:, span]
        query = jnp.concatenate([plain, three_parts(-total_ref[0, :, span], False), blank], axis=0)
        delta = jnp.sum(back.astype(f32) * out_ref[:, span].astype(f32), axis=0, keepdims=True)
        back_rows = jnp.concatenate([back, three_parts(-delta, False), blank], axis=0)
        chances = jnp.exp2(dot_nn(keys, query))
        back_scores = (chances * dot_nn(values, back_rows)).astype(bf16)
        back_value = back_value + dot_nt(back, chances.astype(bf16))
        back_key = back_key + dot_nt(plain, back_scores)
        grad_ref[:, span] = (dot_nn(key_major, back_scores) * SCALING).astype(bf16)
    pair_grad_ref[0, 0, 0:HEAD_DIM, :] = (back_key * (1.0 / LOG2E)).astype(bf16)
    pair_grad_ref[0, 0, HEAD_DIM:, :] = back_value.astype(bf16)


def cross_backward(meta, queries, pairs, attended, back, totals):
    width, places = queries.shape
    rows = pl.BlockSpec((HEAD_DIM, places), lambda h, n: (h, 0))
    return pl.pallas_call(
        cross_backward_kernel,
        grid_spec=pltpu.PrefetchScalarGridSpec(
            num_scalar_prefetch=1,
            grid=(width // HEAD_DIM,),
            in_specs=[
                rows,
                pair_spec(pairs),
                rows,
                rows,
                pl.BlockSpec((1, 1, places), lambda h, n: (h, 0, 0)),
            ],
            out_specs=[rows, pair_spec(pairs)],
        ),
        out_shape=[
            jax.ShapeDtypeStruct((width, places), bf16),
            jax.ShapeDtypeStruct(pairs.shape, bf16),
        ],
        cost_estimate=lasting(36),
        compiler_params=pltpu.CompilerParams(vmem_limit_bytes=VMEM_LIMIT),
        name="cross_backward",
    )(meta, queries, pairs, attended, back, totals)


def normed(summed):
    centred = summed - jnp.mean(summed, axis=-1, keepdims=True)
    variance = jnp.mean(centred * centred, axis=-1, keepdims=True)
    inverse = lax.rsqrt(variance + EPSILON)
    return centred * inverse, inverse


def normed_back(normal, inverse, scaled):
    shared = jnp.mean(scaled, axis=-1, keepdims=True)
    along = jnp.mean(scaled * normal, axis=-1, keepdims=True)
    return (scaled - shared - normal * along) * inverse


def valid_column(meta_ref, quarter, rows):
    start = meta_ref[CONTEXT] * quarter + pl.program_id(0) * rows
    place = lax.broadcasted_iota(jnp.int32, (rows, 1), 0) + start
    return jnp.where(place < meta_ref[LENGTH], 1.0, 0.0)


def add_rows(sum_ref, *terms):
    @pl.when(pl.program_id(0) == 0)
    def _():
        sum_ref[...] = jnp.zeros_like(sum_ref)

    for at, term in enumerate(terms):
        sum_ref[at : at + 1, :] += jnp.sum(term, axis=0, keepdims=True)


def project_kernel(meta_ref, weight_ref, *refs, parts, rows):
    piece_refs, (x_ref, out_ref) = refs[:-2], refs[-2:]
    at_row = lax.broadcasted_iota(jnp.int32, (weight_ref.shape[0], 1), 0)
    scale = jnp.where(lax.rem(at_row, 3 * HEAD_DIM) < HEAD_DIM, QUERY_SCALE, 1.0)
    quarter = x_ref.shape[0] // (len(piece_refs) // parts)
    for at, piece_ref in enumerate(piece_refs):
        step, part = divmod(at, parts)
        result = (dot_nt(weight_ref[...], piece_ref[...]) * scale).astype(bf16)
        for block in range(quarter // (rows * parts)):
            place = (block * parts + part) * rows
            start = pl.multiple_of((meta_ref[CONTEXT] ^ step) * quarter + place, rows)
            run = slice(block * rows, (block + 1) * rows)
            x_ref[pl.ds(start, rows), :] = piece_ref[run, :]
            out_ref[:, pl.ds(start, rows)] = result[:, run]


def project(meta, weight, pieces, parts, rows):
    places, width = pieces[0].shape[0] * len(pieces), pieces[0].shape[1]
    whole = pl.BlockSpec(memory_space=pltpu.VMEM)
    return pl.pallas_call(
        functools.partial(project_kernel, parts=parts, rows=rows),
        in_specs=[pl.BlockSpec(memory_space=pltpu.SMEM)] + [whole] * (1 + len(pieces)),
        out_specs=[whole, whole],
        out_shape=[
            jax.ShapeDtypeStruct((places, width), bf16),
            jax.ShapeDtypeStruct((weight.shape[0], places), bf16),
        ],
        cost_estimate=lasting(10),
        compiler_params=pltpu.CompilerParams(vmem_limit_bytes=VMEM_LIMIT),
        name="project",
    )(meta, weight, *pieces)


def first_kernel(
    meta_ref, x_ref, norm_ref, out_w_ref, query_w_ref, *refs, quarter
):
    att_refs, (sum_ref, low_ref, query_ref, total_ref) = refs[:-4], refs[-4:]
    groups = query_w_ref.shape[0]
    branch = None
    for at in range(groups):
        att = jnp.concatenate([ref[...] for ref in att_refs[at::groups]], axis=0)
        term = dot_tt(att, out_w_ref[meta_ref[CONTEXT] ^ at])
        branch = term if branch is None else branch + term
    x = x_ref[...].astype(f32)
    summed = x + branch
    normal, _ = normed(summed)
    first = normal * norm_ref[0:1, :] + norm_ref[3:4, :]
    first_low = first.astype(bf16)
    sum_ref[...] = summed
    low_ref[...] = first_low
    query = jnp.concatenate([dot_nn(first_low, query_w_ref[at]) for at in range(groups)], axis=1)
    query_ref[...] = (query * QUERY_SCALE).T.astype(bf16)
    valid = valid_column(meta_ref, quarter, x.shape[0])
    add_rows(total_ref, valid * x * x, valid * branch * branch, valid * first * first)


def whole_spec(array):
    zeros = (0,) * array.ndim
    return pl.BlockSpec(array.shape, lambda b, n: zeros, pipeline_mode=pl.Buffered(1))


def first_step(meta, x_all, norms, out_w, query_w, att, rows):
    width = x_all.shape[1]
    quarter = att[0].shape[1]
    blocks = quarter // rows
    tokens = pl.BlockSpec((rows, width), lambda b, n: (b, 0))
    turned = pl.BlockSpec((width, rows), lambda b, n: (0, b))
    return pl.pallas_call(
        functools.partial(first_kernel, quarter=quarter),
        grid_spec=pltpu.PrefetchScalarGridSpec(
            num_scalar_prefetch=1,
            grid=(blocks,),
            in_specs=[
                pl.BlockSpec((rows, width), lambda b, n: (n[CONTEXT] * blocks + b, 0)),
                whole_spec(norms),
                whole_spec(out_w),
                whole_spec(query_w),
            ]
            + [pl.BlockSpec((piece.shape[0], rows), lambda b, n: (0, b)) for piece in att],
            out_specs=[tokens, tokens, turned, pl.BlockSpec((8, width), lambda b, n: (0, 0))],
        ),
        out_shape=[
            jax.ShapeDtypeStruct((quarter, width), f32),
            jax.ShapeDtypeStruct((quarter, width), bf16),
            jax.ShapeDtypeStruct((width, quarter), bf16),
            jax.ShapeDtypeStruct((8, width), f32),
        ],
        cost_estimate=lasting(8),
        compiler_params=pltpu.CompilerParams(vmem_limit_bytes=VMEM_LIMIT),
        name="first_step",
    )(meta, x_all, norms, out_w, query_w, *att)


def gelu_and_slope(inner):
    chance = 0.5 * (1.0 + lax.erf(inner * 0.7071067811865476))
    density = jnp.exp2(inner * inner * (-0.5 * LOG2E)) * 0.3989422804014327
    return inner * chance, chance + inner * density


def feed_kernel(
    meta_ref, att_ref, sum_ref, norm_ref, out_w_ref, feed_ref, *refs, quarter
):
    groups, width = feed_ref.shape[0], sum_ref.shape[1]
    cot_ref, output_ref, *refs = refs
    low_ref, active_ref, inner_ref, back_three_ref, back_two_ref, back_sum_ref, back_att_ref = refs[:7]
    total_ref, slope_ref = refs[7:]
    rows = sum_ref.shape[0]
    part = out_w_ref.shape[2]
    gain = [norm_ref[at : at + 1, :] for at in range(3)]
    bias = [norm_ref[3 + at : 4 + at, :] for at in range(3)]
    branch_two = None
    for at in range(groups):
        term = dot_tt(att_ref[at * part : (at + 1) * part, :], out_w_ref[at])
        branch_two = term if branch_two is None else branch_two + term
    normal, _ = normed(sum_ref[...])
    normal_two, inverse_two = normed(normal * gain[0] + bias[0] + branch_two)
    second = normal_two * gain[1] + bias[1]
    second_low = second.astype(bf16)
    low_ref[...] = second_low
    branch_three = None
    for at in range(groups):
        inner = dot_nn(second_low, feed_ref[at, :, :width])
        active, slope = gelu_and_slope(inner)
        active = active.astype(bf16)
        active_ref[:, at * width : (at + 1) * width] = active
        slope_ref[:, at * width : (at + 1) * width] = slope
        term = dot_nt(active, feed_ref[at, :, width:])
        branch_three = term if branch_three is None else branch_three + term
    normal_three, inverse_three = normed(second + branch_three)
    output_ref[...] = (normal_three * gain[2] + bias[2]).astype(bf16)
    valid = valid_column(meta_ref, quarter, rows)
    back_output = cot_ref[...].astype(f32) * valid
    back_third = normed_back(normal_three, inverse_three, back_output * gain[2])
    back_three = back_third.astype(bf16)
    back_three_ref[...] = back_three
    back_second = back_third
    for at in range(groups):
        back_active = dot_nn(back_three, feed_ref[at, :, width:])
        back_inner = (back_active * slope_ref[:, at * width : (at + 1) * width]).astype(bf16)
        inner_ref[:, at * width : (at + 1) * width] = back_inner
        back_second = back_second + dot_nt(back_inner, feed_ref[at, :, :width])
    back_second_sum = normed_back(normal_two, inverse_two, back_second * gain[1])
    back_sum_ref[...] = back_second_sum
    back_two = back_second_sum.astype(bf16)
    back_two_ref[...] = back_two
    back_att = jnp.concatenate([dot_nn(back_two, out_w_ref[at]) for at in range(groups)], axis=1)
    back_att_ref[...] = back_att.T.astype(bf16)
    add_rows(
        total_ref,
        valid * branch_two * branch_two,
        valid * second * second,
        valid * branch_three * branch_three,
        back_second * normal_two,
        back_output * normal_three,
        back_second,
        back_output,
    )


def feed_step(meta, att, first_sum, norms, out_w, feed, cotangent, rows):
    quarter, width = first_sum.shape
    groups = feed.shape[0]
    hidden_width = groups * width
    tokens = pl.BlockSpec((rows, width), lambda b, n: (b, 0))
    wide = pl.BlockSpec((rows, hidden_width), lambda b, n: (b, 0))
    turned = pl.BlockSpec((width, rows), lambda b, n: (0, b))
    return pl.pallas_call(
        functools.partial(feed_kernel, quarter=quarter),
        grid_spec=pltpu.PrefetchScalarGridSpec(
            num_scalar_prefetch=1,
            grid=(quarter // rows,),
            in_specs=[
                turned,
                tokens,
                whole_spec(norms),
                whole_spec(out_w),
                pl.BlockSpec(
                    (groups, width, 2 * width), lambda b, n: (0, 0, 0), pipeline_mode=pl.Buffered(1)
                ),
                tokens,
            ],
            out_specs=[tokens, tokens, wide, wide, tokens, tokens, tokens, turned]
            + [pl.BlockSpec((8, width), lambda b, n: (0, 0))],
            scratch_shapes=[pltpu.VMEM((rows, hidden_width), f32)],
        ),
        out_shape=[
            jax.ShapeDtypeStruct((quarter, width), bf16),
            jax.ShapeDtypeStruct((quarter, width), bf16),
            jax.ShapeDtypeStruct((quarter, hidden_width), bf16),
            jax.ShapeDtypeStruct((quarter, hidden_width), bf16),
            jax.ShapeDtypeStruct((quarter, width), bf16),
            jax.ShapeDtypeStruct((quarter, width), bf16),
            jax.ShapeDtypeStruct((quarter, width), f32),
            jax.ShapeDtypeStruct((width, quarter), bf16),
            jax.ShapeDtypeStruct((8, width), f32),
        ],
        cost_estimate=lasting(45),
        compiler_params=pltpu.CompilerParams(vmem_limit_bytes=VMEM_LIMIT),
        name="feed_step",
    )(meta, att, first_sum, norms, out_w, feed, cotangent)


def last_kernel(meta_ref, query_ref, back_sum_ref, sum_ref, norm_ref, query_w_ref, out_w_ref, *refs):
    back_refs, (back_ref, low_ref, total_ref) = refs[:-3], refs[-3:]
    groups, _, part = query_w_ref.shape
    back_first = back_sum_ref[...]
    for at in range(groups):
        back_first = back_first + dot_tt(query_ref[at * part : (at + 1) * part, :], query_w_ref[at])
    normal, inverse = normed(sum_ref[...])
    back_first_sum = normed_back(normal, inverse, back_first * norm_ref[0:1, :])
    back_ref[...] = back_first_sum
    back_one = back_first_sum.astype(bf16)
    low_ref[...] = back_one
    for at, ref in enumerate(back_refs):
        ref[...] = dot_nn(back_one, out_w_ref[meta_ref[CONTEXT] ^ at]).T.astype(bf16)
    add_rows(total_ref, back_first * normal, back_first)


def last_step(meta, back_query, back_second_sum, first_sum, norms, query_w, out_w, rows):
    quarter, width = first_sum.shape
    groups, _, part = query_w.shape
    tokens = pl.BlockSpec((rows, width), lambda b, n: (b, 0))
    turned = pl.BlockSpec((width, rows), lambda b, n: (0, b))
    return pl.pallas_call(
        last_kernel,
        grid_spec=pltpu.PrefetchScalarGridSpec(
            num_scalar_prefetch=1,
            grid=(quarter // rows,),
            in_specs=[
                turned,
                tokens,
                tokens,
                whole_spec(norms),
                whole_spec(query_w),
                whole_spec(out_w),
            ],
            out_specs=[pl.BlockSpec((part, rows), lambda b, n: (0, b))] * groups
            + [tokens, tokens, pl.BlockSpec((8, width), lambda b, n: (0, 0))],
        ),
        out_shape=[jax.ShapeDtypeStruct((part, quarter), bf16)] * groups
        + [
            jax.ShapeDtypeStruct((quarter, width), f32),
            jax.ShapeDtypeStruct((quarter, width), bf16),
            jax.ShapeDtypeStruct((8, width), f32),
        ],
        cost_estimate=lasting(8),
        compiler_params=pltpu.CompilerParams(vmem_limit_bytes=VMEM_LIMIT),
        name="last_step",
    )(meta, back_query, back_second_sum, first_sum, norms, query_w, out_w)


def hidden_kernel(meta_ref, back_ref, weight_ref, *refs):
    groups = weight_ref.shape[0]
    whole_ref, part_refs, out_ref = refs[0], refs[1:-1], refs[-1]
    total = back_ref[...]
    for at in range(groups):
        group = meta_ref[CONTEXT] ^ at
        part = [whole_ref[group]] + [ref[...] for ref in part_refs[at::groups]]
        part = jnp.concatenate(part, axis=0)
        total = total + dot_tt(part, weight_ref[group])
    out_ref[...] = total.astype(bf16)


def hidden_step(meta, back_first_sum, weights, parts, rows):
    quarter, width = back_first_sum.shape

    def columns(part):
        lead = part.shape[:-1]
        zeros = (0,) * len(lead)
        return pl.BlockSpec(lead + (rows,), lambda b, n: zeros + (b,))

    return pl.pallas_call(
        hidden_kernel,
        grid_spec=pltpu.PrefetchScalarGridSpec(
            num_scalar_prefetch=1,
            grid=(quarter // rows,),
            in_specs=[
                pl.BlockSpec((rows, width), lambda b, n: (b, 0)),
                whole_spec(weights),
            ]
            + [columns(part) for part in parts],
            out_specs=pl.BlockSpec((rows, width), lambda b, n: (b, 0)),
        ),
        out_shape=jax.ShapeDtypeStruct((quarter, width), bf16),
        cost_estimate=lasting(8),
        compiler_params=pltpu.CompilerParams(vmem_limit_bytes=VMEM_LIMIT),
        name="hidden_step",
    )(meta, back_first_sum, weights, *parts)


def turned_once(pairs):
    @pl.when(pl.program_id(0) == 0)
    def _():
        for source, target in pairs:
            target[...] = source[...].astype(f32).T.astype(bf16)


def put_halves(meta_ref, keep_ref, send_ref, low, high, result):
    shards, rows = keep_ref.shape[1:3]
    core = lax.rem(meta_ref[CONTEXT], 2)
    result = result.astype(bf16)
    for half, (even_ref, odd_ref) in enumerate(((keep_ref, send_ref), (send_ref, keep_ref))):

        @pl.when(core == half)
        def _():
            for shard in range(shards):
                start = 2 * shard * rows
                even_ref[0, shard, :, low:high] = result[start : start + rows]
                odd_ref[0, shard, :, low:high] = result[start + rows : start + 2 * rows]


def feed_grad_kernel(
    meta_ref, low_ref, inner_ref, back_ref, active_ref, two_ref, cross_ref, keep_ref, send_ref, *turned
):
    width = low_ref.shape[1]
    put = functools.partial(put_halves, meta_ref, keep_ref, send_ref)
    turned_once(zip((low_ref, back_ref, two_ref), turned))
    put(0, width, dot_nn(turned[0][...], inner_ref[...]))
    put(width, 2 * width, dot_nn(turned[1][...], active_ref[...]))
    put(2 * width, keep_ref.shape[3], dot_nt(turned[2][...], cross_ref[...]))


def feed_grad(meta, second_low, back_inner, back_three, active, back_two, cross_att, shards):
    tokens, width = second_low.shape
    groups = active.shape[1] // width
    part = width // groups
    left = pl.BlockSpec((tokens, width), lambda b, n: (0, 0))
    right = pl.BlockSpec((tokens, width), lambda b, n: (0, b))
    half = (shards, width // (2 * shards), 2 * width + part)
    return pl.pallas_call(
        feed_grad_kernel,
        grid_spec=pltpu.PrefetchScalarGridSpec(
            num_scalar_prefetch=1,
            grid=(groups,),
            in_specs=[
                left,
                right,
                left,
                right,
                left,
                pl.BlockSpec((part, tokens), lambda b, n: (b, 0)),
            ],
            out_specs=[pl.BlockSpec((1,) + half, lambda b, n: (b, 0, 0, 0))] * 2,
            scratch_shapes=[pltpu.VMEM((width, tokens), bf16)] * 3,
        ),
        out_shape=[jax.ShapeDtypeStruct((groups,) + half, bf16)] * 2,
        cost_estimate=lasting(18),
        compiler_params=pltpu.CompilerParams(vmem_limit_bytes=VMEM_LIMIT),
        name="feed_grad",
    )(meta, second_low, back_inner, back_three, active, back_two, cross_att)


def mixed_grad_kernel(
    meta_ref, one_ref, low_ref, selected_ref, query_ref, pair_ref, *refs
):
    keep_ref, send_ref, *turned = refs[-5:]
    att_refs = refs[:-5]
    turned_once(zip((one_ref, low_ref, selected_ref), turned))
    slot = pl.program_id(0) ^ meta_ref[CONTEXT]
    att = None
    for at in range(4):
        piece = jnp.concatenate([ref[...] for ref in att_refs[at::4]], axis=0)
        att = piece if att is None else jnp.where(slot == at, piece, att)
    result = jnp.concatenate(
        [
            dot_nt(turned[0][...], att),
            dot_nt(turned[1][...], query_ref[...]),
            dot_nt(turned[2][...], pair_ref[0]),
        ],
        axis=1,
    )
    put_halves(meta_ref, keep_ref, send_ref, 0, result.shape[1], result)


def mixed_grad(meta, back_one, first_low, selected, back_query, back_pairs, att, shards):
    tokens, width = back_one.shape
    groups = 4
    part = width // groups
    pair_width, retrieved = back_pairs.shape[1:]
    half = (shards, width // (2 * shards), 2 * part + pair_width)
    return pl.pallas_call(
        mixed_grad_kernel,
        grid_spec=pltpu.PrefetchScalarGridSpec(
            num_scalar_prefetch=1,
            grid=(groups,),
            in_specs=[
                whole_spec(back_one),
                whole_spec(first_low),
                whole_spec(selected),
                pl.BlockSpec((part, tokens), lambda b, n: (b, 0)),
                pl.BlockSpec((1, pair_width, retrieved), lambda b, n: (b, 0, 0)),
            ]
            + [whole_spec(piece) for piece in att],
            out_specs=[pl.BlockSpec((1,) + half, lambda b, n: (b, 0, 0, 0))] * 2,
            scratch_shapes=[
                pltpu.VMEM((width, tokens), bf16),
                pltpu.VMEM((width, tokens), bf16),
                pltpu.VMEM((width, retrieved), bf16),
            ],
        ),
        out_shape=[jax.ShapeDtypeStruct((groups,) + half, bf16)] * 2,
        cost_estimate=lasting(14),
        compiler_params=pltpu.CompilerParams(vmem_limit_bytes=VMEM_LIMIT),
        name="mixed_grad",
    )(meta, back_one, first_low, selected, back_query, back_pairs, *att)


def own_grad_kernel(meta_ref, x_ref, *refs):
    part_refs, out_ref = refs[:-1], refs[-1]
    quarter = part_refs[0].shape[1]
    total = None
    for at, part_ref in enumerate(part_refs):
        start = pl.multiple_of((meta_ref[CONTEXT] ^ at) * quarter, quarter)
        term = dot_nn(part_ref[...], x_ref[pl.ds(start, quarter), :])
        total = term if total is None else total + term
    out_ref[...] = total.T.astype(bf16)


def own_grad(meta, x_all, parts):
    whole = pl.BlockSpec(memory_space=pltpu.VMEM)
    return pl.pallas_call(
        own_grad_kernel,
        in_specs=[pl.BlockSpec(memory_space=pltpu.SMEM)] + [whole] * (1 + len(parts)),
        out_specs=whole,
        out_shape=jax.ShapeDtypeStruct((x_all.shape[1], parts[0].shape[0]), bf16),
        cost_estimate=lasting(7),
        compiler_params=pltpu.CompilerParams(vmem_limit_bytes=VMEM_LIMIT),
        name="own_grad",
    )(meta, x_all, *parts)


def product(spec, left, right):
    return jnp.einsum(spec, left, right, preferred_element_type=f32)


def turn(array, axis, step):
    count = lax.axis_size(axis)
    return lax.ppermute(array, axis, [(at, at ^ step) for at in range(count)])


def to_others(parts, axis):
    return [parts[0]] + [turn(parts[at], axis, at) for at in range(1, len(parts))]


def gather_context(array):
    far = turn(array, "ctx", 2)
    return [array, turn(array, "ctx", 1), far, turn(far, "ctx", 1)]


def gather(array, axis, dim):
    step = 1
    while step < lax.axis_size(axis):
        other = turn(array, axis, step)
        later = (lax.axis_index(axis) & step) > 0
        array = jnp.concatenate(
            [jnp.where(later, other, array), jnp.where(later, array, other)], axis=dim
        )
        step *= 2
    return array


def in_slots(pieces, index):
    for step in (1, 2):
        later = (index & step) > 0
        pieces = [jnp.where(later, pieces[at ^ step], pieces[at]) for at in range(len(pieces))]
    return pieces


def gather_direct(array, axis, dim):
    pieces = [array] + [turn(array, axis, at) for at in range(1, 4)]
    return jnp.concatenate(in_slots(pieces, lax.axis_index(axis)), axis=dim)


def exchange(parts, axes):
    return lax.all_to_all(parts, axes, split_axis=0, concat_axis=0, tiled=True)


def add_up(pieces):
    total = pieces[0].astype(f32)
    for piece in pieces[1:]:
        total = total + piece.astype(f32)
    return total


def sum_everywhere(vector):
    steps = []
    for axis in ("ctx", "tp", "shard"):
        step = 1
        while step < lax.axis_size(axis):
            vector = vector + turn(vector, axis, step)
            steps.append(vector)
            step *= 2
    return steps


class StagedSum:
    def __init__(self, keep, send):
        self.terms, self.send = [keep], send

    def beside(self, kernel):
        self.terms[1:] = [after(term, kernel) for term in self.terms[1:]]

    def over_core(self):
        self.terms.append(turn(self.send, "ctx", 1))

    def over_shard(self):
        count, index = lax.axis_size("shard"), lax.axis_index("shard")

        def part(at):
            return add_up([lax.dynamic_index_in_dim(t, at, 1, keepdims=False) for t in self.terms])

        if count == 2:
            self.send = part(1 - index).astype(bf16)
            own = [lax.dynamic_index_in_dim(t, index, 1, keepdims=False) for t in self.terms]
            self.terms = own + [turn(self.send, "shard", 1)]
        else:
            self.send = jnp.moveaxis(add_up(self.terms).astype(bf16), 1, 0)
            self.terms = [jnp.sum(exchange(self.send, "shard").astype(f32), axis=0).astype(bf16)]

    def over_x(self):
        rows = self.terms[0].shape[1] // 2
        index = lax.axis_index("ctx") // 2

        def part(at):
            return [lax.dynamic_slice_in_dim(t, at * rows, rows, 1) for t in self.terms]

        self.send = add_up(part(1 - index)).astype(bf16)
        self.terms = part(index) + [turn(self.send, "ctx", 2)]

    def send_of_quarter(self):
        self.terms = [add_up(self.terms).astype(bf16)]
        return self.terms[0]

    def over_tensor_at_once(self):
        self.send = add_up(self.terms).astype(bf16)
        self.terms = [exchange(self.send, "tp")]

    def over_tensor(self):
        self.send = add_up(self.terms).astype(bf16)
        index = lax.axis_index("tp")
        parts = [
            lax.dynamic_index_in_dim(self.send, index ^ at, 0, keepdims=False)
            for at in range(self.send.shape[0])
        ]
        self.terms = to_others(parts, "tp")

    def total(self):
        self.send = add_up(self.terms).astype(bf16)
        return self.send

    def spread(self):
        total = self.send
        for step in (2, 1):
            other = turn(total, "ctx", step)
            later = (lax.axis_index("ctx") & step) > 0
            total = jnp.concatenate(
                [jnp.where(later, other, total), jnp.where(later, total, other)], axis=0
            )
        return total.astype(f32)


def after(value, *earlier):
    return lax.optimization_barrier((value,) + earlier)[0]


def per_device(
    hidden,
    bank,
    indices,
    lengths,
    cotangent,
    query_self,
    key_self,
    value_self,
    out_self,
    query_cross,
    key_cross,
    value_cross,
    out_cross,
    up_weight,
    down_weight,
    norm_gain,
    norm_bias,
):
    context_count = lax.axis_size("ctx")
    tensor_count = lax.axis_size("tp")
    shard_index = lax.axis_index("shard")
    context_index = lax.axis_index("ctx")
    tensor_index = lax.axis_index("tp")
    group_sequences, device_places, model_width = hidden.shape
    units = HEADS // context_count
    group_width = units * HEAD_DIM
    quarter = device_places * tensor_count
    shard_rows = query_self.shape[0]
    piece_rows = shard_rows // context_count
    feed_width = up_weight.shape[1]

    swap = [
        (c * tensor_count + z, z * context_count + c)
        for c in range(context_count)
        for z in range(tensor_count)
    ]

    group_lengths = lax.dynamic_slice_in_dim(
        lengths, shard_index * group_sequences, group_sequences
    )
    length = group_lengths[tensor_index]
    meta = jnp.stack([context_index, tensor_index, length] + [length] * units).astype(jnp.int32)

    def by_unit(weights):
        stacked = jnp.stack([w.reshape(-1, units, HEAD_DIM) for w in weights], axis=2)
        return stacked.reshape(weights[0].shape[0], -1)

    local_self = by_unit([query_self, key_self, value_self])
    local_pair = by_unit([key_cross, value_cross])
    self_width, pair_width = local_self.shape[1], local_pair.shape[1]

    def gather_all(columns):
        rows = lax.dynamic_slice_in_dim(columns, context_index * piece_rows, piece_rows, 0)
        everything = lax.all_gather(rows, ("tp", "shard", "ctx"), axis=0, tiled=True)
        return everything.reshape(tensor_count, model_width, columns.shape[1])

    bank_local = bank.shape[1]
    retrieved = indices.shape[1]
    owner_tensor = indices[0] // bank_local
    local_rows = indices[0] - owner_tensor * bank_local
    owned = (owner_tensor == tensor_index)[:, None]
    picked = jnp.where(owned, jnp.take(bank[0], local_rows, axis=0), jnp.zeros((), bf16))

    x_low = exchange(hidden, "tp").reshape(quarter, model_width)
    own_self = gather(lax.ppermute(local_self.T, ("ctx", "tp"), swap), "shard", 1)
    far = after(turn(x_low, "ctx", 2), own_self, picked, meta)
    x_parts = [x_low, turn(x_low, "ctx", 1), far, turn(far, "ctx", 1)]
    picked = exchange(after(picked, x_low).reshape(tensor_count, -1, model_width), "tp")
    x_all, projected = project(meta, own_self, x_parts, 1, device_places)
    projected = projected.reshape(units, 3 * HEAD_DIM, -1)

    norms = jnp.concatenate([norm_gain, norm_bias], axis=0).T
    bundle = [up_weight, down_weight.T, out_self.T, query_cross, out_cross.T, local_pair, norms]
    feed = gather_all(after(jnp.concatenate(bundle, axis=1), x_low))
    bundle = feed[:, :, 2 * feed_width :]
    out_self_t = bundle[:, :, :group_width]
    query_cross_w = bundle[:, :, group_width : 2 * group_width]
    out_cross_t = bundle[:, :, 2 * group_width : 3 * group_width]
    pair_w = bundle[:, :, 3 * group_width : 3 * group_width + pair_width]
    norm_rows = bundle[0, :, 3 * group_width + pair_width :].T.astype(f32)
    norm_rows = jnp.pad(norm_rows, ((0, 2), (0, 0)))

    self_out, self_totals, self_att = [], [], []

    def forward(begin, *ready):
        *out, total = self_forward(meta, after(projected, *ready), context_count, begin, 1)
        self_out.append(out)
        self_totals.append(total)
        self_att.extend(piece.reshape(-1, quarter) for piece in to_others(out, "ctx"))
        return total

    done = forward(1, forward(0))
    picked = jnp.sum(after(picked, done).astype(f32), axis=0).astype(bf16)
    done = forward(2, picked, done, *self_att[:context_count])
    self_att[context_count : 2 * context_count] = [
        after(piece, done) for piece in self_att[context_count : 2 * context_count]
    ]
    picked = after(lax.ppermute(picked, ("ctx", "tp"), swap), done)
    lists = [picked] + [turn(picked, "ctx", at) for at in range(1, context_count)]
    cot = exchange(after(cotangent, *self_att[-context_count:]), "tp")
    first_sum, first_low, cross_query, first_totals = first_step(
        meta, after(x_all, picked), norm_rows, out_self_t, query_cross_w, self_att, device_places
    )
    lists = [after(piece, first_low) for piece in lists]
    selected = jnp.concatenate(in_slots(lists, context_index))
    pairs = product("tdf,kd->tfk", pair_w, selected).astype(bf16)
    pairs = pairs.reshape(context_count, units, 2 * HEAD_DIM, retrieved)
    cross_att, cross_total = cross_forward(meta, cross_query, pairs)
    cot = after(cot, cross_att).reshape(quarter, model_width)
    fed = feed_step(meta, cross_att, first_sum, norm_rows, out_cross_t, feed, cot, device_places)
    output, second_low, active, back_inner, back_three, back_two, back_second_sum, back_cross, totals = fed
    shard_count = lax.axis_size("shard")
    feed_sum = StagedSum(
        *feed_grad(
            meta, second_low, back_inner, back_three, active, back_two, cross_att, shard_count
        )
    )
    feed_sum.over_core()
    output = exchange(output.reshape(tensor_count, device_places, model_width), "tp")
    back_query, back_pairs = cross_backward(
        meta, cross_query, pairs, cross_att, after(back_cross, feed_sum.send), cross_total
    )
    back_pairs = back_pairs.reshape(context_count, pair_width, retrieved)
    feed_sum.over_shard()
    back_selected = product("tfk,tdf->kd", back_pairs, pair_w).astype(bf16)
    back_selected = back_selected.reshape(context_count, -1, model_width)
    *back_self, back_first_sum, back_one, last_totals = last_step(
        meta,
        back_query,
        after(back_second_sum, output, feed_sum.send, back_selected),
        first_sum,
        norm_rows,
        query_cross_w,
        out_self_t,
        device_places,
    )
    back_selected = after(exchange(back_selected, "ctx"), back_one)
    back_self = [piece.reshape(units, HEAD_DIM, quarter) for piece in to_others(back_self, "ctx")]
    mixed_sum = StagedSum(
        *mixed_grad(
            meta, back_one, first_low, selected, back_query, back_pairs, self_att, shard_count
        )
    )
    self_w = gather_all(after(local_self, first_low))

    squares = jnp.sum(jnp.concatenate([first_totals[:3], totals[:3]], axis=0), axis=1)
    rows = jnp.stack(
        [
            last_totals[0],
            totals[3],
            totals[4],
            last_totals[1],
            totals[5],
            totals[6],
            jnp.pad(squares, (0, model_width - squares.shape[0])),
        ]
    )

    def backward(begin, *ready):
        return self_backward(
            meta,
            after(projected, *ready),
            self_totals[begin],
            self_out[begin],
            back_self,
            begin,
            begin,
        )

    def parts_of(grads):
        return [piece.reshape(-1, quarter) for piece in to_others(grads, "ctx")]

    back_selected = jnp.sum(back_selected.astype(f32), axis=0).astype(bf16)
    grads = [backward(0, mixed_sum.send, back_selected)]
    mixed_sum.over_core()
    back_rows = lax.ppermute(back_selected, ("ctx", "tp"), swap)
    for running in (feed_sum, mixed_sum):
        running.beside(grads[0][0])
    back_rows = after(back_rows, grads[0][0])
    feed_sum.over_x()
    mixed_sum.over_shard()

    back_parts = [exchange(jnp.concatenate(in_slots(grads[0], context_index)), "ctx")]
    grads.append(backward(1, back_rows, feed_sum.send, mixed_sum.send, *grads[0]))
    back_rows = [back_rows] + [turn(back_rows, "tp", at) for at in range(1, tensor_count)]
    back_rows = [after(piece, grads[1][0]) for piece in back_rows]
    back_parts = [after(back_parts[0], grads[1][0])]
    own_grads = []
    for running in (feed_sum, mixed_sum):
        running.beside(grads[1][0])
    feed_sum.over_tensor_at_once()
    mixed_sum.over_x()

    back_parts += parts_of(grads[1])
    ready = (feed_sum.send, mixed_sum.send, back_parts[0], *back_rows)
    grads.append(backward(2, *ready, *grads[1]))
    back_parts[2:] = [after(part, grads[2][0]) for part in back_parts[2:]]
    feed_sum.terms = [jnp.sum(after(feed_sum.terms[0], grads[2][0]).astype(f32), axis=0)]
    mixed_sum.beside(grads[2][0])
    back_parts += parts_of(grads[2])
    mixed_sum.over_tensor()
    own_grads = []
    ready = (feed_sum.total(), *back_parts[2:5])
    for at in range(units):
        own_grads.append(
            own_grad(meta, after(x_all, *ready), [p.reshape(-1, quarter) for p in grads[at]])
        )
    own_sum = jnp.concatenate(own_grads, axis=1)
    own_sum = own_sum.reshape(shard_count, -1, own_sum.shape[1])
    back_hidden = hidden_step(
        meta, after(back_first_sum, own_sum), self_w, back_parts, device_places
    )

    if shard_count == 2:
        mine = lax.dynamic_index_in_dim(own_sum, shard_index, 0, keepdims=False)
        other = lax.dynamic_index_in_dim(own_sum, 1 - shard_index, 0, keepdims=False)
        own_sum = add_up([mine, after(turn(other, "shard", 1), back_hidden)])
    else:
        own_sum = jnp.sum(exchange(own_sum, "shard").astype(f32), axis=0)
    mixed_sum.beside(back_hidden)
    mixed_sum.total()
    own_sum = own_sum.astype(bf16).reshape(tensor_count, -1, own_sum.shape[-1])
    own_sum = [
        lax.dynamic_index_in_dim(own_sum, tensor_index ^ at, 0, keepdims=False)
        for at in range(tensor_count)
    ]
    back_rows = [after(piece, back_hidden, mixed_sum.send, *own_sum) for piece in back_rows]
    back_rows = jnp.concatenate(in_slots(back_rows, tensor_index))
    back_hidden = exchange(back_hidden.reshape(tensor_count, device_places, model_width), "tp")
    back_rows = jnp.where(owned, back_rows.astype(f32), 0.0)
    back_bank = jnp.zeros(bank.shape[1:], f32).at[local_rows].add(back_rows)[None]
    own_sum = to_others(own_sum, "tp")
    own_sum = [own_sum[0]] + [after(piece, back_bank) for piece in own_sum[1:]]
    own_sum = add_up(own_sum).astype(bf16)
    own_sum = lax.ppermute(own_sum, ("ctx", "tp"), swap)
    rows_steps = sum_everywhere(after(rows, back_bank))

    own_all = gather_direct(own_sum, "ctx", 0)
    back_mixed = mixed_sum.spread()
    back_feed = feed_sum.spread()
    rows = rows_steps[-1]
    shard_columns = lax.dynamic_slice_in_dim(rows, shard_index * shard_rows, shard_rows, 1)
    back_gain, back_bias = shard_columns[:3], shard_columns[3:6]
    token_total = jnp.sum(lengths).astype(f32) * model_width
    statistics = jnp.sqrt(rows[6, : squares.shape[0]] / token_total)

    def apart(stacked, count):
        split = stacked.reshape(shard_rows, units, count, HEAD_DIM)
        return [split[:, :, at].reshape(shard_rows, group_width).astype(f32) for at in range(count)]

    back_query_self, back_key_self, back_value_self = apart(own_all, 3)
    back_key_cross, back_value_cross = apart(back_mixed[:, 2 * group_width :], 2)
    return (
        output,
        back_hidden.astype(f32),
        back_bank,
        back_query_self,
        back_key_self,
        back_value_self,
        back_mixed[:, :group_width].T,
        back_mixed[:, group_width : 2 * group_width],
        back_key_cross,
        back_value_cross,
        back_feed[:, 2 * feed_width :].T,
        back_feed[:, :feed_width],
        back_feed[:, feed_width : 2 * feed_width].T,
        back_gain,
        back_bias,
        statistics,
    )


def solution(mesh):
    return jax.shard_map(
        per_device,
        mesh=mesh,
        in_specs=(
            P("shard", ("ctx", "tp"), None),
            P(("shard", "ctx"), "tp", None),
            P(("shard", "ctx"), None),
            P(),
            P("shard", ("ctx", "tp"), None),
            P("shard", "tp"),
            P("shard", "tp"),
            P("shard", "tp"),
            P("tp", "shard"),
            P("shard", "tp"),
            P("shard", "tp"),
            P("shard", "tp"),
            P("tp", "shard"),
            P("shard", "tp"),
            P("tp", "shard"),
            P(None, "shard"),
            P(None, "shard"),
        ),
        out_specs=(
            P("shard", ("ctx", "tp"), None),
            P("shard", ("ctx", "tp"), None),
            P(("shard", "ctx"), "tp", None),
            P("shard", "tp"),
            P("shard", "tp"),
            P("shard", "tp"),
            P("tp", "shard"),
            P("shard", "tp"),
            P("shard", "tp"),
            P("shard", "tp"),
            P("tp", "shard"),
            P("shard", "tp"),
            P("tp", "shard"),
            P(None, "shard"),
            P(None, "shard"),
            P(),
        ),
        check_vma=False,
    )
```

```python
import functools

import jax
import jax.numpy as jnp
from jax import lax
from jax.experimental import pallas as pl
from jax.experimental.pallas import tpu as pltpu
from jax.sharding import PartitionSpec as P

HEADS = 12
HEAD_DIM = 64
BLK = 256

EPSILON = 1e-05
NEGATIVE = -1e30
LOG2E = 1.4426950408889634
SCALING = HEAD_DIM**-0.5
QUERY_SCALE = SCALING * LOG2E

KEYS = 512
QUERIES = 1024
CROSS = 1024
VMEM_LIMIT = 56 * 2**20

bf16 = jnp.bfloat16
f32 = jnp.float32

CONTEXT, TENSOR, LENGTH, UNIT_LENGTHS = 0, 1, 2, 3


def lasting(microseconds):
    return pl.CostEstimate(
        flops=int(microseconds * 1.1e9), bytes_accessed=0, transcendentals=0
    )


def dot_nn(left, right):
    return lax.dot_general(left, right, (((1,), (0,)), ((), ())), preferred_element_type=f32)


def dot_nt(left, right):
    return lax.dot_general(left, right, (((1,), (1,)), ((), ())), preferred_element_type=f32)


def dot_tn(left, right):
    return lax.dot_general(left, right, (((0,), (0,)), ((), ())), preferred_element_type=f32)


def dot_tt(left, right):
    return lax.dot_general(left, right, (((0,), (1,)), ((), ())), preferred_element_type=f32)


def row_index(rows, columns):
    return lax.broadcasted_iota(jnp.int32, (rows, columns), 0)


def place_index(rows, columns, start):
    return lax.broadcasted_iota(jnp.int32, (rows, columns), 1) + start


def three_parts(row, ones_row):
    high = row.astype(bf16).astype(f32)
    rest = row - high
    middle = rest.astype(bf16).astype(f32)
    lowest = rest - middle
    at = row_index(16, row.shape[1])
    last = jnp.where(at == 3, 1.0, 0.0) if ones_row else jnp.zeros_like(at, f32)
    rows = jnp.where(at == 0, high, jnp.where(at == 1, middle, jnp.where(at == 2, lowest, last)))
    return rows.astype(bf16)


def self_forward_kernel(meta_ref, x_ref, *refs, begin):
    out_refs, (total_ref, keys, values, even, odd) = refs[:-5], refs[-5:]
    length = meta_ref[UNIT_LENGTHS + begin + pl.program_id(0)]
    places = x_ref.shape[2]
    quarter_tiles = out_refs[0].shape[2] // QUERIES
    per_query = QUERIES // KEYS
    half = BLK
    key_tiles = (length + KEYS - 1) // KEYS

    def prepare(tile, _):
        start = pl.multiple_of(tile * KEYS, KEYS)
        rows = x_ref[0, HEAD_DIM : 2 * HEAD_DIM, pl.ds(start, KEYS)].astype(f32)
        at, place = row_index(16, KEYS), place_index(16, KEYS, start)
        mask = jnp.where((at == 0) & (place >= length), NEGATIVE, 0.0)
        stacked = jnp.concatenate([rows, mask, jnp.zeros((48, KEYS), f32)], axis=0)
        keys[pl.ds(start, KEYS), :] = stacked.T.astype(bf16)
        values[0:HEAD_DIM, pl.ds(start, KEYS)] = x_ref[
            0, 2 * HEAD_DIM : 3 * HEAD_DIM, pl.ds(start, KEYS)
        ]
        return 0

    lax.fori_loop(0, key_tiles, prepare, 0)
    values[HEAD_DIM : HEAD_DIM + 16, :] = jnp.ones((16, places), bf16)

    def query_tile(index, _):
        first_query = pl.multiple_of(index * QUERIES, QUERIES)
        ones_row = jnp.where(row_index(16, QUERIES) == 0, 1.0, 0.0).astype(bf16)
        queries = jnp.concatenate(
            [x_ref[0, 0:HEAD_DIM, pl.ds(first_query, QUERIES)], ones_row, jnp.zeros((48, QUERIES), bf16)],
            axis=0,
        )

        def score(tile, held):
            start = pl.multiple_of(jnp.minimum(tile, key_tiles - 1) * KEYS, KEYS)
            scores = dot_nn(keys[pl.ds(start, KEYS), :], queries)
            held[...] = scores
            return jnp.max(scores, axis=0, keepdims=True)

        def step(tile, held, carry):
            largest, total, next_largest = carry
            updated = jnp.maximum(largest, next_largest)
            start = pl.multiple_of(tile * KEYS, KEYS)
            chances = jnp.exp2(held[...] - updated).astype(bf16)
            total = total * jnp.exp2(largest - updated) + dot_nn(
                values[:, pl.ds(start, KEYS)], chances
            )
            return updated, total

        def two_steps(pair, carry):
            upper = score(2 * pair + 1, odd)
            carry = step(2 * pair, even, carry)
            lower = score(2 * pair + 2, even)
            return *step(2 * pair + 1, odd, (*carry, upper)), lower

        count = jnp.minimum(index * per_query, key_tiles)
        largest = jnp.full((1, QUERIES), NEGATIVE, f32)
        total = jnp.zeros((HEAD_DIM + 16, QUERIES), f32)
        carry = lax.fori_loop(0, count // 2, two_steps, (largest, total, score(0, even)))

        def last_step_of(_, carry):
            return *step(count - 1, even, carry), carry[2]

        largest, total, _ = lax.fori_loop(0, lax.rem(count, 2), last_step_of, carry)

        def part(low, high, start, size, largest, total):
            scores = dot_nn(keys[pl.ds(start, size), :], queries[:, low:high])
            before = largest[:, low:high]
            updated = jnp.maximum(before, jnp.max(scores, axis=0, keepdims=True))
            chances = jnp.exp2(scores - updated).astype(bf16)
            summed = dot_nn(values[:, pl.ds(start, size)], chances)
            return updated, total[:, low:high] * jnp.exp2(before - updated) + summed

        for at in range(per_query):

            def diagonal(_, carry):
                largest, total = carry
                low = at * KEYS
                start = pl.multiple_of(first_query + low, KEYS)
                pieces = [(largest[:, :low], total[:, :low])] if low else []
                pieces.append(part(low, low + half, start, half, largest, total))
                pieces.append(part(low + half, low + KEYS, start, KEYS, largest, total))
                if low + KEYS < QUERIES:
                    pieces.append(part(low + KEYS, QUERIES, start, KEYS, largest, total))
                return tuple(jnp.concatenate(piece, axis=1) for piece in zip(*pieces))

            present = (index * per_query + at < key_tiles).astype(jnp.int32)
            largest, total = lax.fori_loop(0, present, diagonal, (largest, total))
        row_total = total[HEAD_DIM : HEAD_DIM + 1]
        inner = pl.multiple_of(lax.rem(index, quarter_tiles) * QUERIES, QUERIES)
        result = (total[:HEAD_DIM] / row_total).astype(bf16)
        slot = (index // quarter_tiles) ^ meta_ref[CONTEXT]
        for at, out_ref in enumerate(out_refs):

            @pl.when(slot == at)
            def _():
                out_ref[0, :, pl.ds(inner, QUERIES)] = result

        total_ref[0, :, pl.ds(first_query, QUERIES)] = largest + jnp.log2(row_total)
        return 0

    lax.fori_loop(0, places // QUERIES, query_tile, 0)


def self_forward(meta, projected, quarters, begin, units):
    places = projected.shape[2]
    quarter = places // quarters
    return pl.pallas_call(
        functools.partial(self_forward_kernel, begin=begin),
        grid_spec=pltpu.PrefetchScalarGridSpec(
            num_scalar_prefetch=1,
            grid=(units,),
            in_specs=[pl.BlockSpec((1, 3 * HEAD_DIM, places), lambda u, n: (begin + u, 0, 0))],
            out_specs=[pl.BlockSpec((1, HEAD_DIM, quarter), lambda u, n: (u, 0, 0))] * quarters
            + [pl.BlockSpec((1, 1, places), lambda u, n: (u, 0, 0))],
            scratch_shapes=[
                pltpu.VMEM((places, 128), bf16),
                pltpu.VMEM((HEAD_DIM + 16, places), bf16),
                pltpu.VMEM((KEYS, QUERIES), f32),
                pltpu.VMEM((KEYS, QUERIES), f32),
            ],
        ),
        out_shape=[jax.ShapeDtypeStruct((units, HEAD_DIM, quarter), bf16)] * quarters
        + [jax.ShapeDtypeStruct((units, 1, places), f32)],
        cost_estimate=lasting(20 * units),
        compiler_params=pltpu.CompilerParams(vmem_limit_bytes=VMEM_LIMIT),
        name="self_forward",
    )(meta, projected)


def self_backward_kernel(meta_ref, x_ref, total_ref, *refs, begin):
    keys, values, queries, backs, query_sum = refs[-5:]
    quarters = (len(refs) - 5) // 3
    out_refs, back_refs, grad_refs = (refs[at * quarters : (at + 1) * quarters] for at in range(3))
    length = meta_ref[UNIT_LENGTHS + begin + pl.program_id(0)]
    places = x_ref.shape[2]
    quarter_tiles = out_refs[0].shape[2] // KEYS
    half = BLK
    key_tiles = (length + KEYS - 1) // KEYS

    def prepare(tile, _):
        start = pl.multiple_of(tile * KEYS, KEYS)
        key_rows = x_ref[0, HEAD_DIM : 2 * HEAD_DIM, pl.ds(start, KEYS)].astype(f32)
        value_rows = x_ref[0, 2 * HEAD_DIM : 3 * HEAD_DIM, pl.ds(start, KEYS)].astype(f32)
        at, place = row_index(16, KEYS), place_index(16, KEYS, start)
        ones = jnp.where(at < 3, 1.0, 0.0)
        mask = jnp.where((at == 3) & (place >= length), NEGATIVE, ones)
        blank = jnp.zeros((48, KEYS), f32)
        keys[pl.ds(start, KEYS), :] = jnp.concatenate([key_rows, mask, blank], axis=0).T.astype(bf16)
        values[pl.ds(start, KEYS), :] = jnp.concatenate([value_rows, ones, blank], axis=0).T.astype(
            bf16
        )
        blank = blank.astype(bf16)
        queries[:, pl.ds(start, KEYS)] = jnp.concatenate(
            [
                x_ref[0, 0:HEAD_DIM, pl.ds(start, KEYS)],
                three_parts(-total_ref[0, :, pl.ds(start, KEYS)], True),
                blank,
            ],
            axis=0,
        )
        slot = (tile // quarter_tiles) ^ meta_ref[CONTEXT]
        inner = pl.multiple_of(lax.rem(tile, quarter_tiles) * KEYS, KEYS)
        for at in range(quarters):

            @pl.when(slot == at)
            def _():
                back = back_refs[at][0, :, pl.ds(inner, KEYS)]
                out = out_refs[at][0, :, pl.ds(inner, KEYS)]
                delta = jnp.sum(back.astype(f32) * out.astype(f32), axis=0, keepdims=True)
                backs[:, pl.ds(start, KEYS)] = jnp.concatenate(
                    [back, three_parts(-delta, False), blank], axis=0
                )

        query_sum[:, pl.ds(start, KEYS)] = jnp.zeros((HEAD_DIM, KEYS), f32)
        return 0

    lax.fori_loop(0, key_tiles, prepare, 0)

    def tile_terms(key_start, key_size, query_start, query_size, back_key, back_value):
        query = queries[:, pl.ds(query_start, query_size)]
        back = backs[:, pl.ds(query_start, query_size)]
        chances = jnp.exp2(dot_nn(keys[pl.ds(key_start, key_size), :], query))
        back_chances = dot_nn(values[pl.ds(key_start, key_size), :], back)
        back_scores = (chances * back_chances).astype(bf16)
        back_value = back_value + dot_nt(back[:HEAD_DIM], chances.astype(bf16))
        back_key = back_key + dot_nt(query[:HEAD_DIM], back_scores)
        query_sum[:, pl.ds(query_start, query_size)] += dot_nn(
            x_ref[0, HEAD_DIM : 2 * HEAD_DIM, pl.ds(key_start, key_size)], back_scores
        )
        return back_key, back_value

    def write(tile, rows, value):
        inner = pl.multiple_of(lax.rem(tile, quarter_tiles) * KEYS, KEYS)
        slot = (tile // quarter_tiles) ^ meta_ref[CONTEXT]
        for at in range(quarters):

            @pl.when(slot == at)
            def _():
                grad_refs[at][0, rows, pl.ds(inner, KEYS)] = value

    def key_tile(index, _):
        start = pl.multiple_of(index * KEYS, KEYS)
        second = pl.multiple_of(start + half, half)
        blank = jnp.zeros((HEAD_DIM, half), f32)
        first_part = tile_terms(start, half, start, KEYS, blank, blank)
        second_part = tile_terms(second, half, second, half, blank, blank)
        begun = tuple(jnp.concatenate(pair, axis=1) for pair in zip(first_part, second_part))

        def step(tile, carry):
            return tile_terms(start, KEYS, pl.multiple_of(tile * KEYS, KEYS), KEYS, *carry)

        back_key, back_value = lax.fori_loop(index + 1, key_tiles, step, begun)
        both = jnp.concatenate([back_key * (1.0 / LOG2E), back_value], axis=0).astype(bf16)
        write(index, slice(HEAD_DIM, 3 * HEAD_DIM), both)
        return 0

    lax.fori_loop(0, key_tiles, key_tile, 0)

    def finish(tile, _):
        start = pl.multiple_of(tile * KEYS, KEYS)
        write(tile, slice(0, HEAD_DIM), (query_sum[:, pl.ds(start, KEYS)] * SCALING).astype(bf16))
        return 0

    lax.fori_loop(0, key_tiles, finish, 0)

    def clear(tile, _):
        write(tile, slice(0, 3 * HEAD_DIM), jnp.zeros((3 * HEAD_DIM, KEYS), bf16))
        return 0

    lax.fori_loop(key_tiles, places // KEYS, clear, 0)


def self_backward(meta, projected, totals, attended, back, begin, origin):
    units, places = 1, projected.shape[2]
    quarters = len(attended)
    quarter = places // quarters
    return pl.pallas_call(
        functools.partial(self_backward_kernel, begin=begin),
        grid_spec=pltpu.PrefetchScalarGridSpec(
            num_scalar_prefetch=1,
            grid=(units,),
            in_specs=[
                pl.BlockSpec((1, 3 * HEAD_DIM, places), lambda u, n: (begin + u, 0, 0)),
                pl.BlockSpec((1, 1, places), lambda u, n: (begin - origin + u, 0, 0)),
            ]
            + [pl.BlockSpec((1, HEAD_DIM, quarter), lambda u, n: (begin - origin + u, 0, 0))]
            * quarters
            + [pl.BlockSpec((1, HEAD_DIM, quarter), lambda u, n: (begin + u, 0, 0))] * quarters,
            out_specs=[pl.BlockSpec((1, 3 * HEAD_DIM, quarter), lambda u, n: (u, 0, 0))] * quarters,
            scratch_shapes=[
                pltpu.VMEM((places, 128), bf16),
                pltpu.VMEM((places, 128), bf16),
                pltpu.VMEM((128, places), bf16),
                pltpu.VMEM((128, places), bf16),
                pltpu.VMEM((HEAD_DIM, places), f32),
            ],
        ),
        out_shape=[jax.ShapeDtypeStruct((units, 3 * HEAD_DIM, quarter), bf16)] * quarters,
        cost_estimate=lasting(30 * units),
        compiler_params=pltpu.CompilerParams(vmem_limit_bytes=VMEM_LIMIT),
        name="self_backward",
    )(meta, projected, totals, *attended, *back)


def cross_forward_kernel(meta_ref, query_ref, pair_ref, out_ref, total_ref):
    places = query_ref.shape[1]
    keys = pair_ref[0, 0, 0:HEAD_DIM, :].astype(f32).T.astype(bf16)
    values = jnp.concatenate(
        [pair_ref[0, 0, HEAD_DIM:, :], jnp.ones((16, pair_ref.shape[3]), bf16)], axis=0
    )
    for start in range(0, places, CROSS):
        scores = dot_nn(keys, query_ref[:, start : start + CROSS])
        largest = jnp.max(scores, axis=0, keepdims=True)
        chances = jnp.exp2(scores - largest).astype(bf16)
        total = dot_nn(values, chances)
        row_total = total[HEAD_DIM : HEAD_DIM + 1]
        out_ref[:, start : start + CROSS] = (total[:HEAD_DIM] / row_total).astype(bf16)
        total_ref[0, :, start : start + CROSS] = largest + jnp.log2(row_total)


def pair_spec(pairs):
    units = pairs.shape[1]

    def place(h, meta):
        return h // units, h % units, 0, 0

    return pl.BlockSpec((1, 1) + pairs.shape[2:], place)


def cross_forward(meta, queries, pairs):
    width, places = queries.shape
    rows = pl.BlockSpec((HEAD_DIM, places), lambda h, n: (h, 0))
    return pl.pallas_call(
        cross_forward_kernel,
        grid_spec=pltpu.PrefetchScalarGridSpec(
            num_scalar_prefetch=1,
            grid=(width // HEAD_DIM,),
            in_specs=[rows, pair_spec(pairs)],
            out_specs=[rows, pl.BlockSpec((1, 1, places), lambda h, n: (h, 0, 0))],
        ),
        out_shape=[
            jax.ShapeDtypeStruct((width, places), bf16),
            jax.ShapeDtypeStruct((width // HEAD_DIM, 1, places), f32),
        ],
        cost_estimate=lasting(25),
        compiler_params=pltpu.CompilerParams(vmem_limit_bytes=VMEM_LIMIT),
        name="cross_forward",
    )(meta, queries, pairs)


def cross_backward_kernel(
    meta_ref, query_ref, pair_ref, out_ref, back_ref, total_ref, grad_ref, pair_grad_ref
):
    places = query_ref.shape[1]
    rows = pair_ref.shape[3]
    at = row_index(64, rows)
    ones = jnp.where(at < 3, 1.0, 0.0)
    key_major = pair_ref[0, 0, 0:HEAD_DIM, :]
    keys = jnp.concatenate([key_major.astype(f32), ones], axis=0).T.astype(bf16)
    values = jnp.concatenate([pair_ref[0, 0, HEAD_DIM:, :].astype(f32), ones], axis=0).T.astype(bf16)
    blank = jnp.zeros((48, KEYS), bf16)
    back_key = jnp.zeros((HEAD_DIM, rows), f32)
    back_value = jnp.zeros((HEAD_DIM, rows), f32)
    for start in range(0, places, KEYS):
        span = slice(start, start + KEYS)
        plain, back = query_ref[:, span], back_ref[:, span]
        query = jnp.concatenate([plain, three_parts(-total_ref[0, :, span], False), blank], axis=0)
        delta = jnp.sum(back.astype(f32) * out_ref[:, span].astype(f32), axis=0, keepdims=True)
        back_rows = jnp.concatenate([back, three_parts(-delta, False), blank], axis=0)
        chances = jnp.exp2(dot_nn(keys, query))
        back_scores = (chances * dot_nn(values, back_rows)).astype(bf16)
        back_value = back_value + dot_nt(back, chances.astype(bf16))
        back_key = back_key + dot_nt(plain, back_scores)
        grad_ref[:, span] = (dot_nn(key_major, back_scores) * SCALING).astype(bf16)
    pair_grad_ref[0, 0, 0:HEAD_DIM, :] = (back_key * (1.0 / LOG2E)).astype(bf16)
    pair_grad_ref[0, 0, HEAD_DIM:, :] = back_value.astype(bf16)


def cross_backward(meta, queries, pairs, attended, back, totals):
    width, places = queries.shape
    rows = pl.BlockSpec((HEAD_DIM, places), lambda h, n: (h, 0))
    return pl.pallas_call(
        cross_backward_kernel,
        grid_spec=pltpu.PrefetchScalarGridSpec(
            num_scalar_prefetch=1,
            grid=(width // HEAD_DIM,),
            in_specs=[
                rows,
                pair_spec(pairs),
                rows,
                rows,
                pl.BlockSpec((1, 1, places), lambda h, n: (h, 0, 0)),
            ],
            out_specs=[rows, pair_spec(pairs)],
        ),
        out_shape=[
            jax.ShapeDtypeStruct((width, places), bf16),
            jax.ShapeDtypeStruct(pairs.shape, bf16),
        ],
        cost_estimate=lasting(36),
        compiler_params=pltpu.CompilerParams(vmem_limit_bytes=VMEM_LIMIT),
        name="cross_backward",
    )(meta, queries, pairs, attended, back, totals)


def normed(summed):
    centred = summed - jnp.mean(summed, axis=-1, keepdims=True)
    variance = jnp.mean(centred * centred, axis=-1, keepdims=True)
    inverse = lax.rsqrt(variance + EPSILON)
    return centred * inverse, inverse


def normed_back(normal, inverse, scaled):
    shared = jnp.mean(scaled, axis=-1, keepdims=True)
    along = jnp.mean(scaled * normal, axis=-1, keepdims=True)
    return (scaled - shared - normal * along) * inverse


def valid_column(meta_ref, quarter, rows):
    start = meta_ref[CONTEXT] * quarter + pl.program_id(0) * rows
    place = lax.broadcasted_iota(jnp.int32, (rows, 1), 0) + start
    return jnp.where(place < meta_ref[LENGTH], 1.0, 0.0)


def add_rows(sum_ref, *terms):
    @pl.when(pl.program_id(0) == 0)
    def _():
        sum_ref[...] = jnp.zeros_like(sum_ref)

    for at, term in enumerate(terms):
        sum_ref[at : at + 1, :] += jnp.sum(term, axis=0, keepdims=True)


def project_kernel(meta_ref, weight_ref, *refs, parts, rows):
    piece_refs, (x_ref, out_ref) = refs[:-2], refs[-2:]
    at_row = lax.broadcasted_iota(jnp.int32, (weight_ref.shape[0], 1), 0)
    scale = jnp.where(lax.rem(at_row, 3 * HEAD_DIM) < HEAD_DIM, QUERY_SCALE, 1.0)
    quarter = x_ref.shape[0] // (len(piece_refs) // parts)
    for at, piece_ref in enumerate(piece_refs):
        step, part = divmod(at, parts)
        result = (dot_nt(weight_ref[...], piece_ref[...]) * scale).astype(bf16)
        for block in range(quarter // (rows * parts)):
            place = (block * parts + part) * rows
            start = pl.multiple_of((meta_ref[CONTEXT] ^ step) * quarter + place, rows)
            run = slice(block * rows, (block + 1) * rows)
            x_ref[pl.ds(start, rows), :] = piece_ref[run, :]
            out_ref[:, pl.ds(start, rows)] = result[:, run]


def project(meta, weight, pieces, parts, rows):
    places, width = pieces[0].shape[0] * len(pieces), pieces[0].shape[1]
    whole = pl.BlockSpec(memory_space=pltpu.VMEM)
    return pl.pallas_call(
        functools.partial(project_kernel, parts=parts, rows=rows),
        in_specs=[pl.BlockSpec(memory_space=pltpu.SMEM)] + [whole] * (1 + len(pieces)),
        out_specs=[whole, whole],
        out_shape=[
            jax.ShapeDtypeStruct((places, width), bf16),
            jax.ShapeDtypeStruct((weight.shape[0], places), bf16),
        ],
        cost_estimate=lasting(10),
        compiler_params=pltpu.CompilerParams(vmem_limit_bytes=VMEM_LIMIT),
        name="project",
    )(meta, weight, *pieces)


def first_kernel(
    meta_ref, x_ref, norm_ref, out_w_ref, query_w_ref, *refs, quarter
):
    att_refs, (sum_ref, low_ref, query_ref, total_ref) = refs[:-4], refs[-4:]
    groups = query_w_ref.shape[0]
    branch = None
    for at in range(groups):
        att = jnp.concatenate([ref[...] for ref in att_refs[at::groups]], axis=0)
        term = dot_tt(att, out_w_ref[meta_ref[CONTEXT] ^ at])
        branch = term if branch is None else branch + term
    x = x_ref[...].astype(f32)
    summed = x + branch
    normal, _ = normed(summed)
    first = normal * norm_ref[0:1, :] + norm_ref[3:4, :]
    first_low = first.astype(bf16)
    sum_ref[...] = summed
    low_ref[...] = first_low
    query = jnp.concatenate([dot_nn(first_low, query_w_ref[at]) for at in range(groups)], axis=1)
    query_ref[...] = (query * QUERY_SCALE).T.astype(bf16)
    valid = valid_column(meta_ref, quarter, x.shape[0])
    add_rows(total_ref, valid * x * x, valid * branch * branch, valid * first * first)


def whole_spec(array):
    zeros = (0,) * array.ndim
    return pl.BlockSpec(array.shape, lambda b, n: zeros, pipeline_mode=pl.Buffered(1))


def first_step(meta, x_all, norms, out_w, query_w, att, rows):
    width = x_all.shape[1]
    quarter = att[0].shape[1]
    blocks = quarter // rows
    tokens = pl.BlockSpec((rows, width), lambda b, n: (b, 0))
    turned = pl.BlockSpec((width, rows), lambda b, n: (0, b))
    return pl.pallas_call(
        functools.partial(first_kernel, quarter=quarter),
        grid_spec=pltpu.PrefetchScalarGridSpec(
            num_scalar_prefetch=1,
            grid=(blocks,),
            in_specs=[
                pl.BlockSpec((rows, width), lambda b, n: (n[CONTEXT] * blocks + b, 0)),
                whole_spec(norms),
                whole_spec(out_w),
                whole_spec(query_w),
            ]
            + [pl.BlockSpec((piece.shape[0], rows), lambda b, n: (0, b)) for piece in att],
            out_specs=[tokens, tokens, turned, pl.BlockSpec((8, width), lambda b, n: (0, 0))],
        ),
        out_shape=[
            jax.ShapeDtypeStruct((quarter, width), f32),
            jax.ShapeDtypeStruct((quarter, width), bf16),
            jax.ShapeDtypeStruct((width, quarter), bf16),
            jax.ShapeDtypeStruct((8, width), f32),
        ],
        cost_estimate=lasting(8),
        compiler_params=pltpu.CompilerParams(vmem_limit_bytes=VMEM_LIMIT),
        name="first_step",
    )(meta, x_all, norms, out_w, query_w, *att)


def gelu_and_slope(inner):
    chance = 0.5 * (1.0 + lax.erf(inner * 0.7071067811865476))
    density = jnp.exp2(inner * inner * (-0.5 * LOG2E)) * 0.3989422804014327
    return inner * chance, chance + inner * density


def feed_kernel(
    meta_ref, att_ref, sum_ref, norm_ref, out_w_ref, feed_ref, *refs, quarter
):
    groups, width = feed_ref.shape[0], sum_ref.shape[1]
    cot_ref, output_ref, *refs = refs
    low_ref, active_ref, inner_ref, back_three_ref, back_two_ref, back_sum_ref, back_att_ref = refs[:7]
    total_ref, slope_ref = refs[7:]
    rows = sum_ref.shape[0]
    part = out_w_ref.shape[2]
    gain = [norm_ref[at : at + 1, :] for at in range(3)]
    bias = [norm_ref[3 + at : 4 + at, :] for at in range(3)]
    branch_two = None
    for at in range(groups):
        term = dot_tt(att_ref[at * part : (at + 1) * part, :], out_w_ref[at])
        branch_two = term if branch_two is None else branch_two + term
    normal, _ = normed(sum_ref[...])
    normal_two, inverse_two = normed(normal * gain[0] + bias[0] + branch_two)
    second = normal_two * gain[1] + bias[1]
    second_low = second.astype(bf16)
    low_ref[...] = second_low
    branch_three = None
    for at in range(groups):
        inner = dot_nn(second_low, feed_ref[at, :, :width])
        active, slope = gelu_and_slope(inner)
        active = active.astype(bf16)
        active_ref[:, at * width : (at + 1) * width] = active
        slope_ref[:, at * width : (at + 1) * width] = slope
        term = dot_nt(active, feed_ref[at, :, width:])
        branch_three = term if branch_three is None else branch_three + term
    normal_three, inverse_three = normed(second + branch_three)
    output_ref[...] = (normal_three * gain[2] + bias[2]).astype(bf16)
    valid = valid_column(meta_ref, quarter, rows)
    back_output = cot_ref[...].astype(f32) * valid
    back_third = normed_back(normal_three, inverse_three, back_output * gain[2])
    back_three = back_third.astype(bf16)
    back_three_ref[...] = back_three
    back_second = back_third
    for at in range(groups):
        back_active = dot_nn(back_three, feed_ref[at, :, width:])
        back_inner = (back_active * slope_ref[:, at * width : (at + 1) * width]).astype(bf16)
        inner_ref[:, at * width : (at + 1) * width] = back_inner
        back_second = back_second + dot_nt(back_inner, feed_ref[at, :, :width])
    back_second_sum = normed_back(normal_two, inverse_two, back_second * gain[1])
    back_sum_ref[...] = back_second_sum
    back_two = back_second_sum.astype(bf16)
    back_two_ref[...] = back_two
    back_att = jnp.concatenate([dot_nn(back_two, out_w_ref[at]) for at in range(groups)], axis=1)
    back_att_ref[...] = back_att.T.astype(bf16)
    add_rows(
        total_ref,
        valid * branch_two * branch_two,
        valid * second * second,
        valid * branch_three * branch_three,
        back_second * normal_two,
        back_output * normal_three,
        back_second,
        back_output,
    )


def feed_step(meta, att, first_sum, norms, out_w, feed, cotangent, rows):
    quarter, width = first_sum.shape
    groups = feed.shape[0]
    hidden_width = groups * width
    tokens = pl.BlockSpec((rows, width), lambda b, n: (b, 0))
    wide = pl.BlockSpec((rows, hidden_width), lambda b, n: (b, 0))
    turned = pl.BlockSpec((width, rows), lambda b, n: (0, b))
    return pl.pallas_call(
        functools.partial(feed_kernel, quarter=quarter),
        grid_spec=pltpu.PrefetchScalarGridSpec(
            num_scalar_prefetch=1,
            grid=(quarter // rows,),
            in_specs=[
                turned,
                tokens,
                whole_spec(norms),
                whole_spec(out_w),
                pl.BlockSpec(
                    (groups, width, 2 * width), lambda b, n: (0, 0, 0), pipeline_mode=pl.Buffered(1)
                ),
                tokens,
            ],
            out_specs=[tokens, tokens, wide, wide, tokens, tokens, tokens, turned]
            + [pl.BlockSpec((8, width), lambda b, n: (0, 0))],
            scratch_shapes=[pltpu.VMEM((rows, hidden_width), f32)],
        ),
        out_shape=[
            jax.ShapeDtypeStruct((quarter, width), bf16),
            jax.ShapeDtypeStruct((quarter, width), bf16),
            jax.ShapeDtypeStruct((quarter, hidden_width), bf16),
            jax.ShapeDtypeStruct((quarter, hidden_width), bf16),
            jax.ShapeDtypeStruct((quarter, width), bf16),
            jax.ShapeDtypeStruct((quarter, width), bf16),
            jax.ShapeDtypeStruct((quarter, width), f32),
            jax.ShapeDtypeStruct((width, quarter), bf16),
            jax.ShapeDtypeStruct((8, width), f32),
        ],
        cost_estimate=lasting(45),
        compiler_params=pltpu.CompilerParams(vmem_limit_bytes=VMEM_LIMIT),
        name="feed_step",
    )(meta, att, first_sum, norms, out_w, feed, cotangent)


def last_kernel(meta_ref, query_ref, back_sum_ref, sum_ref, norm_ref, query_w_ref, out_w_ref, *refs):
    back_refs, (back_ref, low_ref, total_ref) = refs[:-3], refs[-3:]
    groups, _, part = query_w_ref.shape
    back_first = back_sum_ref[...]
    for at in range(groups):
        back_first = back_first + dot_tt(query_ref[at * part : (at + 1) * part, :], query_w_ref[at])
    normal, inverse = normed(sum_ref[...])
    back_first_sum = normed_back(normal, inverse, back_first * norm_ref[0:1, :])
    back_ref[...] = back_first_sum
    back_one = back_first_sum.astype(bf16)
    low_ref[...] = back_one
    for at, ref in enumerate(back_refs):
        ref[...] = dot_nn(back_one, out_w_ref[meta_ref[CONTEXT] ^ at]).T.astype(bf16)
    add_rows(total_ref, back_first * normal, back_first)


def last_step(meta, back_query, back_second_sum, first_sum, norms, query_w, out_w, rows):
    quarter, width = first_sum.shape
    groups, _, part = query_w.shape
    tokens = pl.BlockSpec((rows, width), lambda b, n: (b, 0))
    turned = pl.BlockSpec((width, rows), lambda b, n: (0, b))
    return pl.pallas_call(
        last_kernel,
        grid_spec=pltpu.PrefetchScalarGridSpec(
            num_scalar_prefetch=1,
            grid=(quarter // rows,),
            in_specs=[
                turned,
                tokens,
                tokens,
                whole_spec(norms),
                whole_spec(query_w),
                whole_spec(out_w),
            ],
            out_specs=[pl.BlockSpec((part, rows), lambda b, n: (0, b))] * groups
            + [tokens, tokens, pl.BlockSpec((8, width), lambda b, n: (0, 0))],
        ),
        out_shape=[jax.ShapeDtypeStruct((part, quarter), bf16)] * groups
        + [
            jax.ShapeDtypeStruct((quarter, width), f32),
            jax.ShapeDtypeStruct((quarter, width), bf16),
            jax.ShapeDtypeStruct((8, width), f32),
        ],
        cost_estimate=lasting(8),
        compiler_params=pltpu.CompilerParams(vmem_limit_bytes=VMEM_LIMIT),
        name="last_step",
    )(meta, back_query, back_second_sum, first_sum, norms, query_w, out_w)


def hidden_kernel(meta_ref, back_ref, weight_ref, *refs):
    groups = weight_ref.shape[0]
    whole_ref, part_refs, out_ref = refs[0], refs[1:-1], refs[-1]
    total = back_ref[...]
    for at in range(groups):
        group = meta_ref[CONTEXT] ^ at
        part = [whole_ref[group]] + [ref[...] for ref in part_refs[at::groups]]
        part = jnp.concatenate(part, axis=0)
        total = total + dot_tt(part, weight_ref[group])
    out_ref[...] = total.astype(bf16)


def hidden_step(meta, back_first_sum, weights, parts, rows):
    quarter, width = back_first_sum.shape

    def columns(part):
        lead = part.shape[:-1]
        zeros = (0,) * len(lead)
        return pl.BlockSpec(lead + (rows,), lambda b, n: zeros + (b,))

    return pl.pallas_call(
        hidden_kernel,
        grid_spec=pltpu.PrefetchScalarGridSpec(
            num_scalar_prefetch=1,
            grid=(quarter // rows,),
            in_specs=[
                pl.BlockSpec((rows, width), lambda b, n: (b, 0)),
                whole_spec(weights),
            ]
            + [columns(part) for part in parts],
            out_specs=pl.BlockSpec((rows, width), lambda b, n: (b, 0)),
        ),
        out_shape=jax.ShapeDtypeStruct((quarter, width), bf16),
        cost_estimate=lasting(8),
        compiler_params=pltpu.CompilerParams(vmem_limit_bytes=VMEM_LIMIT),
        name="hidden_step",
    )(meta, back_first_sum, weights, *parts)


def turned_once(pairs):
    @pl.when(pl.program_id(0) == 0)
    def _():
        for source, target in pairs:
            target[...] = source[...].astype(f32).T.astype(bf16)


def put_halves(meta_ref, keep_ref, send_ref, low, high, result):
    shards, rows = keep_ref.shape[1:3]
    core = lax.rem(meta_ref[CONTEXT], 2)
    result = result.astype(bf16)
    for half, (even_ref, odd_ref) in enumerate(((keep_ref, send_ref), (send_ref, keep_ref))):

        @pl.when(core == half)
        def _():
            for shard in range(shards):
                start = 2 * shard * rows
                even_ref[0, shard, :, low:high] = result[start : start + rows]
                odd_ref[0, shard, :, low:high] = result[start + rows : start + 2 * rows]


def feed_grad_kernel(
    meta_ref, low_ref, inner_ref, back_ref, active_ref, two_ref, cross_ref, keep_ref, send_ref, *turned
):
    width = low_ref.shape[1]
    put = functools.partial(put_halves, meta_ref, keep_ref, send_ref)
    turned_once(zip((low_ref, back_ref, two_ref), turned))
    put(0, width, dot_nn(turned[0][...], inner_ref[...]))
    put(width, 2 * width, dot_nn(turned[1][...], active_ref[...]))
    put(2 * width, keep_ref.shape[3], dot_nt(turned[2][...], cross_ref[...]))


def feed_grad(meta, second_low, back_inner, back_three, active, back_two, cross_att, shards):
    tokens, width = second_low.shape
    groups = active.shape[1] // width
    part = width // groups
    left = pl.BlockSpec((tokens, width), lambda b, n: (0, 0))
    right = pl.BlockSpec((tokens, width), lambda b, n: (0, b))
    half = (shards, width // (2 * shards), 2 * width + part)
    return pl.pallas_call(
        feed_grad_kernel,
        grid_spec=pltpu.PrefetchScalarGridSpec(
            num_scalar_prefetch=1,
            grid=(groups,),
            in_specs=[
                left,
                right,
                left,
                right,
                left,
                pl.BlockSpec((part, tokens), lambda b, n: (b, 0)),
            ],
            out_specs=[pl.BlockSpec((1,) + half, lambda b, n: (b, 0, 0, 0))] * 2,
            scratch_shapes=[pltpu.VMEM((width, tokens), bf16)] * 3,
        ),
        out_shape=[jax.ShapeDtypeStruct((groups,) + half, bf16)] * 2,
        cost_estimate=lasting(18),
        compiler_params=pltpu.CompilerParams(vmem_limit_bytes=VMEM_LIMIT),
        name="feed_grad",
    )(meta, second_low, back_inner, back_three, active, back_two, cross_att)


def mixed_grad_kernel(
    meta_ref, one_ref, low_ref, selected_ref, query_ref, pair_ref, *refs
):
    keep_ref, send_ref, *turned = refs[-5:]
    att_refs = refs[:-5]
    turned_once(zip((one_ref, low_ref, selected_ref), turned))
    slot = pl.program_id(0) ^ meta_ref[CONTEXT]
    att = None
    for at in range(4):
        piece = jnp.concatenate([ref[...] for ref in att_refs[at::4]], axis=0)
        att = piece if att is None else jnp.where(slot == at, piece, att)
    result = jnp.concatenate(
        [
            dot_nt(turned[0][...], att),
            dot_nt(turned[1][...], query_ref[...]),
            dot_nt(turned[2][...], pair_ref[0]),
        ],
        axis=1,
    )
    put_halves(meta_ref, keep_ref, send_ref, 0, result.shape[1], result)


def mixed_grad(meta, back_one, first_low, selected, back_query, back_pairs, att, shards):
    tokens, width = back_one.shape
    groups = 4
    part = width // groups
    pair_width, retrieved = back_pairs.shape[1:]
    half = (shards, width // (2 * shards), 2 * part + pair_width)
    return pl.pallas_call(
        mixed_grad_kernel,
        grid_spec=pltpu.PrefetchScalarGridSpec(
            num_scalar_prefetch=1,
            grid=(groups,),
            in_specs=[
                whole_spec(back_one),
                whole_spec(first_low),
                whole_spec(selected),
                pl.BlockSpec((part, tokens), lambda b, n: (b, 0)),
                pl.BlockSpec((1, pair_width, retrieved), lambda b, n: (b, 0, 0)),
            ]
            + [whole_spec(piece) for piece in att],
            out_specs=[pl.BlockSpec((1,) + half, lambda b, n: (b, 0, 0, 0))] * 2,
            scratch_shapes=[
                pltpu.VMEM((width, tokens), bf16),
                pltpu.VMEM((width, tokens), bf16),
                pltpu.VMEM((width, retrieved), bf16),
            ],
        ),
        out_shape=[jax.ShapeDtypeStruct((groups,) + half, bf16)] * 2,
        cost_estimate=lasting(14),
        compiler_params=pltpu.CompilerParams(vmem_limit_bytes=VMEM_LIMIT),
        name="mixed_grad",
    )(meta, back_one, first_low, selected, back_query, back_pairs, *att)


def own_grad_kernel(meta_ref, x_ref, *refs):
    part_refs, out_ref = refs[:-1], refs[-1]
    quarter = part_refs[0].shape[1]
    total = None
    for at, part_ref in enumerate(part_refs):
        start = pl.multiple_of((meta_ref[CONTEXT] ^ at) * quarter, quarter)
        term = dot_nn(part_ref[...], x_ref[pl.ds(start, quarter), :])
        total = term if total is None else total + term
    out_ref[...] = total.T.astype(bf16)


def own_grad(meta, x_all, parts):
    whole = pl.BlockSpec(memory_space=pltpu.VMEM)
    return pl.pallas_call(
        own_grad_kernel,
        in_specs=[pl.BlockSpec(memory_space=pltpu.SMEM)] + [whole] * (1 + len(parts)),
        out_specs=whole,
        out_shape=jax.ShapeDtypeStruct((x_all.shape[1], parts[0].shape[0]), bf16),
        cost_estimate=lasting(7),
        compiler_params=pltpu.CompilerParams(vmem_limit_bytes=VMEM_LIMIT),
        name="own_grad",
    )(meta, x_all, *parts)


def product(spec, left, right):
    return jnp.einsum(spec, left, right, preferred_element_type=f32)


def turn(array, axis, step):
    count = lax.axis_size(axis)
    return lax.ppermute(array, axis, [(at, at ^ step) for at in range(count)])


def to_others(parts, axis):
    return [parts[0]] + [turn(parts[at], axis, at) for at in range(1, len(parts))]


def gather_context(array):
    far = turn(array, "ctx", 2)
    return [array, turn(array, "ctx", 1), far, turn(far, "ctx", 1)]


def gather(array, axis, dim):
    step = 1
    while step < lax.axis_size(axis):
        other = turn(array, axis, step)
        later = (lax.axis_index(axis) & step) > 0
        array = jnp.concatenate(
            [jnp.where(later, other, array), jnp.where(later, array, other)], axis=dim
        )
        step *= 2
    return array


def in_slots(pieces, index):
    for step in (1, 2):
        later = (index & step) > 0
        pieces = [jnp.where(later, pieces[at ^ step], pieces[at]) for at in range(len(pieces))]
    return pieces


def gather_direct(array, axis, dim):
    pieces = [array] + [turn(array, axis, at) for at in range(1, 4)]
    return jnp.concatenate(in_slots(pieces, lax.axis_index(axis)), axis=dim)


def exchange(parts, axes):
    return lax.all_to_all(parts, axes, split_axis=0, concat_axis=0, tiled=True)


def add_up(pieces):
    total = pieces[0].astype(f32)
    for piece in pieces[1:]:
        total = total + piece.astype(f32)
    return total


def sum_everywhere(vector):
    steps = []
    for axis in ("ctx", "tp", "shard"):
        step = 1
        while step < lax.axis_size(axis):
            vector = vector + turn(vector, axis, step)
            steps.append(vector)
            step *= 2
    return steps


class StagedSum:
    def __init__(self, keep, send):
        self.terms, self.send = [keep], send

    def beside(self, kernel):
        self.terms[1:] = [after(term, kernel) for term in self.terms[1:]]

    def over_core(self):
        self.terms.append(turn(self.send, "ctx", 1))

    def over_shard(self):
        count, index = lax.axis_size("shard"), lax.axis_index("shard")

        def part(at):
            return add_up([lax.dynamic_index_in_dim(t, at, 1, keepdims=False) for t in self.terms])

        if count == 2:
            self.send = part(1 - index).astype(bf16)
            own = [lax.dynamic_index_in_dim(t, index, 1, keepdims=False) for t in self.terms]
            self.terms = own + [turn(self.send, "shard", 1)]
        else:
            self.send = jnp.moveaxis(add_up(self.terms).astype(bf16), 1, 0)
            self.terms = [jnp.sum(exchange(self.send, "shard").astype(f32), axis=0).astype(bf16)]

    def over_x(self):
        rows = self.terms[0].shape[1] // 2
        index = lax.axis_index("ctx") // 2

        def part(at):
            return [lax.dynamic_slice_in_dim(t, at * rows, rows, 1) for t in self.terms]

        self.send = add_up(part(1 - index)).astype(bf16)
        self.terms = part(index) + [turn(self.send, "ctx", 2)]

    def send_of_quarter(self):
        self.terms = [add_up(self.terms).astype(bf16)]
        return self.terms[0]

    def over_tensor_at_once(self):
        self.send = add_up(self.terms).astype(bf16)
        self.terms = [exchange(self.send, "tp")]

    def over_tensor(self):
        self.send = add_up(self.terms).astype(bf16)
        index = lax.axis_index("tp")
        parts = [
            lax.dynamic_index_in_dim(self.send, index ^ at, 0, keepdims=False)
            for at in range(self.send.shape[0])
        ]
        self.terms = to_others(parts, "tp")

    def total(self):
        self.send = add_up(self.terms).astype(bf16)
        return self.send

    def spread(self):
        total = self.send
        for step in (2, 1):
            other = turn(total, "ctx", step)
            later = (lax.axis_index("ctx") & step) > 0
            total = jnp.concatenate(
                [jnp.where(later, other, total), jnp.where(later, total, other)], axis=0
            )
        return total.astype(f32)


def after(value, *earlier):
    return lax.optimization_barrier((value,) + earlier)[0]


def per_device(
    hidden,
    bank,
    indices,
    lengths,
    cotangent,
    query_self,
    key_self,
    value_self,
    out_self,
    query_cross,
    key_cross,
    value_cross,
    out_cross,
    up_weight,
    down_weight,
    norm_gain,
    norm_bias,
):
    context_count = lax.axis_size("ctx")
    tensor_count = lax.axis_size("tp")
    shard_index = lax.axis_index("shard")
    context_index = lax.axis_index("ctx")
    tensor_index = lax.axis_index("tp")
    group_sequences, device_places, model_width = hidden.shape
    units = HEADS // context_count
    group_width = units * HEAD_DIM
    quarter = device_places * tensor_count
    shard_rows = query_self.shape[0]
    piece_rows = shard_rows // context_count
    feed_width = up_weight.shape[1]

    swap = [
        (c * tensor_count + z, z * context_count + c)
        for c in range(context_count)
        for z in range(tensor_count)
    ]

    group_lengths = lax.dynamic_slice_in_dim(
        lengths, shard_index * group_sequences, group_sequences
    )
    length = group_lengths[tensor_index]
    meta = jnp.stack([context_index, tensor_index, length] + [length] * units).astype(jnp.int32)

    def by_unit(weights):
        stacked = jnp.stack([w.reshape(-1, units, HEAD_DIM) for w in weights], axis=2)
        return stacked.reshape(weights[0].shape[0], -1)

    local_self = by_unit([query_self, key_self, value_self])
    local_pair = by_unit([key_cross, value_cross])
    self_width, pair_width = local_self.shape[1], local_pair.shape[1]

    def gather_all(columns):
        rows = lax.dynamic_slice_in_dim(columns, context_index * piece_rows, piece_rows, 0)
        everything = lax.all_gather(rows, ("tp", "shard", "ctx"), axis=0, tiled=True)
        return everything.reshape(tensor_count, model_width, columns.shape[1])

    bank_local = bank.shape[1]
    retrieved = indices.shape[1]
    owner_tensor = indices[0] // bank_local
    local_rows = indices[0] - owner_tensor * bank_local
    owned = (owner_tensor == tensor_index)[:, None]
    picked = jnp.where(owned, jnp.take(bank[0], local_rows, axis=0), jnp.zeros((), bf16))

    x_low = exchange(hidden, "tp").reshape(quarter, model_width)
    own_self = gather(lax.ppermute(local_self.T, ("ctx", "tp"), swap), "shard", 1)
    far = after(turn(x_low, "ctx", 2), own_self, picked, meta)
    x_parts = [x_low, turn(x_low, "ctx", 1), far, turn(far, "ctx", 1)]
    picked = exchange(after(picked, x_low).reshape(tensor_count, -1, model_width), "tp")
    x_all, projected = project(meta, own_self, x_parts, 1, device_places)
    projected = projected.reshape(units, 3 * HEAD_DIM, -1)

    norms = jnp.concatenate([norm_gain, norm_bias], axis=0).T
    bundle = [up_weight, down_weight.T, out_self.T, query_cross, out_cross.T, local_pair, norms]
    feed = gather_all(after(jnp.concatenate(bundle, axis=1), x_low))
    bundle = feed[:, :, 2 * feed_width :]
    out_self_t = bundle[:, :, :group_width]
    query_cross_w = bundle[:, :, group_width : 2 * group_width]
    out_cross_t = bundle[:, :, 2 * group_width : 3 * group_width]
    pair_w = bundle[:, :, 3 * group_width : 3 * group_width + pair_width]
    norm_rows = bundle[0, :, 3 * group_width + pair_width :].T.astype(f32)
    norm_rows = jnp.pad(norm_rows, ((0, 2), (0, 0)))

    self_out, self_totals, self_att = [], [], []

    def forward(begin, *ready):
        *out, total = self_forward(meta, after(projected, *ready), context_count, begin, 1)
        self_out.append(out)
        self_totals.append(total)
        self_att.extend(piece.reshape(-1, quarter) for piece in to_others(out, "ctx"))
        return total

    done = forward(1, forward(0))
    picked = jnp.sum(after(picked, done).astype(f32), axis=0).astype(bf16)
    done = forward(2, picked, done, *self_att[:context_count])
    self_att[context_count : 2 * context_count] = [
        after(piece, done) for piece in self_att[context_count : 2 * context_count]
    ]
    picked = after(lax.ppermute(picked, ("ctx", "tp"), swap), done)
    lists = [picked] + [turn(picked, "ctx", at) for at in range(1, context_count)]
    cot = exchange(after(cotangent, *self_att[-context_count:]), "tp")
    first_sum, first_low, cross_query, first_totals = first_step(
        meta, after(x_all, picked), norm_rows, out_self_t, query_cross_w, self_att, device_places
    )
    lists = [after(piece, first_low) for piece in lists]
    selected = jnp.concatenate(in_slots(lists, context_index))
    pairs = product("tdf,kd->tfk", pair_w, selected).astype(bf16)
    pairs = pairs.reshape(context_count, units, 2 * HEAD_DIM, retrieved)
    cross_att, cross_total = cross_forward(meta, cross_query, pairs)
    cot = after(cot, cross_att).reshape(quarter, model_width)
    fed = feed_step(meta, cross_att, first_sum, norm_rows, out_cross_t, feed, cot, device_places)
    output, second_low, active, back_inner, back_three, back_two, back_second_sum, back_cross, totals = fed
    shard_count = lax.axis_size("shard")
    feed_sum = StagedSum(
        *feed_grad(
            meta, second_low, back_inner, back_three, active, back_two, cross_att, shard_count
        )
    )
    feed_sum.over_core()
    output = exchange(output.reshape(tensor_count, device_places, model_width), "tp")
    self_w = gather_all(after(local_self, first_low))
    back_query, back_pairs = cross_backward(
        meta, cross_query, pairs, cross_att, after(back_cross, feed_sum.send, self_w), cross_total
    )
    back_pairs = back_pairs.reshape(context_count, pair_width, retrieved)
    feed_sum.over_shard()
    back_selected = product("tfk,tdf->kd", back_pairs, pair_w).astype(bf16)
    back_selected = back_selected.reshape(context_count, -1, model_width)
    *back_self, back_first_sum, back_one, last_totals = last_step(
        meta,
        back_query,
        after(back_second_sum, output, feed_sum.send, back_selected),
        first_sum,
        norm_rows,
        query_cross_w,
        out_self_t,
        device_places,
    )
    back_selected = after(exchange(back_selected, "ctx"), back_one)
    back_self = [piece.reshape(units, HEAD_DIM, quarter) for piece in to_others(back_self, "ctx")]
    mixed_sum = StagedSum(
        *mixed_grad(
            meta, back_one, first_low, selected, back_query, back_pairs, self_att, shard_count
        )
    )

    squares = jnp.sum(jnp.concatenate([first_totals[:3], totals[:3]], axis=0), axis=1)
    rows = jnp.stack(
        [
            last_totals[0],
            totals[3],
            totals[4],
            last_totals[1],
            totals[5],
            totals[6],
            jnp.pad(squares, (0, model_width - squares.shape[0])),
        ]
    )

    def backward(begin, *ready):
        return self_backward(
            meta,
            after(projected, *ready),
            self_totals[begin],
            self_out[begin],
            back_self,
            begin,
            begin,
        )

    def parts_of(grads):
        return [piece.reshape(-1, quarter) for piece in to_others(grads, "ctx")]

    back_selected = jnp.sum(back_selected.astype(f32), axis=0).astype(bf16)
    grads = [backward(0, mixed_sum.send, back_selected)]
    mixed_sum.over_core()
    back_rows = lax.ppermute(back_selected, ("ctx", "tp"), swap)
    for running in (feed_sum, mixed_sum):
        running.beside(grads[0][0])
    back_rows = after(back_rows, grads[0][0])
    feed_sum.over_x()
    mixed_sum.over_shard()

    back_parts = [exchange(jnp.concatenate(in_slots(grads[0], context_index)), "ctx")]
    grads.append(backward(1, back_rows, feed_sum.send, mixed_sum.send, *grads[0]))
    back_rows = [back_rows] + [turn(back_rows, "tp", at) for at in range(1, tensor_count)]
    back_rows = [after(piece, grads[1][0]) for piece in back_rows]
    back_parts = [after(back_parts[0], grads[1][0])]
    own_grads = []
    for running in (feed_sum, mixed_sum):
        running.beside(grads[1][0])
    feed_sum.over_tensor_at_once()
    mixed_sum.over_x()

    back_parts += parts_of(grads[1])
    ready = (feed_sum.send, mixed_sum.send, back_parts[0], *back_rows)
    grads.append(backward(2, *ready, *grads[1]))
    back_parts[2:] = [after(part, grads[2][0]) for part in back_parts[2:]]
    feed_sum.terms = [jnp.sum(after(feed_sum.terms[0], grads[2][0]).astype(f32), axis=0)]
    mixed_sum.beside(grads[2][0])
    back_parts += parts_of(grads[2])
    mixed_sum.over_tensor()
    own_grads = []
    ready = (feed_sum.total(), *back_parts[2:5])
    for at in range(units):
        own_grads.append(
            own_grad(meta, after(x_all, *ready), [p.reshape(-1, quarter) for p in grads[at]])
        )
    own_sum = jnp.concatenate(own_grads, axis=1)
    own_sum = own_sum.reshape(shard_count, -1, own_sum.shape[1])
    back_hidden = hidden_step(
        meta, after(back_first_sum, own_sum), self_w, back_parts, device_places
    )

    if shard_count == 2:
        mine = lax.dynamic_index_in_dim(own_sum, shard_index, 0, keepdims=False)
        other = lax.dynamic_index_in_dim(own_sum, 1 - shard_index, 0, keepdims=False)
        own_sum = add_up([mine, after(turn(other, "shard", 1), back_hidden)])
    else:
        own_sum = jnp.sum(exchange(own_sum, "shard").astype(f32), axis=0)
    mixed_sum.beside(back_hidden)
    mixed_sum.total()
    own_sum = own_sum.astype(bf16).reshape(tensor_count, -1, own_sum.shape[-1])
    own_sum = [
        lax.dynamic_index_in_dim(own_sum, tensor_index ^ at, 0, keepdims=False)
        for at in range(tensor_count)
    ]
    back_rows = [after(piece, back_hidden, mixed_sum.send, *own_sum) for piece in back_rows]
    back_rows = jnp.concatenate(in_slots(back_rows, tensor_index))
    back_hidden = exchange(back_hidden.reshape(tensor_count, device_places, model_width), "tp")
    back_rows = jnp.where(owned, back_rows.astype(f32), 0.0)
    back_bank = jnp.zeros(bank.shape[1:], f32).at[local_rows].add(back_rows)[None]
    own_sum = to_others(own_sum, "tp")
    own_sum = [own_sum[0]] + [after(piece, back_bank) for piece in own_sum[1:]]
    own_sum = add_up(own_sum).astype(bf16)
    own_sum = lax.ppermute(own_sum, ("ctx", "tp"), swap)
    rows_steps = sum_everywhere(after(rows, back_bank))

    own_all = gather_direct(own_sum, "ctx", 0)
    back_mixed = mixed_sum.spread()
    back_feed = feed_sum.spread()
    rows = rows_steps[-1]
    shard_columns = lax.dynamic_slice_in_dim(rows, shard_index * shard_rows, shard_rows, 1)
    back_gain, back_bias = shard_columns[:3], shard_columns[3:6]
    token_total = jnp.sum(lengths).astype(f32) * model_width
    statistics = jnp.sqrt(rows[6, : squares.shape[0]] / token_total)

    def apart(stacked, count):
        split = stacked.reshape(shard_rows, units, count, HEAD_DIM)
        return [split[:, :, at].reshape(shard_rows, group_width).astype(f32) for at in range(count)]

    back_query_self, back_key_self, back_value_self = apart(own_all, 3)
    back_key_cross, back_value_cross = apart(back_mixed[:, 2 * group_width :], 2)
    return (
        output,
        back_hidden.astype(f32),
        back_bank,
        back_query_self,
        back_key_self,
        back_value_self,
        back_mixed[:, :group_width].T,
        back_mixed[:, group_width : 2 * group_width],
        back_key_cross,
        back_value_cross,
        back_feed[:, 2 * feed_width :].T,
        back_feed[:, :feed_width],
        back_feed[:, feed_width : 2 * feed_width].T,
        back_gain,
        back_bias,
        statistics,
    )


def solution(mesh):
    return jax.shard_map(
        per_device,
        mesh=mesh,
        in_specs=(
            P("shard", ("ctx", "tp"), None),
            P(("shard", "ctx"), "tp", None),
            P(("shard", "ctx"), None),
            P(),
            P("shard", ("ctx", "tp"), None),
            P("shard", "tp"),
            P("shard", "tp"),
            P("shard", "tp"),
            P("tp", "shard"),
            P("shard", "tp"),
            P("shard", "tp"),
            P("shard", "tp"),
            P("tp", "shard"),
            P("shard", "tp"),
            P("tp", "shard"),
            P(None, "shard"),
            P(None, "shard"),
        ),
        out_specs=(
            P("shard", ("ctx", "tp"), None),
            P("shard", ("ctx", "tp"), None),
            P(("shard", "ctx"), "tp", None),
            P("shard", "tp"),
            P("shard", "tp"),
            P("shard", "tp"),
            P("tp", "shard"),
            P("shard", "tp"),
            P("shard", "tp"),
            P("shard", "tp"),
            P("tp", "shard"),
            P("shard", "tp"),
            P("tp", "shard"),
            P(None, "shard"),
            P(None, "shard"),
            P(),
        ),
        check_vma=False,
    )
```
